128 devices in a mesh: lvl: 2 (over core), win: 64 (over z, x, y).
Axes of the slice: x: 4, y: 4, z: 4, core: 2. Of those that a mesh axis runs over, the one named last changes fastest.
Arguments:
- tokens_in: bfloat16 [2, 6, 9216, 192], P('lvl', None, 'win'), may hold values from -6 to 6
- enc_gains: float32 [12, 2, 192], replicated, may hold values from 0.5 to 1.5
- enc_shifts: float32 [12, 2, 192], replicated, may hold values from -1.5 to 1.5
- enc_qkv: bfloat16 [12, 192, 576], replicated, may hold values from -0.4375 to 0.4375
- enc_out: bfloat16 [12, 192, 192], replicated, may hold values from -1.75 to 1.75
- enc_up: bfloat16 [12, 192, 768], replicated, may hold values from -0.4375 to 0.4375
- enc_down: bfloat16 [12, 768, 192], replicated, may hold values from -0.4375 to 0.4375
- enc_lift: bfloat16 [12, 192, 384], replicated, may hold values from -0.4375 to 0.4375
- fus_gains: float32 [2, 384], replicated, may hold values from 0.5 to 1.5
- fus_shifts: float32 [2, 384], replicated, may hold values from -1.5 to 1.5
- fus_qkv: bfloat16 [384, 1152], replicated, may hold values from -0.3125 to 0.3125
- fus_out: bfloat16 [384, 384], replicated, may hold values from -1.25 to 1.25
- fus_up: bfloat16 [384, 1536], replicated, may hold values from -0.3125 to 0.3125
- fus_down: bfloat16 [1536, 384], replicated, may hold values from -0.3125 to 0.3125
- fus_table: float32 [12, 16, 3312], replicated, may hold values from -3 to 3
- target: bfloat16 [2, 6, 9216, 384], P(None, 'lvl', 'win'), may hold values from -6 to 6
- loss_code: int32 [2, 6, 9216], P(None, 'lvl', 'win'), may hold values from 0 to 7
- level_group: int32 [12], replicated, may hold values from 0 to 11, each once
- window_type: int32 [6, 128], P('lvl', 'win'), may hold values from 0 to 15
- pos_index: int32 [144, 144], replicated, may hold values from 0 to 3311
Outputs:
- output: bfloat16 [2, 6, 9216, 384], P(None, 'lvl', 'win')
- x_grad: float32 [2, 6, 9216, 192], P('lvl', None, 'win')
- enc_gains_grad: float32 [12, 2, 192], replicated
- enc_shifts_grad: float32 [12, 2, 192], replicated
- enc_qkv_grad: float32 [12, 192, 576], replicated
- enc_out_grad: float32 [12, 192, 192], replicated
- enc_up_grad: float32 [12, 192, 768], replicated
- enc_down_grad: float32 [12, 768, 192], replicated
- enc_lift_grad: float32 [12, 192, 384], replicated
- fus_gains_grad: float32 [2, 384], replicated
- fus_shifts_grad: float32 [2, 384], replicated
- fus_qkv_grad: float32 [384, 1152], replicated
- fus_out_grad: float32 [384, 384], replicated
- fus_up_grad: float32 [384, 1536], replicated
- fus_down_grad: float32 [1536, 384], replicated
- fus_table_grad: float32 [12, 16, 3312], replicated
The draws below stay inside these ranges and needn't reach their ends.
Inputs may be any that keep to these rules, and one draw needn't show every extreme that they name: `level_group`: a permutation of the groups.
All inputs are finite; a program needn't handle non-finite values.
Results may differ from the reference program's by a relative error of at most 0.018.
Values may be sent and summed in bfloat16 or wider, within the bound.
A program may use at most 320 MiB of HBM per device.

```python
import math
import jax
import jax.numpy as jnp
import numpy as np
from jax import lax

D1 = 192
D2 = 384
HEADS1 = 6
HEADS2 = 12
FF1 = 768
FF2 = 1536
WTOK = 144
NPOS = 3312
BT = 16
ETOK = 72
PAIRS = 6
GROUPS = 12
HWIN = 128
HTOK = 9216


def place_ends(entries, rng, smallest, high):
    extent = entries.shape
    index_at = [jax.random.randint(jax.random.fold_in(rng, axis), (), 0, extent[axis]) for axis in range(len(extent))]
    entries = entries.at[tuple(index_at)].set(smallest)
    longest = extent.index(max(extent))
    index_at[longest] = (index_at[longest] + 1) % extent[longest]
    return entries.at[tuple(index_at)].set(high)


def level_of(rng, extent, shards, low, largest):
    level, own = 1.0, jax.random.fold_in(rng, 6)
    for axis_at, parts in shards:
        draws = jnp.exp(jax.random.uniform(jax.random.fold_in(own, axis_at), (parts,), jnp.float32, low / len(shards), largest / len(shards)))
        level = level * jnp.repeat(draws, extent[axis_at] // parts).reshape([-1 if axis == axis_at else 1 for axis in range(len(extent))])
    return level


def cumulative_ranks(count, lean):
    portions = [(1 << 20) // math.isqrt(rank ** lean) + 1 for rank in range(1, count + 1)]
    width = 1 + sum(portions) // (1 << 30)
    return np.cumsum(np.array([max(1, weight // width) for weight in portions]))


def skewed_ids(key, extent, number_of, slope):
    grid = cumulative_ranks(number_of, slope)
    ticket = jax.random.randint(jax.random.fold_in(key, 1), extent, 0, int(grid[number_of - 1]))
    rank = jnp.searchsorted(jnp.asarray(grid, jnp.int32), ticket, side="right")
    return jax.random.permutation(jax.random.fold_in(key, 2), number_of)[rank].astype(jnp.int32)


def scatter_about(rng, shape, deviation, most, cuts=(), held_as=jnp.bfloat16):
    drawn = deviation * jax.random.normal(rng, shape, jnp.float32)
    if cuts:
        drawn = drawn * level_of(rng, shape, cuts, -0.22, 0.18)
    return jnp.clip(drawn, -most, most).astype(held_as)


def setup_inputs(seed: int = 0) -> dict:
    arg_keys = jax.random.split(jax.random.key(seed), 21)
    tokens_in = scatter_about(arg_keys[0], (2, PAIRS, HTOK, D1), 1.0, 6.0, ((0, 2), (2, 64)))
    enc_gains = jnp.clip(1.0 + 0.1 * jax.random.normal(arg_keys[1], (GROUPS, 2, D1), jnp.float32), 0.5, 1.5)
    enc_shifts = scatter_about(arg_keys[2], (GROUPS, 2, D1), 0.3, 1.5, (), jnp.float32)
    enc_qkv = scatter_about(arg_keys[3], (GROUPS, D1, 3 * D1), D1 ** -0.5, 0.4375)
    enc_out = scatter_about(arg_keys[4], (GROUPS, D1, D1), (D1 // 16) ** -0.5, 1.75)
    enc_up = scatter_about(arg_keys[5], (GROUPS, D1, FF1), D1 ** -0.5, 0.4375)
    enc_down = scatter_about(arg_keys[6], (GROUPS, FF1, D1), (FF1 // 4) ** -0.5, 0.4375)
    enc_lift = scatter_about(arg_keys[7], (GROUPS, D1, D2), D1 ** -0.5, 0.4375)
    fus_gains = jnp.clip(1.0 + 0.1 * jax.random.normal(arg_keys[8], (2, D2), jnp.float32), 0.5, 1.5)
    fus_shifts = scatter_about(arg_keys[9], (2, D2), 0.3, 1.5, (), jnp.float32)
    fus_qkv = scatter_about(arg_keys[10], (D2, 3 * D2), D2 ** -0.5, 0.3125)
    fus_out = scatter_about(arg_keys[11], (D2, D2), (D2 // 16) ** -0.5, 1.25)
    fus_up = scatter_about(arg_keys[12], (D2, FF2), D2 ** -0.5, 0.3125)
    fus_down = scatter_about(arg_keys[13], (FF2, D2), (FF2 // 4) ** -0.5, 0.3125)
    fus_table = scatter_about(arg_keys[14], (HEADS2, BT, NPOS), 0.5, 3.0, (), jnp.float32)
    target = scatter_about(arg_keys[15], (2, PAIRS, HTOK, D2), 1.0, 6.0, ((1, 2), (2, 64)))
    loss_code = place_ends(skewed_ids(arg_keys[16], (2, PAIRS, HTOK), 8, 2), jax.random.fold_in(arg_keys[16], 3), 0, 7).astype(jnp.int32)
    level_group = jax.random.permutation(arg_keys[17], GROUPS).astype(jnp.int32)
    window_type = place_ends(jax.random.randint(arg_keys[18], (PAIRS, HWIN), 0, BT), jax.random.fold_in(arg_keys[18], 1), 0, BT - 1).astype(jnp.int32)
    pos_index = place_ends(jax.random.randint(arg_keys[19], (WTOK, WTOK), 0, NPOS), jax.random.fold_in(arg_keys[19], 1), 0, NPOS - 1).astype(jnp.int32)
    return {"tokens_in": tokens_in, "enc_gains": enc_gains, "enc_shifts": enc_shifts, "enc_qkv": enc_qkv, "enc_out": enc_out, "enc_up": enc_up, "enc_down": enc_down, "enc_lift": enc_lift, "fus_gains": fus_gains, "fus_shifts": fus_shifts, "fus_qkv": fus_qkv, "fus_out": fus_out, "fus_up": fus_up, "fus_down": fus_down, "fus_table": fus_table, "target": target, "loss_code": loss_code, "level_group": level_group, "window_type": window_type, "pos_index": pos_index}


PRECISE = lax.Precision.HIGHEST
EPS = 1e-05

@jax.custom_vjp
def low(v):
    return lax.optimization_barrier(v.astype(jnp.bfloat16)).astype(jnp.float32)

@jax.custom_vjp
def low_back(v):
    return v

def low_keep(v):
    return (low(v), None)

def low_pass(kept, grad):
    return (grad,)

def back_keep(v):
    return (v, None)

def back_low(kept, grad):
    return (low(grad),)
low.defvjp(low_keep, low_pass)
low_back.defvjp(back_keep, back_low)

def layer_norm(values, gain, shift):
    mean_val = lax.optimization_barrier(jnp.mean(values, -1, keepdims=True))
    centred = values - mean_val
    spread = lax.optimization_barrier(jnp.mean(centred * centred, -1, keepdims=True))
    return centred * lax.rsqrt(spread + EPS) * gain + shift

def matmul(activations, matrix):
    return jnp.einsum('wtd,df->wtf', activations, matrix, precision=PRECISE)

def attend(normed, w_qkv, w_out, head_count, bias_add):
    dims_in = normed.shape
    features = dims_in[2]
    head_size = features // head_count
    mixed_qkv = low(low_back(matmul(normed, w_qkv)))
    qkv_parts = mixed_qkv.reshape(dims_in[:2] + (3, head_count, head_size))
    queries = qkv_parts[:, :, 0]
    key_heads = qkv_parts[:, :, 1]
    value_heads = qkv_parts[:, :, 2]
    scores = jnp.einsum('wihe,wjhe->whij', queries, key_heads, precision=PRECISE) * head_size ** (-0.5)
    if bias_add is not None:
        scores = scores + bias_add
    scores = low_back(scores)
    probs_low = low(jax.nn.softmax(scores, axis=-1))
    attended = jnp.einsum('whij,wjhe->wihe', probs_low, value_heads, precision=PRECISE).reshape(dims_in)
    attended = low(low_back(attended))
    return low_back(matmul(attended, w_out))

def swin_block(values, gain_pair, shift_pair, w_qkv, w_out, w_up, w_down, head_count, bias_add):
    normed = low(layer_norm(values, gain_pair[0], shift_pair[0]))
    hidden = values + attend(normed, w_qkv, w_out, head_count, bias_add)
    normed_second = low(layer_norm(hidden, gain_pair[1], shift_pair[1]))
    inner_act = low_back(matmul(normed_second, w_up))
    active = low(jax.nn.gelu(inner_act, approximate=False))
    return hidden + low_back(matmul(active, w_down))

def encode_row(packed):
    values, gain_pair, shift_pair, w_qkv, w_out, w_up, w_down, w_lift = packed
    result = swin_block(values, gain_pair, shift_pair, w_qkv, w_out, w_up, w_down, HEADS1, None)
    return low(low_back(matmul(low(result), w_lift)))

def reference(tokens_in, enc_gains, enc_shifts, enc_qkv, enc_out, enc_up, enc_down, enc_lift, fus_gains, fus_shifts, fus_qkv, fus_out, fus_up, fus_down, fus_table, target, loss_code, level_group, window_type, pos_index):
    params = tuple((weight.astype(jnp.float32) for weight in (enc_gains, enc_shifts, enc_qkv, enc_out, enc_up, enc_down, enc_lift, fus_gains, fus_shifts, fus_qkv, fus_out, fus_up, fus_down, fus_table)))

    def forward(inputs, e_gains, e_shifts, e_qkv, e_out, e_up, e_down, e_lift, f_gains, f_shifts, f_qkv, f_out, f_up, f_down, table):
        row_values = inputs.reshape(2 * PAIRS, HWIN, ETOK, D1)
        by_group = tuple((jnp.take(weight, level_group, axis=0) for weight in (e_gains, e_shifts, e_qkv, e_out, e_up, e_down, e_lift)))
        lifted = lax.map(jax.checkpoint(encode_row), (row_values,) + by_group)
        windows = lifted.reshape(2, PAIRS, HWIN, ETOK, D2).transpose(1, 2, 0, 3, 4).reshape(PAIRS, HWIN, WTOK, D2)
        flat_table = table.reshape(HEADS2, BT * NPOS)

        def join(packed):
            win_values, window_kinds = packed
            lookup = window_kinds[:, None, None] * NPOS + pos_index[None]
            bias_add = jnp.transpose(jnp.take(flat_table, lookup, axis=1), (1, 0, 2, 3))
            return swin_block(win_values, f_gains, f_shifts, f_qkv, f_out, f_up, f_down, HEADS2, bias_add)
        joined = lax.map(jax.checkpoint(join), (windows, window_type))
        return joined.reshape(PAIRS, HWIN, 2, ETOK, D2).transpose(2, 0, 1, 3, 4).reshape(2, PAIRS, HTOK, D2)
    output, pullback = jax.vjp(forward, tokens_in.astype(jnp.float32), *params)
    code_weight = 0.5 * jnp.exp(0.35 * loss_code.astype(jnp.float32))
    cotangent = code_weight[..., None] * target.astype(jnp.float32)
    grads = pullback(cotangent)
    return (output.astype(jnp.bfloat16), grads[0], grads[1], grads[2], grads[3], grads[4], grads[5], grads[6], grads[7], grads[8], grads[9], grads[10], grads[11], grads[12], grads[13], grads[14])
```

```python
import functools

import jax
import jax.numpy as jnp
from jax import lax
from jax.experimental import pallas as pl
from jax.experimental.pallas import tpu as pltpu
from jax.sharding import PartitionSpec as P

HEADS1 = 6
HEADS2 = 12
HEAD = 32
EPS = 1e-05
LANES = 128
SPAN = 256
PER = 2
EXTRA = 16
VMEM_LIMIT = 60 * 1024 * 1024

BF = jnp.bfloat16
F32 = jnp.float32


def nn(a, b):
    return lax.dot_general(a, b, (((1,), (0,)), ((), ())), preferred_element_type=F32)


def nt(a, b):
    return lax.dot_general(a, b, (((1,), (1,)), ((), ())), preferred_element_type=F32)


def tn(a, b):
    return lax.dot_general(a, b, (((0,), (0,)), ((), ())), preferred_element_type=F32)


def type_picker(kinds_row, heads, types):
    shape = (heads * types, kinds_row.shape[1])
    row = lax.broadcasted_iota(jnp.int32, shape, 0)
    column = lax.broadcasted_iota(jnp.int32, shape, 1)
    same_head = (row // types) == (column % heads)
    return (same_head & ((row % types) == kinds_row)).astype(F32).astype(BF)


def lay_positions(pos_ref, all_pos):
    keys = pos_ref.shape[0]
    tails = keys - LANES
    all_pos[:keys] = pos_ref[...].astype(F32).T[:, :LANES].astype(jnp.int32)
    all_pos[keys : keys + tails] = pos_ref[LANES:, :LANES]
    all_pos[keys + tails :] = jnp.full((tails, LANES), -1, jnp.int32)
    all_pos[keys + tails :, : keys - LANES] = pos_ref[LANES:, LANES:]


def one_hot_of(pos):
    low = jnp.bitwise_and(pos, SPAN - 1)
    return (lax.broadcasted_iota(jnp.int32, (SPAN, pos.shape[1]), 0) == low).astype(F32).astype(BF)


def gather_kernel(heads, types, kinds_ref, table_ref, pos_ref, main_ref, out_tail_ref, t2, all_pos, scr):
    rows = kinds_ref.shape[1]
    high = t2.shape[0] // rows
    keys = main_ref.shape[1]
    tails = keys - LANES
    count = table_ref.shape[1]
    lay_positions(pos_ref, all_pos)
    picker = type_picker(kinds_ref[...], heads, types)
    for k in range(high):
        width = min(SPAN, count - k * SPAN)
        part = table_ref[:, k * SPAN : k * SPAN + width].astype(BF)
        t2[k * rows : (k + 1) * rows, :width] = tn(picker, part).astype(BF)
        if width < SPAN:
            t2[k * rows : (k + 1) * rows, width:] = jnp.zeros((rows, SPAN - width), BF)

    def look(eight, dest, at):
        for s in range(0, 8, PER):
            pos = jnp.concatenate([eight[s + j : s + j + 1] for j in range(PER)], 1)
            top = jnp.right_shift(pos, 8)
            spread = nn(t2[...], one_hot_of(pos))
            picked = jnp.zeros((rows, PER * LANES), F32)
            for k in range(high):
                picked = jnp.where(top == k, spread[k * rows : (k + 1) * rows], picked)
            for j in range(PER):
                dest[:, pl.ds(at + s + j, 1), :] = picked[:, j * LANES : (j + 1) * LANES].reshape(rows, 1, LANES)

    @pl.loop(0, keys // 8)
    def _(i):
        at = pl.multiple_of(i * 8, 8)
        look(all_pos[pl.ds(at, 8), :], main_ref, at)

    @pl.loop(0, 2 * tails // 8)
    def _(i):
        at = pl.multiple_of(i * 8, 8)
        look(all_pos[pl.ds(keys + at, 8), :], scr, at)

    per = out_tail_ref.shape[2] // tails

    @pl.loop(0, out_tail_ref.shape[0])
    def _(i):
        first = scr[pl.ds(i * per, per), :tails].reshape(per * tails, LANES)
        second = scr[pl.ds(i * per, per), tails:].reshape(per * tails, LANES)
        out_tail_ref[pl.ds(i, 1), 0:LANES, :] = first.T.reshape(1, LANES, per * tails)
        out_tail_ref[pl.ds(i, 1), LANES:keys, :] = second.T[: keys - LANES].reshape(
            1, keys - LANES, per * tails
        )


def gather_bias(kinds_row, table, pos_index):
    heads, types, count = table.shape
    rows = kinds_row.shape[1]
    keys = pos_index.shape[0]
    tails = keys - LANES
    groups = rows * HEAD // LANES
    high = -(-count // SPAN)
    return pl.pallas_call(
        functools.partial(gather_kernel, heads, types),
        out_shape=(
            jax.ShapeDtypeStruct((rows, keys, LANES), F32),
            jax.ShapeDtypeStruct((groups, keys, rows // groups * tails), F32),
        ),
        in_specs=[pl.BlockSpec(memory_space=pltpu.VMEM)] * 3,
        out_specs=(pl.BlockSpec(memory_space=pltpu.VMEM),) * 2,
        scratch_shapes=[
            pltpu.VMEM((high * rows, SPAN), BF),
            pltpu.VMEM((keys + 2 * tails, LANES), jnp.int32),
            pltpu.VMEM((rows, 2 * tails, LANES), F32),
        ],
        compiler_params=pltpu.CompilerParams(vmem_limit_bytes=VMEM_LIMIT),
        name="gather_bias",
    )(kinds_row, table.reshape(heads * types, count), pos_index)


def scatter_kernel(heads, types, kinds_ref, main_ref, tail_in_ref, pos_ref, out_ref, acc, all_pos, scr):
    rows = kinds_ref.shape[1]
    high = out_ref.shape[0]
    keys = main_ref.shape[1]
    tails = keys - LANES
    lay_positions(pos_ref, all_pos)
    scr[:, :keys] = main_ref[...].astype(F32)
    per = tail_in_ref.shape[2] // tails
    scr[:, keys + tails :] = jnp.zeros((rows, tails, LANES), F32)

    @pl.loop(0, tail_in_ref.shape[0])
    def _(i):
        block = tail_in_ref[pl.ds(i, 1)].reshape(keys, per * tails).astype(F32)
        scr[pl.ds(i * per, per), keys : keys + tails] = block[:LANES].T.reshape(per, tails, LANES)
        scr[pl.ds(i * per, per), keys + tails :, : keys - LANES] = block[LANES:].T.reshape(per, tails, keys - LANES)

    acc[...] = jnp.zeros_like(acc)

    @pl.loop(0, (keys + 2 * tails) // 8)
    def _(i):
        at = pl.multiple_of(i * 8, 8)
        eight = all_pos[pl.ds(at, 8), :]
        total = None
        for s in range(0, 8, PER):
            pos = jnp.concatenate([eight[s + j : s + j + 1] for j in range(PER)], 1)
            terms = jnp.concatenate([scr[:, pl.ds(at + s + j, 1), :].reshape(rows, LANES) for j in range(PER)], 1)
            top = jnp.right_shift(pos, 8)
            parts = jnp.concatenate([jnp.where(top == k, terms, 0.0) for k in range(high)], 0)
            term = nt(parts.astype(BF), one_hot_of(pos))
            total = term if total is None else total + term
        acc[...] += total

    picker = type_picker(kinds_ref[...], heads, types)
    for k in range(high):
        out_ref[k] = nn(picker, acc[k * rows : (k + 1) * rows].astype(BF)).astype(BF)


def scatter_bias(kinds_row, ds_main, ds_tail, pos_index, table_shape):
    heads, types, count = table_shape
    rows, keys = ds_main.shape[:2]
    tails = keys - LANES
    high = -(-count // SPAN)
    return pl.pallas_call(
        functools.partial(scatter_kernel, heads, types),
        out_shape=jax.ShapeDtypeStruct((high, heads * types, SPAN), BF),
        in_specs=[pl.BlockSpec(memory_space=pltpu.VMEM)] * 4,
        out_specs=pl.BlockSpec(memory_space=pltpu.VMEM),
        scratch_shapes=[
            pltpu.VMEM((high * rows, SPAN), F32),
            pltpu.VMEM((keys + 2 * tails, LANES), jnp.int32),
            pltpu.VMEM((rows, keys + 2 * tails, LANES), F32),
        ],
        compiler_params=pltpu.CompilerParams(vmem_limit_bytes=VMEM_LIMIT),
        name="scatter_bias",
    )(kinds_row, ds_main, ds_tail, pos_index)


def norm(values):
    centred = values - jnp.mean(values, -1, keepdims=True)
    spread = jnp.mean(centred * centred, -1, keepdims=True)
    scale = lax.rsqrt(spread + EPS)
    return centred * scale, scale


def norm_back(grad, gain, unit, scale):
    scaled = grad * gain
    first = jnp.mean(scaled, -1, keepdims=True)
    second = jnp.mean(scaled * unit, -1, keepdims=True)
    return (scaled - first - unit * second) * scale


def gelu_pair(v):
    half = jnp.exp(-0.5 * v * v)
    t = 1.0 / (1.0 + 0.23164189 * jnp.abs(v))
    series = t * (0.127414796 + t * (-0.142248368 + t * (0.7107068705 + t * (-0.7265760135 + t * 0.5307027145))))
    tail = series * half
    phi = jnp.where(v >= 0.0, 1.0 - tail, tail)
    return v * phi, phi + v * half * 0.3989422804014327


def head_masks(width):
    lane = lax.broadcasted_iota(jnp.int32, (1, width), 1)
    return [(lane // HEAD) == h for h in range(width // HEAD)]


def keep(mask, values):
    return jnp.where(mask, values, 0.0)


def softmax_rows(scores):
    top = jnp.max(scores, 0, keepdims=True)
    e = jnp.exp(scores - top)
    return e * (1.0 / jnp.sum(e, 0, keepdims=True))


def score_back(prob, grad):
    return prob * (grad - jnp.sum(grad * prob, 0, keepdims=True))


def pair_kernel(
    groups_ref,
    x_ref,
    e_gain0, e_gain1, e_shift0, e_shift1,
    e_qkv0, e_qkv1, e_out0, e_out1, e_up0, e_up1, e_down0, e_down1, e_lift0, e_lift1,
    f_gain, f_shift, f_qkv, f_out, f_up, f_down,
    bias_main, bias_tail,
    target_ref, code_ref,
    out_ref, xg_ref, enc_ref, fus_ref, ds_main, ds_tail,
    acc, acc_norm, n1_s, q_s, k_s, v_s, p_s, o_s, n2_s, h_s, act_s, gp_s, res_s,
    win_s, fq, fk, fv, fp, fo, fdq, fdk, fdv, fh, fn2, fdy, fgrad,
):
    step = pl.program_id(0)
    rows = x_ref.shape[2]
    width1 = x_ref.shape[3]
    width2 = f_qkv.shape[0]
    half = rows // 2
    keys = rows
    root = HEAD ** (-0.5)
    masks1 = head_masks(width1)
    masks2 = head_masks(LANES)
    gains1, shifts1 = (e_gain0, e_gain1), (e_shift0, e_shift1)
    w_qkv, w_out, w_up = (e_qkv0, e_qkv1), (e_out0, e_out1), (e_up0, e_up1)
    w_down, w_lift = (e_down0, e_down1), (e_lift0, e_lift1)

    def stack1(values):
        return jnp.concatenate([keep(m, values) for m in masks1], 0).astype(BF)

    def fold1(stacked):
        total = keep(masks1[0], stacked[:half])
        for h in range(1, HEADS1):
            total += keep(masks1[h], stacked[h * half : (h + 1) * half])
        return total

    for l in range(2):
        x = x_ref[l, 0].astype(F32)
        z1, _ = norm(x)
        n1 = (z1 * gains1[l][0, 0:1] + shifts1[l][0, 0:1]).astype(BF)
        n1_s[l] = n1
        qkv = nn(n1, w_qkv[l][0])
        q_s[l] = qkv[:, :width1].astype(BF).astype(F32)
        k_s[l] = qkv[:, width1 : 2 * width1].astype(BF).astype(F32)
        v_s[l] = qkv[:, 2 * width1 :].astype(BF).astype(F32)
        for w in range(2):
            part = slice(w * half, (w + 1) * half)
            scores = nt(k_s[l, part].astype(BF), stack1(q_s[l, part])) * root
            prob = softmax_rows(scores)
            p_s[l, w] = prob
            o_s[l, part] = fold1(tn(prob.astype(BF), v_s[l, part].astype(BF)))
        h = x + nn(o_s[l].astype(BF), w_out[l][0])
        h_s[l] = h
        z2, _ = norm(h)
        n2 = (z2 * gains1[l][0, 1:2] + shifts1[l][0, 1:2]).astype(BF)
        n2_s[l] = n2
        act, slope = gelu_pair(nn(n2, w_up[l][0]))
        act = act.astype(BF)
        act_s[l] = act
        gp_s[l] = slope
        res = (h + nn(act, w_down[l][0])).astype(BF)
        res_s[l] = res
        lifted = nn(res, w_lift[l][0]).astype(BF).astype(F32)
        for w in range(2):
            win_s[w * rows + l * half : w * rows + (l + 1) * half] = lifted[w * half : (w + 1) * half]

    eye = lax.broadcasted_iota(jnp.int32, (rows, rows), 0) == lax.broadcasted_iota(jnp.int32, (rows, rows), 1)
    for l in range(2):
        weight = 0.5 * jnp.exp(0.35 * code_ref[l, 0].astype(F32))
        column = jnp.sum(jnp.where(eye, weight, 0.0), 1, keepdims=True)
        direction = column * target_ref[l, 0].astype(F32)
        for w in range(2):
            fdy[w * rows + l * half : w * rows + (l + 1) * half] = direction[w * half : (w + 1) * half]

    lane_groups = width2 // LANES
    z1, _ = norm(win_s[...])
    fn1 = (z1 * f_gain[0:1] + f_shift[0:1]).astype(BF)
    for t, dest in enumerate((fq, fk, fv)):
        part = nn(fn1, f_qkv[:, t * width2 : (t + 1) * width2]).astype(BF)
        for w in range(2):
            for g in range(lane_groups):
                dest[w * lane_groups + g] = part[w * rows : (w + 1) * rows, g * LANES : (g + 1) * LANES]
    tails = rows - LANES

    def stacks(values):
        main = values[:LANES]
        tail = values[LANES:].astype(F32)
        return [keep(m, main.astype(F32)).astype(BF) for m in masks2] + [
            jnp.concatenate([keep(m, tail) for m in masks2], 0).astype(BF)
        ]

    heads = LANES // HEAD

    def fold2(parts):
        main = keep(masks2[0], parts[0])
        tail = keep(masks2[0], parts[heads][:tails])
        for h in range(1, heads):
            main += keep(masks2[h], parts[h])
            tail += keep(masks2[h], parts[heads][h * tails : (h + 1) * tails])
        return jnp.concatenate([main, tail], 0)

    @pl.loop(0, 2 * lane_groups)
    def _(i):
        key = fk[i]
        val = fv[i]
        outs = []
        for j, query in enumerate(stacks(fq[i])):
            bias = bias_main[i * heads + j] if j < heads else bias_tail[i]
            prob = softmax_rows(nt(key, query) * root + bias)
            if j < heads:
                fp[i, :, j * LANES : (j + 1) * LANES] = prob
            else:
                fp[i, :, j * LANES :] = prob
            outs.append(tn(prob.astype(BF), val))
        fo[i] = fold2(outs).astype(BF)

    def joined(ref):
        return jnp.concatenate(
            [jnp.concatenate([ref[w * lane_groups + g] for g in range(lane_groups)], 1) for w in range(2)], 0
        )

    hidden = win_s[...] + nn(joined(fo), f_out[...])
    fh[...] = hidden
    z2, _ = norm(hidden)
    fn2[...] = (z2 * f_gain[1:2] + f_shift[1:2]).astype(BF)

    @pl.when(step == 0)
    def _():
        acc[...] = jnp.zeros_like(acc)
        acc_norm[...] = jnp.zeros_like(acc_norm)

    blocks = f_up.shape[1] // width2
    win_s_block = width2
    fgrad[...] = jnp.zeros_like(fgrad)

    @pl.loop(0, blocks)
    def _(j):
        at = pl.multiple_of(j * win_s_block, LANES)
        up = f_up[:, pl.ds(at, win_s_block)]
        down = f_down[pl.ds(at, win_s_block), :]
        n2 = fn2[...]
        low = fdy[...].astype(BF)
        act, slope = gelu_pair(nn(n2, up))
        act = act.astype(BF)
        fh[...] += nn(act, down)
        inner_grad = (nt(low, down) * slope).astype(BF)
        acc[pl.ds(8 * width2 + at, win_s_block), :] += tn(act, low)
        acc[pl.ds(4 * width2 + at, win_s_block), :] += tn(n2, inner_grad)
        fgrad[...] += nt(inner_grad, up)

    for l in range(2):
        for w in range(2):
            out_ref[l, 0, w * half : (w + 1) * half] = fh[w * rows + l * half : w * rows + (l + 1) * half].astype(BF)

    hidden = win_s[...] + nn(joined(fo), f_out[...])
    z2, r2 = norm(hidden)
    grad = fgrad[...]
    acc_norm[1:2] += jnp.sum(grad * z2, 0, keepdims=True)
    acc_norm[3:4] += jnp.sum(grad, 0, keepdims=True)
    hidden_grad = fdy[...] + norm_back(grad, f_gain[1:2], z2, r2)
    fgrad[...] = hidden_grad
    low = hidden_grad.astype(BF)
    acc[3 * width2 : 4 * width2] += tn(joined(fo), low)
    att_grad = nt(low, f_out[...]).astype(BF)
    for w in range(2):
        for g in range(lane_groups):
            fo[w * lane_groups + g] = att_grad[w * rows : (w + 1) * rows, g * LANES : (g + 1) * LANES]

    @pl.loop(0, 2 * lane_groups)
    def _(i):
        key = fk[i]
        val = fv[i]
        queries = stacks(fq[i])
        dq = []
        dk = jnp.zeros((keys, LANES), F32)
        dv = jnp.zeros((keys, LANES), F32)
        for j, grads in enumerate(stacks(fo[i])):
            prob = fp[i, :, j * LANES : (j + 1) * LANES] if j < heads else fp[i, :, j * LANES :]
            ds = score_back(prob, nt(val, grads)).astype(BF)
            if j < heads:
                ds_main[i * heads + j] = ds
            else:
                ds_tail[i] = ds
            dv += nn(prob.astype(BF), grads)
            dk += nn(ds, queries[j])
            dq.append(tn(ds, key))
        fdq[i] = (fold2(dq) * root).astype(BF)
        fdk[i] = (dk * root).astype(BF)
        fdv[i] = dv.astype(BF)

    z1, r1 = norm(win_s[...])
    n1 = (z1 * f_gain[0:1] + f_shift[0:1]).astype(BF)
    first = jnp.zeros((2 * rows, width2), F32)
    for t, src in enumerate((fdq, fdk, fdv)):
        part = joined(src)
        acc[t * width2 : (t + 1) * width2] += tn(n1, part)
        first += nt(part, f_qkv[:, t * width2 : (t + 1) * width2])
    acc_norm[0:1] += jnp.sum(first * z1, 0, keepdims=True)
    acc_norm[2:3] += jnp.sum(first, 0, keepdims=True)
    fgrad[...] += norm_back(first, f_gain[0:1], z1, r1)

    @pl.when(step == pl.num_programs(0) - 1)
    def _():
        fus_ref[: 12 * width2] = acc[...].astype(BF)
        fus_ref[12 * width2 :] = jnp.pad(acc_norm[...], ((0, EXTRA - 4), (0, 0))).astype(BF)

    for l in range(2):
        lift_grad = jnp.concatenate(
            [fgrad[w * rows + l * half : w * rows + (l + 1) * half] for w in range(2)], 0
        ).astype(BF)
        enc_ref[0, l, 4 * width1 : 5 * width1] = tn(res_s[l], lift_grad).astype(BF)
        d_out = nt(lift_grad, w_lift[l][0])
        low = d_out.astype(BF)
        down_grad = tn(act_s[l], low).astype(BF)
        enc_ref[0, l, 5 * width1 : 7 * width1, :width1] = down_grad[: 2 * width1]
        enc_ref[0, l, 5 * width1 : 7 * width1, width1:] = down_grad[2 * width1 :]
        inner_grad = (nt(low, w_down[l][0]) * gp_s[l]).astype(BF)
        up_grad = tn(n2_s[l], inner_grad).astype(BF)
        enc_ref[0, l, 2 * width1 : 3 * width1] = up_grad[:, : 2 * width1]
        enc_ref[0, l, 3 * width1 : 4 * width1] = up_grad[:, 2 * width1 :]
        grad = nt(inner_grad, w_up[l][0])
        z2, r2 = norm(h_s[l])
        norms = [None, jnp.sum(grad * z2, 0, keepdims=True), None, jnp.sum(grad, 0, keepdims=True)]
        hidden_grad = d_out + norm_back(grad, gains1[l][0, 1:2], z2, r2)
        low = hidden_grad.astype(BF)
        enc_ref[0, l, width1 : 2 * width1, width1:] = tn(o_s[l].astype(BF), low).astype(BF)
        att_grad = nt(low, w_out[l][0]).astype(BF).astype(F32)
        parts = []
        for w in range(2):
            part = slice(w * half, (w + 1) * half)
            prob = p_s[l, w]
            grads = stack1(att_grad[part])
            ds = score_back(prob, nt(v_s[l, part].astype(BF), grads)).astype(BF)
            dv = nn(prob.astype(BF), grads)
            dk = nn(ds, stack1(q_s[l, part])) * root
            dq = fold1(tn(ds, k_s[l, part].astype(BF))) * root
            parts.append(jnp.concatenate([dq, dk, dv], 1))
        mixed = jnp.concatenate(parts, 0).astype(BF)
        qkv_grad = tn(n1_s[l], mixed).astype(BF)
        enc_ref[0, l, :width1] = qkv_grad[:, : 2 * width1]
        enc_ref[0, l, width1 : 2 * width1, :width1] = qkv_grad[:, 2 * width1 :]
        first = nt(mixed, w_qkv[l][0])
        z1, r1 = norm(x_ref[l, 0].astype(F32))
        norms[0] = jnp.sum(first * z1, 0, keepdims=True)
        norms[2] = jnp.sum(first, 0, keepdims=True)
        norms = jnp.pad(jnp.concatenate(norms, 0), ((0, EXTRA - 4), (0, width1)))
        enc_ref[0, l, 7 * width1 :] = norms.astype(BF)
        xg_ref[l, 0] = hidden_grad + norm_back(first, gains1[l][0, 0:1], z1, r1)


def pair_blocks(chosen, x, enc, fus, bias_main, bias_tail, target, code):
    _, pairs, rows, width1 = x.shape
    width2 = fus[2].shape[0]
    ff1 = enc[4].shape[2]
    half = rows // 2
    groups = 2 * width2 // LANES
    heads = LANES // HEAD
    tails = rows - LANES
    packed1 = 7 * width1 + EXTRA
    packed2 = 12 * width2 + EXTRA

    def by_group(array, level):
        return pl.BlockSpec((1,) + array.shape[1:], lambda q, s, level=level: (s[level * pairs + q], 0, 0))

    def whole(array):
        return pl.BlockSpec(array.shape, lambda q, s: (0,) * array.ndim, pipeline_mode=pl.Buffered(1))

    enc_args, enc_specs = [], []
    for array in enc:
        for level in range(2):
            enc_args.append(array)
            enc_specs.append(by_group(array, level))
    in_specs = (
        [pl.BlockSpec((2, 1, rows, width1), lambda q, s: (0, q, 0, 0))]
        + enc_specs
        + [whole(a) for a in fus]
        + [
            pl.BlockSpec((groups * heads, rows, LANES), lambda q, s: (q, 0, 0)),
            pl.BlockSpec((groups, rows, heads * tails), lambda q, s: (q, 0, 0)),
            pl.BlockSpec((2, 1, rows, width2), lambda q, s: (0, q, 0, 0)),
            pl.BlockSpec((2, 1, 1, rows), lambda q, s: (0, q, 0, 0)),
        ]
    )
    out_shape = (
        jax.ShapeDtypeStruct((2, pairs, rows, width2), BF),
        jax.ShapeDtypeStruct((2, pairs, rows, width1), F32),
        jax.ShapeDtypeStruct((pairs, 2, packed1, 2 * width1), BF),
        jax.ShapeDtypeStruct((packed2, width2), BF),
        jax.ShapeDtypeStruct((pairs * groups * heads, rows, LANES), BF),
        jax.ShapeDtypeStruct((pairs * groups, rows, heads * tails), BF),
    )
    out_specs = (
        pl.BlockSpec((2, 1, rows, width2), lambda q, s: (0, q, 0, 0)),
        pl.BlockSpec((2, 1, rows, width1), lambda q, s: (0, q, 0, 0)),
        pl.BlockSpec((1, 2, packed1, 2 * width1), lambda q, s: (q, 0, 0, 0)),
        pl.BlockSpec((packed2, width2), lambda q, s: (0, 0)),
        pl.BlockSpec((groups * heads, rows, LANES), lambda q, s: (q, 0, 0)),
        pl.BlockSpec((groups, rows, heads * tails), lambda q, s: (q, 0, 0)),
    )
    stacked = groups // 2 * 0 + HEADS1 * half
    lanes = heads * LANES + heads * tails
    scratch = [
        pltpu.VMEM((12 * width2, width2), F32),
        pltpu.VMEM((4, width2), F32),
        pltpu.VMEM((2, rows, width1), BF),
        pltpu.VMEM((2, rows, width1), F32),
        pltpu.VMEM((2, rows, width1), F32),
        pltpu.VMEM((2, rows, width1), F32),
        pltpu.VMEM((2, 2, half, stacked), F32),
        pltpu.VMEM((2, rows, width1), F32),
        pltpu.VMEM((2, rows, width1), BF),
        pltpu.VMEM((2, rows, width1), F32),
        pltpu.VMEM((2, rows, ff1), BF),
        pltpu.VMEM((2, rows, ff1), F32),
        pltpu.VMEM((2, rows, width1), BF),
        pltpu.VMEM((2 * rows, width2), F32),
        pltpu.VMEM((groups, rows, LANES), BF),
        pltpu.VMEM((groups, rows, LANES), BF),
        pltpu.VMEM((groups, rows, LANES), BF),
        pltpu.VMEM((groups, rows, lanes), F32),
        pltpu.VMEM((groups, rows, LANES), BF),
        pltpu.VMEM((groups, rows, LANES), BF),
        pltpu.VMEM((groups, rows, LANES), BF),
        pltpu.VMEM((groups, rows, LANES), BF),
        pltpu.VMEM((2 * rows, width2), F32),
        pltpu.VMEM((2 * rows, width2), BF),
        pltpu.VMEM((2 * rows, width2), F32),
        pltpu.VMEM((2 * rows, width2), F32),
    ]
    return pl.pallas_call(
        pair_kernel,
        out_shape=out_shape,
        grid_spec=pltpu.PrefetchScalarGridSpec(
            num_scalar_prefetch=1,
            grid=(pairs,),
            in_specs=in_specs,
            out_specs=out_specs,
            scratch_shapes=scratch,
        ),
        compiler_params=pltpu.CompilerParams(vmem_limit_bytes=VMEM_LIMIT),
        name="pair_blocks",
    )(chosen, x, *enc_args, *fus, bias_main, bias_tail, target, code)


def unpack_kernel(place_ref, enc_ref, fus_ref, fus_extra, table_in, gain_ref, shift_ref, qkv_ref, out_ref, up_ref, down_ref, lift_ref, fg_ref, fs_ref, fq_ref, fo_ref, fu_ref, fd_ref, table_ref):
    width = qkv_ref.shape[1]
    part = enc_ref.at[0]
    norms = part[7 * width :].astype(F32)
    gain_ref[0] = norms[0:2, :width]
    shift_ref[0] = norms[2:4, :width]
    qkv_ref[0, :, : 2 * width] = part[:width].astype(F32)
    qkv_ref[0, :, 2 * width :] = part[width : 2 * width, :width].astype(F32)
    out_ref[0] = part[width : 2 * width, width:].astype(F32)
    up_ref[0, :, : 2 * width] = part[2 * width : 3 * width].astype(F32)
    up_ref[0, :, 2 * width :] = part[3 * width : 4 * width].astype(F32)
    lift_ref[0] = part[4 * width : 5 * width].astype(F32)
    down_ref[0, : 2 * width] = part[5 * width : 7 * width, :width].astype(F32)
    down_ref[0, 2 * width :] = part[5 * width : 7 * width, width:].astype(F32)
    i = pl.program_id(0)
    joining = fus_ref[...].astype(F32)

    @pl.when(i < 3)
    def _():
        fq_ref[...] = joining

    @pl.when(i == 3)
    def _():
        fo_ref[...] = joining

    @pl.when((i >= 4) & (i < 8))
    def _():
        fu_ref[...] = joining

    @pl.when(i >= 8)
    def _():
        fd_ref[...] = joining

    heads, types, count = table_ref.shape

    @pl.when(i == 0)
    def _():
        extra = fus_extra[...].astype(F32)
        fg_ref[...] = extra[0:2]
        fs_ref[...] = extra[2:4]
        for k in range(table_in.shape[0]):
            size = min(SPAN, count - k * SPAN)
            block = table_in[k].astype(F32).reshape(heads, types, SPAN)
            table_ref[:, :, k * SPAN : k * SPAN + size] = block[:, :, :size]


def unpack(place, enc, fus, table, table_shape):
    groups = enc.shape[0]
    width1 = enc.shape[2] // 2
    width2 = fus.shape[1]
    sizes1 = [(2, width1), (2, width1), (width1, 3 * width1), (width1, width1), (width1, 4 * width1), (4 * width1, width1), (width1, 2 * width1)]
    sizes2 = [(2, width2), (2, width2), (width2, 3 * width2), (width2, width2), (width2, 4 * width2), (4 * width2, width2)]
    square = (width2, width2)
    return pl.pallas_call(
        unpack_kernel,
        out_shape=tuple(jax.ShapeDtypeStruct((groups,) + s, F32) for s in sizes1)
        + tuple(jax.ShapeDtypeStruct(s, F32) for s in sizes2)
        + (jax.ShapeDtypeStruct(table_shape, F32),),
        grid_spec=pltpu.PrefetchScalarGridSpec(
            num_scalar_prefetch=1,
            grid=(groups,),
            in_specs=[
                pl.BlockSpec((1,) + enc.shape[1:], lambda i, s: (s[i], 0, 0)),
                pl.BlockSpec(square, lambda i, s: (i, 0)),
                pl.BlockSpec((EXTRA, width2), lambda i, s: (12 * width2 // EXTRA, 0)),
                pl.BlockSpec(table.shape, lambda i, s: (0, 0, 0)),
            ],
            out_specs=tuple(pl.BlockSpec((1,) + s, lambda i, s: (i, 0, 0)) for s in sizes1)
            + (
                pl.BlockSpec((2, width2), lambda i, s: (0, 0)),
                pl.BlockSpec((2, width2), lambda i, s: (0, 0)),
                pl.BlockSpec(square, lambda i, s: (0, jnp.minimum(i, 2))),
                pl.BlockSpec(square, lambda i, s: (0, 0)),
                pl.BlockSpec(square, lambda i, s: (0, jnp.clip(i - 4, 0, 3))),
                pl.BlockSpec(square, lambda i, s: (jnp.clip(i - 8, 0, 3), 0)),
                pl.BlockSpec(table_shape, lambda i, s: (0, 0, 0)),
            ),
        ),
        compiler_params=pltpu.CompilerParams(vmem_limit_bytes=VMEM_LIMIT),
        name="unpack",
    )(place, enc, fus, fus, table)


def shards(
    tokens_in,
    enc_gains,
    enc_shifts,
    enc_qkv,
    enc_out,
    enc_up,
    enc_down,
    enc_lift,
    fus_gains,
    fus_shifts,
    fus_qkv,
    fus_out,
    fus_up,
    fus_down,
    fus_table,
    target,
    loss_code,
    level_group,
    window_type,
    pos_index,
):
    pairs = target.shape[1]
    all_rows = level_group.shape[0]
    side = lax.axis_index("lvl")
    heads = fus_table.shape[0]
    x = lax.all_to_all(tokens_in, "lvl", split_axis=1, concat_axis=0, tiled=True)
    held = level_group.reshape(2, 2, pairs)
    chosen = lax.dynamic_index_in_dim(held, side, 1, keepdims=False).reshape(2 * pairs)
    kinds = jnp.repeat(window_type.reshape(-1), heads)[None]
    bias_main, bias_tail = gather_bias(kinds, fus_table, pos_index)
    output, x_grad, enc, fus, ds_main, ds_tail = pair_blocks(
        chosen,
        x,
        (enc_gains, enc_shifts, enc_qkv, enc_out, enc_up, enc_down, enc_lift),
        (fus_gains, fus_shifts, fus_qkv, fus_out, fus_up, fus_down),
        bias_main,
        bias_tail,
        target,
        loss_code[:, :, None],
    )
    table = scatter_bias(kinds, ds_main, ds_tail, pos_index, fus_table.shape)
    x_grad = lax.all_to_all(x_grad, "lvl", split_axis=0, concat_axis=1, tiled=True)

    def on_side(array):
        rows = array.reshape((1, all_rows // 2) + array.shape[2:])
        spread = jnp.concatenate([rows, jnp.zeros_like(rows)], 0)
        return jnp.where(side == 0, spread, spread[::-1]).reshape((all_rows,) + array.shape[2:])

    enc, fus, table = lax.psum((on_side(enc), fus, table), ("lvl", "win"))
    order = jnp.transpose(held, (1, 2, 0)).reshape(-1)
    spot = jnp.arange(all_rows, dtype=jnp.int32)
    place = jnp.sum(jnp.where(order[None] == spot[:, None], spot[None], 0), 1)
    grads = unpack(place, enc, fus, table, fus_table.shape)
    return (output, x_grad, *grads)


def solution(mesh):
    copied = P()
    in_specs = (
        (P("lvl", None, "win", None),)
        + (copied,) * 14
        + (P(None, "lvl", "win", None), P(None, "lvl", "win"), copied, P("lvl", "win"), copied)
    )
    out_specs = (P(None, "lvl", "win", None), P("lvl", None, "win", None)) + (copied,) * 14
    return jax.shard_map(shards, mesh=mesh, in_specs=in_specs, out_specs=out_specs, check_vma=False)
```

```python
import functools

import jax
import jax.numpy as jnp
from jax import lax
from jax.experimental import pallas as pl
from jax.experimental.pallas import tpu as pltpu
from jax.sharding import PartitionSpec as P

HEADS1 = 6
HEADS2 = 12
HEAD = 32
EPS = 1e-05
LANES = 128
SPAN = 256
PER = 2
ROWS1 = 4096
EXTRA = 16
VMEM_LIMIT = 60 * 1024 * 1024

BF = jnp.bfloat16
F32 = jnp.float32


def nn(a, b):
    return lax.dot_general(a, b, (((1,), (0,)), ((), ())), preferred_element_type=F32)


def nt(a, b):
    return lax.dot_general(a, b, (((1,), (1,)), ((), ())), preferred_element_type=F32)


def tn(a, b):
    return lax.dot_general(a, b, (((0,), (0,)), ((), ())), preferred_element_type=F32)


def type_picker(kinds_row, heads, types):
    shape = (heads * types, kinds_row.shape[1])
    row = lax.broadcasted_iota(jnp.int32, shape, 0)
    column = lax.broadcasted_iota(jnp.int32, shape, 1)
    same_head = (row // types) == (column % heads)
    return (same_head & ((row % types) == kinds_row)).astype(F32).astype(BF)


def lay_positions(pos_ref, all_pos):
    keys = pos_ref.shape[0]
    tails = keys - LANES
    all_pos[:keys] = pos_ref[...].astype(F32).T[:, :LANES].astype(jnp.int32)
    all_pos[keys : keys + tails] = pos_ref[LANES:, :LANES]
    all_pos[keys + tails :] = jnp.full((tails, LANES), -1, jnp.int32)
    all_pos[keys + tails :, : keys - LANES] = pos_ref[LANES:, LANES:]


def one_hot_of(pos):
    low = jnp.bitwise_and(pos, SPAN - 1)
    return (lax.broadcasted_iota(jnp.int32, (SPAN, pos.shape[1]), 0) == low).astype(F32).astype(BF)


def gather_kernel(heads, types, kinds_ref, table_ref, pos_ref, main_ref, out_tail_ref, t2, all_pos, scr):
    rows = kinds_ref.shape[1]
    high = t2.shape[0] // rows
    keys = main_ref.shape[1]
    tails = keys - LANES
    count = table_ref.shape[1]
    lay_positions(pos_ref, all_pos)
    picker = type_picker(kinds_ref[...], heads, types)
    for k in range(high):
        width = min(SPAN, count - k * SPAN)
        part = table_ref[:, k * SPAN : k * SPAN + width].astype(BF)
        t2[k * rows : (k + 1) * rows, :width] = tn(picker, part).astype(BF)
        if width < SPAN:
            t2[k * rows : (k + 1) * rows, width:] = jnp.zeros((rows, SPAN - width), BF)

    def look(eight, dest, at):
        for s in range(0, 8, PER):
            pos = jnp.concatenate([eight[s + j : s + j + 1] for j in range(PER)], 1)
            top = jnp.right_shift(pos, 8)
            spread = nn(t2[...], one_hot_of(pos))
            picked = jnp.zeros((rows, PER * LANES), F32)
            for k in range(high):
                picked = jnp.where(top == k, spread[k * rows : (k + 1) * rows], picked)
            for j in range(PER):
                dest[:, pl.ds(at + s + j, 1), :] = picked[:, j * LANES : (j + 1) * LANES].reshape(rows, 1, LANES)

    @pl.loop(0, keys // 8)
    def _(i):
        at = pl.multiple_of(i * 8, 8)
        look(all_pos[pl.ds(at, 8), :], main_ref, at)

    @pl.loop(0, 2 * tails // 8)
    def _(i):
        at = pl.multiple_of(i * 8, 8)
        look(all_pos[pl.ds(keys + at, 8), :], scr, at)

    per = out_tail_ref.shape[2] // tails

    @pl.loop(0, out_tail_ref.shape[0])
    def _(i):
        first = scr[pl.ds(i * per, per), :tails].reshape(per * tails, LANES)
        second = scr[pl.ds(i * per, per), tails:].reshape(per * tails, LANES)
        out_tail_ref[pl.ds(i, 1), 0:LANES, :] = first.T.reshape(1, LANES, per * tails)
        out_tail_ref[pl.ds(i, 1), LANES:keys, :] = second.T[: keys - LANES].reshape(
            1, keys - LANES, per * tails
        )


def gather_bias(kinds_row, table, pos_index):
    heads, types, count = table.shape
    rows = kinds_row.shape[1]
    keys = pos_index.shape[0]
    tails = keys - LANES
    groups = rows * HEAD // LANES
    high = -(-count // SPAN)
    return pl.pallas_call(
        functools.partial(gather_kernel, heads, types),
        out_shape=(
            jax.ShapeDtypeStruct((rows, keys, LANES), F32),
            jax.ShapeDtypeStruct((groups, keys, rows // groups * tails), F32),
        ),
        in_specs=[pl.BlockSpec(memory_space=pltpu.VMEM)] * 3,
        out_specs=(pl.BlockSpec(memory_space=pltpu.VMEM),) * 2,
        scratch_shapes=[
            pltpu.VMEM((high * rows, SPAN), BF),
            pltpu.VMEM((keys + 2 * tails, LANES), jnp.int32),
            pltpu.VMEM((rows, 2 * tails, LANES), F32),
        ],
        compiler_params=pltpu.CompilerParams(vmem_limit_bytes=VMEM_LIMIT),
        name="gather_bias",
    )(kinds_row, table.reshape(heads * types, count), pos_index)


def scatter_kernel(heads, types, kinds_ref, main_ref, tail_in_ref, pos_ref, out_ref, acc, all_pos, scr):
    rows = kinds_ref.shape[1]
    high = acc.shape[0] // rows
    keys = main_ref.shape[1]
    tails = keys - LANES
    lay_positions(pos_ref, all_pos)
    scr[:, :keys] = main_ref[...].astype(F32)
    per = tail_in_ref.shape[2] // tails
    scr[:, keys + tails :] = jnp.zeros((rows, tails, LANES), F32)

    @pl.loop(0, tail_in_ref.shape[0])
    def _(i):
        block = tail_in_ref[pl.ds(i, 1)].reshape(keys, per * tails).astype(F32)
        scr[pl.ds(i * per, per), keys : keys + tails] = block[:LANES].T.reshape(per, tails, LANES)
        scr[pl.ds(i * per, per), keys + tails :, : keys - LANES] = block[LANES:].T.reshape(per, tails, keys - LANES)

    acc[...] = jnp.zeros_like(acc)

    @pl.loop(0, (keys + 2 * tails) // 8)
    def _(i):
        at = pl.multiple_of(i * 8, 8)
        eight = all_pos[pl.ds(at, 8), :]
        total = None
        for s in range(0, 8, PER):
            pos = jnp.concatenate([eight[s + j : s + j + 1] for j in range(PER)], 1)
            terms = jnp.concatenate([scr[:, pl.ds(at + s + j, 1), :].reshape(rows, LANES) for j in range(PER)], 1)
            top = jnp.right_shift(pos, 8)
            parts = jnp.concatenate([jnp.where(top == k, terms, 0.0) for k in range(high)], 0)
            term = nt(parts.astype(BF), one_hot_of(pos))
            total = term if total is None else total + term
        acc[...] += total

    picker = type_picker(kinds_ref[...], heads, types)
    many = heads * types
    for k in range(high):
        part = nn(picker, acc[k * rows : (k + 1) * rows].astype(BF)).astype(BF)
        for j in range(SPAN // LANES):
            n = k * (SPAN // LANES) + j
            at = n % high * many
            out_ref[n // high, at : at + many] = part[:, j * LANES : (j + 1) * LANES]


def scatter_bias(kinds_row, ds_main, ds_tail, pos_index, table_shape):
    heads, types, count = table_shape
    rows, keys = ds_main.shape[:2]
    tails = keys - LANES
    high = -(-count // SPAN)
    return pl.pallas_call(
        functools.partial(scatter_kernel, heads, types),
        out_shape=jax.ShapeDtypeStruct((2, high * heads * types, LANES), BF),
        in_specs=[pl.BlockSpec(memory_space=pltpu.VMEM)] * 4,
        out_specs=pl.BlockSpec(memory_space=pltpu.VMEM),
        scratch_shapes=[
            pltpu.VMEM((high * rows, SPAN), F32),
            pltpu.VMEM((keys + 2 * tails, LANES), jnp.int32),
            pltpu.VMEM((rows, keys + 2 * tails, LANES), F32),
        ],
        compiler_params=pltpu.CompilerParams(vmem_limit_bytes=VMEM_LIMIT),
        name="scatter_bias",
    )(kinds_row, ds_main, ds_tail, pos_index)


def norm(values):
    centred = values - jnp.mean(values, -1, keepdims=True)
    spread = jnp.mean(centred * centred, -1, keepdims=True)
    scale = lax.rsqrt(spread + EPS)
    return centred * scale, scale


def norm_back(grad, gain, unit, scale):
    scaled = grad * gain
    first = jnp.mean(scaled, -1, keepdims=True)
    second = jnp.mean(scaled * unit, -1, keepdims=True)
    return (scaled - first - unit * second) * scale


def gelu_pair(v):
    half = jnp.exp(-0.5 * v * v)
    t = 1.0 / (1.0 + 0.23164189 * jnp.abs(v))
    series = t * (0.127414796 + t * (-0.142248368 + t * (0.7107068705 + t * (-0.7265760135 + t * 0.5307027145))))
    tail = series * half
    phi = jnp.where(v >= 0.0, 1.0 - tail, tail)
    return v * phi, phi + v * half * 0.3989422804014327


def head_masks(width):
    lane = lax.broadcasted_iota(jnp.int32, (1, width), 1)
    return [(lane // HEAD) == h for h in range(width // HEAD)]


def keep(mask, values):
    return jnp.where(mask, values, 0.0)


def put_panels(ref, at, values):
    rows = values.shape[0]
    for j in range(values.shape[1] // LANES):
        ref[at + j * rows : at + (j + 1) * rows] = values[:, j * LANES : (j + 1) * LANES].astype(ref.dtype)


def softmax_rows(scores):
    top = jnp.max(scores, 0, keepdims=True)
    e = jnp.exp(scores - top)
    return e * (1.0 / jnp.sum(e, 0, keepdims=True))


def score_back(prob, grad):
    return prob * (grad - jnp.sum(grad * prob, 0, keepdims=True))


def pair_kernel(
    groups_ref,
    x_ref,
    e_gain0, e_gain1, e_shift0, e_shift1,
    e_qkv0, e_qkv1, e_out0, e_out1, e_up0, e_up1, e_down0, e_down1, e_lift0, e_lift1,
    f_gain, f_shift, f_qkv, f_out, f_up, f_down,
    bias_main, bias_tail,
    target_ref, code_ref,
    out_ref, xg_ref, enc_ref, fus_ref, ds_main, ds_tail,
    acc, acc_norm, n1_s, q_s, k_s, v_s, p_s, o_s, n2_s, h_s, act_s, gp_s, res_s,
    win_s, fq, fk, fv, fp, fo, fdq, fdk, fdv, fh, fn2, fdy, fgrad,
):
    step = pl.program_id(0)
    rows = x_ref.shape[2]
    width1 = x_ref.shape[3]
    width2 = f_qkv.shape[0]
    half = rows // 2
    keys = rows
    root = HEAD ** (-0.5)
    masks1 = head_masks(width1)
    masks2 = head_masks(LANES)
    gains1, shifts1 = (e_gain0, e_gain1), (e_shift0, e_shift1)
    w_qkv, w_out, w_up = (e_qkv0, e_qkv1), (e_out0, e_out1), (e_up0, e_up1)
    w_down, w_lift = (e_down0, e_down1), (e_lift0, e_lift1)

    def stack1(values):
        return jnp.concatenate([keep(m, values) for m in masks1], 0).astype(BF)

    def fold1(stacked):
        total = keep(masks1[0], stacked[:half])
        for h in range(1, HEADS1):
            total += keep(masks1[h], stacked[h * half : (h + 1) * half])
        return total

    for l in range(2):
        x = x_ref[l, 0].astype(F32)
        z1, _ = norm(x)
        n1 = (z1 * gains1[l][0, 0:1] + shifts1[l][0, 0:1]).astype(BF)
        n1_s[l] = n1
        qkv = nn(n1, w_qkv[l][0])
        q_s[l] = qkv[:, :width1].astype(BF).astype(F32)
        k_s[l] = qkv[:, width1 : 2 * width1].astype(BF).astype(F32)
        v_s[l] = qkv[:, 2 * width1 :].astype(BF).astype(F32)
        for w in range(2):
            part = slice(w * half, (w + 1) * half)
            scores = nt(k_s[l, part].astype(BF), stack1(q_s[l, part])) * root
            prob = softmax_rows(scores)
            p_s[l, w] = prob
            o_s[l, part] = fold1(tn(prob.astype(BF), v_s[l, part].astype(BF)))
        h = x + nn(o_s[l].astype(BF), w_out[l][0])
        h_s[l] = h
        z2, _ = norm(h)
        n2 = (z2 * gains1[l][0, 1:2] + shifts1[l][0, 1:2]).astype(BF)
        n2_s[l] = n2
        act, slope = gelu_pair(nn(n2, w_up[l][0]))
        act = act.astype(BF)
        act_s[l] = act
        gp_s[l] = slope
        res = (h + nt(act, w_down[l][0])).astype(BF)
        res_s[l] = res
        lifted = nn(res, w_lift[l][0]).astype(BF).astype(F32)
        for w in range(2):
            win_s[w * rows + l * half : w * rows + (l + 1) * half] = lifted[w * half : (w + 1) * half]

    eye = lax.broadcasted_iota(jnp.int32, (rows, rows), 0) == lax.broadcasted_iota(jnp.int32, (rows, rows), 1)
    for l in range(2):
        weight = 0.5 * jnp.exp(0.35 * code_ref[l, 0].astype(F32))
        column = jnp.sum(jnp.where(eye, weight, 0.0), 1, keepdims=True)
        direction = column * target_ref[l, 0].astype(F32)
        for w in range(2):
            fdy[w * rows + l * half : w * rows + (l + 1) * half] = direction[w * half : (w + 1) * half]

    lane_groups = width2 // LANES
    z1, _ = norm(win_s[...])
    fn1 = (z1 * f_gain[0:1] + f_shift[0:1]).astype(BF)
    for t, dest in enumerate((fq, fk, fv)):
        part = nn(fn1, f_qkv[:, t * width2 : (t + 1) * width2]).astype(BF)
        for w in range(2):
            for g in range(lane_groups):
                dest[w * lane_groups + g] = part[w * rows : (w + 1) * rows, g * LANES : (g + 1) * LANES]
    tails = rows - LANES

    def stacks(values):
        main = values[:LANES]
        tail = values[LANES:].astype(F32)
        return [keep(m, main.astype(F32)).astype(BF) for m in masks2] + [
            jnp.concatenate([keep(m, tail) for m in masks2], 0).astype(BF)
        ]

    heads = LANES // HEAD

    def fold2(parts):
        main = keep(masks2[0], parts[0])
        tail = keep(masks2[0], parts[heads][:tails])
        for h in range(1, heads):
            main += keep(masks2[h], parts[h])
            tail += keep(masks2[h], parts[heads][h * tails : (h + 1) * tails])
        return jnp.concatenate([main, tail], 0)

    @pl.loop(0, 2 * lane_groups)
    def _(i):
        key = fk[i]
        val = fv[i]
        outs = []
        for j, query in enumerate(stacks(fq[i])):
            bias = bias_main[i * heads + j] if j < heads else bias_tail[i]
            prob = softmax_rows(nt(key, query) * root + bias)
            if j < heads:
                fp[i, :, j * LANES : (j + 1) * LANES] = prob
            else:
                fp[i, :, j * LANES :] = prob
            outs.append(tn(prob.astype(BF), val))
        fo[i] = fold2(outs).astype(BF)

    def joined(ref):
        return jnp.concatenate(
            [jnp.concatenate([ref[w * lane_groups + g] for g in range(lane_groups)], 1) for w in range(2)], 0
        )

    hidden = win_s[...] + nn(joined(fo), f_out[...])
    fh[...] = hidden
    z2, _ = norm(hidden)
    fn2[...] = (z2 * f_gain[1:2] + f_shift[1:2]).astype(BF)

    @pl.when(step == 0)
    def _():
        acc[...] = jnp.zeros_like(acc)
        acc_norm[...] = jnp.zeros_like(acc_norm)

    blocks = f_up.shape[1] // width2
    win_s_block = width2
    fgrad[...] = jnp.zeros_like(fgrad)

    @pl.loop(0, blocks)
    def _(j):
        at = pl.multiple_of(j * win_s_block, LANES)
        up = f_up[:, pl.ds(at, win_s_block)]
        down = f_down[pl.ds(at, win_s_block), :]
        n2 = fn2[...]
        low = fdy[...].astype(BF)
        act, slope = gelu_pair(nn(n2, up))
        act = act.astype(BF)
        fh[...] += nn(act, down)
        inner_grad = (nt(low, down) * slope).astype(BF)
        acc[pl.ds(8 * width2 + at, win_s_block), :] += tn(act, low)
        acc[pl.ds(4 * width2 + at, win_s_block), :] += tn(n2, inner_grad)
        fgrad[...] += nt(inner_grad, up)

    for l in range(2):
        for w in range(2):
            out_ref[l, 0, w * half : (w + 1) * half] = fh[w * rows + l * half : w * rows + (l + 1) * half].astype(BF)

    hidden = win_s[...] + nn(joined(fo), f_out[...])
    z2, r2 = norm(hidden)
    grad = fgrad[...]
    acc_norm[1:2] += jnp.sum(grad * z2, 0, keepdims=True)
    acc_norm[3:4] += jnp.sum(grad, 0, keepdims=True)
    hidden_grad = fdy[...] + norm_back(grad, f_gain[1:2], z2, r2)
    fgrad[...] = hidden_grad
    low = hidden_grad.astype(BF)
    acc[3 * width2 : 4 * width2] += tn(joined(fo), low)
    att_grad = nt(low, f_out[...]).astype(BF)
    for w in range(2):
        for g in range(lane_groups):
            fo[w * lane_groups + g] = att_grad[w * rows : (w + 1) * rows, g * LANES : (g + 1) * LANES]

    @pl.loop(0, 2 * lane_groups)
    def _(i):
        key = fk[i]
        val = fv[i]
        queries = stacks(fq[i])
        dq = []
        dk = jnp.zeros((keys, LANES), F32)
        dv = jnp.zeros((keys, LANES), F32)
        for j, grads in enumerate(stacks(fo[i])):
            prob = fp[i, :, j * LANES : (j + 1) * LANES] if j < heads else fp[i, :, j * LANES :]
            ds = score_back(prob, nt(val, grads)).astype(BF)
            if j < heads:
                ds_main[i * heads + j] = ds
            else:
                ds_tail[i] = ds
            dv += nn(prob.astype(BF), grads)
            dk += nn(ds, queries[j])
            dq.append(tn(ds, key))
        fdq[i] = (fold2(dq) * root).astype(BF)
        fdk[i] = (dk * root).astype(BF)
        fdv[i] = dv.astype(BF)

    z1, r1 = norm(win_s[...])
    n1 = (z1 * f_gain[0:1] + f_shift[0:1]).astype(BF)
    first = jnp.zeros((2 * rows, width2), F32)
    for t, src in enumerate((fdq, fdk, fdv)):
        part = joined(src)
        acc[t * width2 : (t + 1) * width2] += tn(n1, part)
        first += nt(part, f_qkv[:, t * width2 : (t + 1) * width2])
    acc_norm[0:1] += jnp.sum(first * z1, 0, keepdims=True)
    acc_norm[2:3] += jnp.sum(first, 0, keepdims=True)
    fgrad[...] += norm_back(first, f_gain[0:1], z1, r1)

    @pl.when(step == pl.num_programs(0) - 1)
    def _():
        for n in range(12 * lane_groups):
            block, lane = n // lane_groups, n % lane_groups * LANES
            at = n % (6 * lane_groups) * width2
            panel = acc[block * width2 : (block + 1) * width2, lane : lane + LANES]
            fus_ref[n // (6 * lane_groups), at : at + width2] = panel.astype(BF)
        norms = acc_norm[...]
        norms = jnp.concatenate(
            [norms[:, g * LANES : (g + 1) * LANES] for g in range(lane_groups)] + [jnp.zeros((EXTRA - 4 * lane_groups, LANES), F32)], 0
        )
        at = 6 * lane_groups * width2
        fus_ref[0, at:] = norms.astype(BF)
        fus_ref[1, at:] = jnp.zeros((EXTRA, LANES), BF)

    for l in range(2):
        packed = enc_ref.at[0, l]
        lift_grad = jnp.concatenate(
            [fgrad[w * rows + l * half : w * rows + (l + 1) * half] for w in range(2)], 0
        ).astype(BF)
        put_panels(packed, 12 * width1, tn(res_s[l], lift_grad))
        d_out = nt(lift_grad, w_lift[l][0])
        low = d_out.astype(BF)
        put_panels(packed, 15 * width1, tn(low, act_s[l]))
        inner_grad = (nn(low, w_down[l][0]) * gp_s[l]).astype(BF)
        put_panels(packed, 6 * width1, tn(n2_s[l], inner_grad))
        grad = nt(inner_grad, w_up[l][0])
        z2, r2 = norm(h_s[l])
        norms = [None, jnp.sum(grad * z2, 0, keepdims=True), None, jnp.sum(grad, 0, keepdims=True)]
        hidden_grad = d_out + norm_back(grad, gains1[l][0, 1:2], z2, r2)
        low = hidden_grad.astype(BF)
        out_grad = tn(o_s[l].astype(BF), low)
        att_grad = nt(low, w_out[l][0]).astype(BF).astype(F32)
        parts = []
        for w in range(2):
            part = slice(w * half, (w + 1) * half)
            prob = p_s[l, w]
            grads = stack1(att_grad[part])
            ds = score_back(prob, nt(v_s[l, part].astype(BF), grads)).astype(BF)
            dv = nn(prob.astype(BF), grads)
            dk = nn(ds, stack1(q_s[l, part])) * root
            dq = fold1(tn(ds, k_s[l, part].astype(BF))) * root
            parts.append(jnp.concatenate([dq, dk, dv], 1))
        mixed = jnp.concatenate(parts, 0).astype(BF)
        put_panels(packed, 0, jnp.concatenate([tn(n1_s[l], mixed), out_grad], 1))
        first = nt(mixed, w_qkv[l][0])
        z1, r1 = norm(x_ref[l, 0].astype(F32))
        norms[0] = jnp.sum(first * z1, 0, keepdims=True)
        norms[2] = jnp.sum(first, 0, keepdims=True)
        norms = jnp.pad(jnp.concatenate(norms, 0), ((0, 4), (0, 2 * LANES - width1)))
        norms = jnp.concatenate([norms[:4, :LANES], norms[:4, LANES:], jnp.zeros((8, LANES), F32)], 0)
        packed[21 * width1 : 21 * width1 + EXTRA] = norms.astype(BF)
        packed[21 * width1 + EXTRA :] = jnp.zeros((packed.shape[0] - 21 * width1 - EXTRA, LANES), BF)
        xg_ref[l, 0] = hidden_grad + norm_back(first, gains1[l][0, 0:1], z1, r1)


def pair_blocks(chosen, x, enc, fus, bias_main, bias_tail, target, code):
    _, pairs, rows, width1 = x.shape
    width2 = fus[2].shape[0]
    ff1 = enc[4].shape[2]
    half = rows // 2
    groups = 2 * width2 // LANES
    heads = LANES // HEAD
    tails = rows - LANES
    packed1 = ROWS1
    packed2 = 6 * width2 * width2 // LANES + EXTRA

    def by_group(array, level):
        return pl.BlockSpec((1,) + array.shape[1:], lambda q, s, level=level: (s[level * pairs + q], 0, 0))

    def whole(array):
        return pl.BlockSpec(array.shape, lambda q, s: (0,) * array.ndim, pipeline_mode=pl.Buffered(1))

    enc_args, enc_specs = [], []
    for array in enc:
        for level in range(2):
            enc_args.append(array)
            enc_specs.append(by_group(array, level))
    in_specs = (
        [pl.BlockSpec((2, 1, rows, width1), lambda q, s: (0, q, 0, 0))]
        + enc_specs
        + [whole(a) for a in fus]
        + [
            pl.BlockSpec((groups * heads, rows, LANES), lambda q, s: (q, 0, 0)),
            pl.BlockSpec((groups, rows, heads * tails), lambda q, s: (q, 0, 0)),
            pl.BlockSpec((2, 1, rows, width2), lambda q, s: (0, q, 0, 0)),
            pl.BlockSpec((2, 1, 1, rows), lambda q, s: (0, q, 0, 0)),
        ]
    )
    out_shape = (
        jax.ShapeDtypeStruct((2, pairs, rows, width2), BF),
        jax.ShapeDtypeStruct((2, pairs, rows, width1), F32),
        jax.ShapeDtypeStruct((pairs, 2, packed1, LANES), BF),
        jax.ShapeDtypeStruct((2, packed2, LANES), BF),
        jax.ShapeDtypeStruct((pairs * groups * heads, rows, LANES), BF),
        jax.ShapeDtypeStruct((pairs * groups, rows, heads * tails), BF),
    )
    out_specs = (
        pl.BlockSpec((2, 1, rows, width2), lambda q, s: (0, q, 0, 0)),
        pl.BlockSpec((2, 1, rows, width1), lambda q, s: (0, q, 0, 0)),
        pl.BlockSpec((1, 2, packed1, LANES), lambda q, s: (q, 0, 0, 0)),
        pl.BlockSpec((2, packed2, LANES), lambda q, s: (0, 0, 0)),
        pl.BlockSpec((groups * heads, rows, LANES), lambda q, s: (q, 0, 0)),
        pl.BlockSpec((groups, rows, heads * tails), lambda q, s: (q, 0, 0)),
    )
    stacked = groups // 2 * 0 + HEADS1 * half
    lanes = heads * LANES + heads * tails
    scratch = [
        pltpu.VMEM((12 * width2, width2), F32),
        pltpu.VMEM((4, width2), F32),
        pltpu.VMEM((2, rows, width1), BF),
        pltpu.VMEM((2, rows, width1), F32),
        pltpu.VMEM((2, rows, width1), F32),
        pltpu.VMEM((2, rows, width1), F32),
        pltpu.VMEM((2, 2, half, stacked), F32),
        pltpu.VMEM((2, rows, width1), F32),
        pltpu.VMEM((2, rows, width1), BF),
        pltpu.VMEM((2, rows, width1), F32),
        pltpu.VMEM((2, rows, ff1), BF),
        pltpu.VMEM((2, rows, ff1), F32),
        pltpu.VMEM((2, rows, width1), BF),
        pltpu.VMEM((2 * rows, width2), F32),
        pltpu.VMEM((groups, rows, LANES), BF),
        pltpu.VMEM((groups, rows, LANES), BF),
        pltpu.VMEM((groups, rows, LANES), BF),
        pltpu.VMEM((groups, rows, lanes), F32),
        pltpu.VMEM((groups, rows, LANES), BF),
        pltpu.VMEM((groups, rows, LANES), BF),
        pltpu.VMEM((groups, rows, LANES), BF),
        pltpu.VMEM((groups, rows, LANES), BF),
        pltpu.VMEM((2 * rows, width2), F32),
        pltpu.VMEM((2 * rows, width2), BF),
        pltpu.VMEM((2 * rows, width2), F32),
        pltpu.VMEM((2 * rows, width2), F32),
    ]
    return pl.pallas_call(
        pair_kernel,
        out_shape=out_shape,
        grid_spec=pltpu.PrefetchScalarGridSpec(
            num_scalar_prefetch=1,
            grid=(pairs,),
            in_specs=in_specs,
            out_specs=out_specs,
            scratch_shapes=scratch,
        ),
        compiler_params=pltpu.CompilerParams(vmem_limit_bytes=VMEM_LIMIT),
        name="pair_blocks",
    )(chosen, x, *enc_args, *fus, bias_main, bias_tail, target, code)


def unpack_kernel(
    place_ref, enc_ref, fus_ref, fus_extra, table_in,
    gain_ref, shift_ref, qkv_ref, out_ref, up_ref, down_ref, lift_ref,
    fg_ref, fs_ref, fq_ref, fo_ref, fu_ref, fd_ref, table_ref,
):
    width = qkv_ref.shape[1]

    def panel(n):
        return enc_ref[0, n * width : (n + 1) * width].astype(F32)

    half = LANES // 2
    for n in range(4):
        qkv_ref[0, :, n * LANES : (n + 1) * LANES] = panel(n)
    mixed, last = panel(4), panel(5)
    qkv_ref[0, :, 4 * LANES :] = mixed[:, :half]
    out_ref[0] = jnp.concatenate([mixed[:, half:], last], 1)
    for n in range(6):
        up_ref[0, :, n * LANES : (n + 1) * LANES] = panel(6 + n)
        down_ref[0, :, n * LANES : (n + 1) * LANES] = panel(15 + n)
    for n in range(3):
        lift_ref[0, :, n * LANES : (n + 1) * LANES] = panel(12 + n)
    norms = enc_ref[0, 21 * width : 21 * width + EXTRA].astype(F32)
    norms = jnp.concatenate([norms[0:4], norms[4:8]], 1)[:, :width]
    gain_ref[0] = norms[0:2]
    shift_ref[0] = norms[2:4]
    i = pl.program_id(0)
    size = fo_ref.shape[0]

    def joining(dest):
        for n in range(size // LANES):
            dest[:, n * LANES : (n + 1) * LANES] = fus_ref[0, n * size : (n + 1) * size].astype(F32)

    @pl.when(i < 3)
    def _():
        joining(fq_ref)

    @pl.when(i == 3)
    def _():
        joining(fo_ref)

    @pl.when((i >= 4) & (i < 8))
    def _():
        joining(fu_ref)

    @pl.when(i >= 8)
    def _():
        joining(fd_ref)

    heads, types, count = table_ref.shape

    @pl.when(i == 0)
    def _():
        extra = fus_extra[0].astype(F32)
        extra = jnp.concatenate([extra[4 * n : 4 * n + 4] for n in range(size // LANES)], 1)
        fg_ref[...] = extra[0:2]
        fs_ref[...] = extra[2:4]
        each = heads * types
        per = table_in.shape[1] // each
        for n in range(2 * per):
            wide = min(LANES, count - n * LANES)
            if wide > 0:
                at = n % per * each
                block = table_in[n // per, at : at + each].astype(F32).reshape(heads, types, LANES)
                table_ref[:, :, n * LANES : n * LANES + wide] = block[:, :, :wide]


def unpack(place, enc, fus, table_at, width1, width2, table_shape):
    groups = enc.shape[0]
    heads, types, count = table_shape
    table_rows = -(-count // SPAN) * heads * types
    panels = width2 * width2 // LANES
    sizes1 = [(2, width1), (2, width1), (width1, 3 * width1), (width1, width1), (width1, 4 * width1), (width1, 4 * width1), (width1, 2 * width1)]
    sizes2 = [(2, width2), (2, width2), (width2, 3 * width2), (width2, width2), (width2, 4 * width2), (4 * width2, width2)]
    square = (width2, width2)
    return pl.pallas_call(
        unpack_kernel,
        out_shape=tuple(jax.ShapeDtypeStruct((groups,) + s, F32) for s in sizes1)
        + tuple(jax.ShapeDtypeStruct(s, F32) for s in sizes2)
        + (jax.ShapeDtypeStruct(table_shape, F32),),
        grid_spec=pltpu.PrefetchScalarGridSpec(
            num_scalar_prefetch=1,
            grid=(groups,),
            in_specs=[
                pl.BlockSpec((1,) + enc.shape[1:], lambda i, s: (s[i], 0, 0)),
                pl.BlockSpec((1, panels, LANES), lambda i, s: (i // 6, i % 6, 0)),
                pl.BlockSpec((1, EXTRA, LANES), lambda i, s: (0, 6 * panels // EXTRA, 0)),
                pl.BlockSpec((2, table_rows, LANES), lambda i, s: (0, table_at // table_rows, 0)),
            ],
            out_specs=tuple(pl.BlockSpec((1,) + s, lambda i, s: (i, 0, 0)) for s in sizes1)
            + (
                pl.BlockSpec((2, width2), lambda i, s: (0, 0)),
                pl.BlockSpec((2, width2), lambda i, s: (0, 0)),
                pl.BlockSpec(square, lambda i, s: (0, jnp.minimum(i, 2))),
                pl.BlockSpec(square, lambda i, s: (0, 0)),
                pl.BlockSpec(square, lambda i, s: (0, jnp.clip(i - 4, 0, 3))),
                pl.BlockSpec(square, lambda i, s: (jnp.clip(i - 8, 0, 3), 0)),
                pl.BlockSpec(table_shape, lambda i, s: (0, 0, 0)),
            ),
        ),
        compiler_params=pltpu.CompilerParams(vmem_limit_bytes=VMEM_LIMIT),
        name="unpack",
    )(place, enc, fus, fus, fus)


RING = 4
STRIDES = (16, 4, 1)
ORDERS = ((0, 1, 2), (1, 2, 0), (2, 0, 1))
MESH = pl.DeviceIdType.MESH


def coordinate(axis):
    return lax.rem(lax.axis_index("win") // STRIDES[axis], RING)


def along(axis, hops):
    place = lax.axis_index("win")
    mine = coordinate(axis)
    other = lax.rem(mine + hops, RING)
    return (lax.axis_index("lvl"), place + (other - mine) * STRIDES[axis])


def partner():
    return (1 - lax.axis_index("lvl"), lax.axis_index("win"))


class Copies:
    def __init__(self, send, recv, local):
        self.sems = (send, recv, local)
        self.remote = 0
        self.near = 0
        self.started = []
        self.ready = []

    def send(self, src, dst, device):
        copy = pltpu.make_async_remote_copy(
            src, dst, self.sems[0].at[self.remote], self.sems[1].at[self.remote], device_id=device, device_id_type=MESH
        )
        self.remote += 1
        copy.start()
        self.started.append(copy)
        return copy

    def move(self, src, dst):
        copy = pltpu.make_async_copy(src, dst, self.sems[2].at[self.near])
        self.near += 1
        copy.start()
        return copy

    def finish(self):
        for copy in self.started:
            copy.wait_send()


def add_rows(dest, at, rows, others):
    step = max(s for s in (128, 96, 64, 48, 32, 16) if rows % s == 0)

    @pl.loop(0, rows // step)
    def _(i):
        here = pl.ds(pl.multiple_of(at + i * step, 16), step)
        total = dest[here, :].astype(F32)
        for ref, start in others:
            total += ref[pl.ds(pl.multiple_of(start + i * step, 16), step), :].astype(F32)
        dest[here, :] = total.astype(BF)


def reduce_part(copies, source, own, out, box, base, chunk, order, side):
    big, mid = 16 * chunk, 4 * chunk
    half = big // 2
    axes = order
    here = [coordinate(a) for a in axes]

    def rows(ref, at, size):
        return ref.at[pl.ds(pl.multiple_of(at, 16), size)]

    def top(hops):
        return base + lax.rem(here[0] + hops, RING) * big

    at_mine = top(0)
    first = [0, half]
    whole = [big, 2 * big]
    up = along(axes[0], 1)
    down = along(axes[0], RING - 1)
    m1 = (
        copies.send(rows(source, top(2), half), rows(box, first[0], half), up),
        copies.send(rows(source, top(2) + half, half), rows(box, first[1], half), down),
    )
    m2 = (
        copies.send(rows(source, top(1) + half, half), rows(box, whole[0] + half, half), up),
        copies.send(rows(source, top(3), half), rows(box, whole[1], half), down),
    )
    yield
    m1[0].wait_recv()
    add_rows(own, top(1), half, [(box, first[0])])
    m3a = copies.send(rows(own, top(1), half), rows(box, whole[0], half), up)
    m1[1].wait_recv()
    add_rows(own, top(3) + half, half, [(box, first[1])])
    m3b = copies.send(rows(own, top(3) + half, half), rows(box, whole[1] + half, half), down)
    yield
    for copy in m2 + (m3a, m3b):
        copy.wait_recv()
    add_rows(own, at_mine, big, [(box, whole[0]), (box, whole[1])])

    start, size, slot = at_mine, mid, 3 * big
    for axis, place in ((axes[1], here[1]), (axes[2], here[2])):
        sent = []
        for n, hops in enumerate((1, 3, 2)):
            at = start + lax.rem(place + hops, RING) * size
            sent.append(copies.send(rows(own, at, size), rows(box, slot + n * size, size), along(axis, hops)))
        yield
        for copy in sent:
            copy.wait_recv()
        start = start + place * size
        add_rows(own, start, size, [(box, slot + n * size) for n in range(3)])
        slot += 3 * size
        size //= 4

    size = chunk
    place = rows(out, start, size)
    kept = copies.move(rows(own, start, size), place)
    sent = [copies.send(rows(own, start, size), place, along(axes[2], hops)) for hops in (1, 3, 2)]
    yield
    kept.wait()
    for copy in sent:
        copy.wait_recv()
    start = at_mine + here[1] * mid
    place = rows(out, start, mid)
    sent = [copies.send(place, place, along(axes[1], hops)) for hops in (1, 3, 2)]
    yield
    for copy in sent:
        copy.wait_recv()
    mine = rows(out, at_mine, big)
    sent = [copies.send(mine, mine, up), copies.send(mine, mine, down)]
    over = [copies.send(mine, mine, partner())]
    yield
    sent[0].wait_recv()
    below = rows(out, top(3), half)
    onward = [copies.send(below, below, up)]
    lower = rows(out, top(3), big)
    over.append(copies.send(lower, lower, partner()))
    sent[1].wait_recv()
    above = rows(out, top(1) + half, half)
    onward.append(copies.send(above, above, down))
    upper = rows(out, top(1), big)
    over.append(copies.send(upper, upper, partner()))
    yield
    for copy in onward:
        copy.wait_recv()
    last = rows(out, top(2), big)
    over.append(copies.send(last, last, partner()))
    yield
    for copy in over:
        copy.wait_recv()


def advance(parts):
    for part in parts:
        next(part, None)


def reduce_kernel(
    chunks1, chunks2, table_at, enc_ref, fus_ref, table_ref, enc_out, fus_out, own1, own2, peer, *rest
):
    boxes, (send, recv, local) = rest[:-3], rest[-3:]
    side = lax.axis_index("lvl")
    barrier = pltpu.get_barrier_semaphore()
    friends = [along(axis, hops) for axis in range(3) for hops in (1, 2, 3)] + [partner()]
    for device in friends:
        pl.semaphore_signal(barrier, inc=1, device_id=device, device_id_type=MESH)
    pl.semaphore_wait(barrier, len(friends))
    copies = Copies(send, recv, local)
    fus_rows, table_rows = fus_ref.shape[1], table_ref.shape[1]
    give = [
        copies.send(fus_ref.at[1 - side], peer.at[:fus_rows], partner()),
        copies.send(table_ref.at[1 - side], peer.at[table_at : table_at + table_rows], partner()),
    ]
    taken = [
        copies.move(fus_ref.at[side], own2.at[:fus_rows]),
        copies.move(table_ref.at[side], own2.at[table_at : table_at + table_rows]),
    ]
    loaded = copies.move(enc_ref, own1)
    parts1, parts2 = [], []
    base = 0
    for n, chunk in enumerate(chunks1):
        parts1.append(
            reduce_part(copies, enc_ref, own1, enc_out.at[side], boxes[n], base, chunk, ORDERS[n], side)
        )
        base += 64 * chunk
    base = 0
    for n, chunk in enumerate(chunks2):
        parts2.append(
            reduce_part(copies, own2, own2, fus_out.at[side], boxes[len(chunks1) + n], base, chunk, ORDERS[n], side)
        )
        base += 64 * chunk
    advance(parts1)
    end = table_at + table_rows
    own2[fus_rows:table_at] = jnp.zeros((table_at - fus_rows, LANES), BF)
    own2[end:] = jnp.zeros((own2.shape[0] - end, LANES), BF)
    for copy in taken:
        copy.wait()
    for copy in give:
        copy.wait_recv()
    add_rows(own2, 0, fus_rows, [(peer, 0)])
    add_rows(own2, table_at, table_rows, [(peer, table_at)])
    advance(parts2)
    loaded.wait()
    for _ in range(9):
        advance(parts1)
        advance(parts2)
    copies.finish()


def reduce_all(enc, fus, table, chunks1, chunks2, table_at):
    rows1, rows2 = 64 * sum(chunks1), 64 * sum(chunks2)
    remote = 2 + 26 * (len(chunks1) + len(chunks2))
    anywhere = pl.BlockSpec(memory_space=pl.ANY)
    return pl.pallas_call(
        functools.partial(reduce_kernel, chunks1, chunks2, table_at),
        out_shape=(
            jax.ShapeDtypeStruct((2, rows1, LANES), BF),
            jax.ShapeDtypeStruct((2, rows2, LANES), BF),
        ),
        in_specs=[anywhere] * 3,
        out_specs=(anywhere, anywhere),
        scratch_shapes=[
            pltpu.VMEM((rows1, LANES), BF),
            pltpu.VMEM((rows2, LANES), BF),
            pltpu.VMEM((rows2, LANES), BF),
        ]
        + [pltpu.VMEM((63 * chunk, LANES), BF) for chunk in chunks1 + chunks2]
        + [
            pltpu.SemaphoreType.DMA((remote,)),
            pltpu.SemaphoreType.DMA((remote,)),
            pltpu.SemaphoreType.DMA((3 + len(chunks1) + len(chunks2),)),
        ],
        compiler_params=pltpu.CompilerParams(
            vmem_limit_bytes=VMEM_LIMIT, collective_id=0, has_side_effects=True
        ),
        name="reduce_all",
    )(enc, fus, table)


def shards(
    tokens_in,
    enc_gains,
    enc_shifts,
    enc_qkv,
    enc_out,
    enc_up,
    enc_down,
    enc_lift,
    fus_gains,
    fus_shifts,
    fus_qkv,
    fus_out,
    fus_up,
    fus_down,
    fus_table,
    target,
    loss_code,
    level_group,
    window_type,
    pos_index,
):
    pairs = target.shape[1]
    all_rows = level_group.shape[0]
    side = lax.axis_index("lvl")
    heads = fus_table.shape[0]
    x = lax.all_to_all(tokens_in, "lvl", split_axis=1, concat_axis=0, tiled=True)
    held = level_group.reshape(2, 2, pairs)
    chosen = lax.dynamic_index_in_dim(held, side, 1, keepdims=False).reshape(2 * pairs)
    kinds = jnp.repeat(window_type.reshape(-1), heads)[None]
    bias_main, bias_tail = gather_bias(kinds, fus_table, pos_index)
    output, x_grad, enc, fus, ds_main, ds_tail = pair_blocks(
        chosen,
        x,
        (enc_gains, enc_shifts, enc_qkv, enc_out, enc_up, jnp.swapaxes(enc_down, 1, 2), enc_lift),
        (fus_gains, fus_shifts, fus_qkv, fus_out, fus_up, fus_down),
        bias_main,
        bias_tail,
        target,
        loss_code[:, :, None],
    )
    table = scatter_bias(kinds, ds_main, ds_tail, pos_index, fus_table.shape)
    x_grad = lax.all_to_all(x_grad, "lvl", split_axis=0, concat_axis=1, tiled=True)

    table_rows = table.shape[1]
    table_at = -(-fus.shape[1] // table_rows) * table_rows
    enc = enc.reshape(-1, LANES)
    chunks1 = cut(enc.shape[0])
    enc, fus = reduce_all(enc, fus, table, chunks1, cut(table_at + table_rows), table_at)

    order = jnp.transpose(held, (1, 2, 0)).reshape(-1)
    spot = jnp.arange(all_rows, dtype=jnp.int32)
    place = jnp.sum(jnp.where(order[None] == spot[:, None], spot[None], 0), 1)
    grads = unpack(
        place, enc.reshape(all_rows, ROWS1, LANES), fus, table_at, enc_out.shape[1], fus_out.shape[0], fus_table.shape
    )
    return (output, x_grad, *grads[:5], jnp.swapaxes(grads[5], 1, 2), *grads[6:])


def cut(rows):
    tiles = -(-rows // (64 * 16))
    return tuple(16 * ((tiles + 2 - n) // 3) for n in range(3))


def solution(mesh):
    copied = P()
    in_specs = (
        (P("lvl", None, "win", None),)
        + (copied,) * 14
        + (P(None, "lvl", "win", None), P(None, "lvl", "win"), copied, P("lvl", "win"), copied)
    )
    out_specs = (P(None, "lvl", "win", None), P("lvl", None, "win", None)) + (copied,) * 14
    return jax.shard_map(shards, mesh=mesh, in_specs=in_specs, out_specs=out_specs, check_vma=False)
```

```python
import functools

import jax
import jax.numpy as jnp
from jax import lax
from jax.experimental import pallas as pl
from jax.experimental.pallas import tpu as pltpu
from jax.sharding import PartitionSpec as P

HEADS1 = 6
HEADS2 = 12
HEAD = 32
EPS = 1e-05
LANES = 128
SPAN = 256
PER = 4
UNROLL = 6
ROWS1 = 4096
CHUNKS1 = (48, 48, 32)
CHUNKS2 = (48, 32, 32)
CHUNKS3 = (16, 16, 16)
EXTRA = 16
VMEM_LIMIT = 60 * 1024 * 1024

BF = jnp.bfloat16
F32 = jnp.float32


def nn(a, b):
    return lax.dot_general(a, b, (((1,), (0,)), ((), ())), preferred_element_type=F32)


def nt(a, b):
    return lax.dot_general(a, b, (((1,), (1,)), ((), ())), preferred_element_type=F32)


def tn(a, b):
    return lax.dot_general(a, b, (((0,), (0,)), ((), ())), preferred_element_type=F32)


RING = 4
STRIDES = (16, 4, 1)
ORDERS = ((0, 1, 2), (1, 2, 0), (2, 0, 1))
MESH = pl.DeviceIdType.MESH
MESSAGES = 26


def coordinate(axis):
    return lax.rem(lax.axis_index("win") // STRIDES[axis], RING)


def along(axis, hops):
    place = lax.axis_index("win")
    mine = coordinate(axis)
    other = lax.rem(mine + hops, RING)
    return (lax.axis_index("lvl"), place + (other - mine) * STRIDES[axis])


def partner():
    return (1 - lax.axis_index("lvl"), lax.axis_index("win"))


def add_rows(dest, at, rows, others):
    step = max(s for s in (128, 112, 96, 64, 48, 32, 16) if rows % s == 0)

    @pl.loop(0, rows // step)
    def _(i):
        here = pl.ds(pl.multiple_of(at + i * step, 16), step)
        total = dest[here, :].astype(F32)
        for ref, start in others:
            total += ref[pl.ds(pl.multiple_of(start + i * step, 16), step), :].astype(F32)
        dest[here, :] = total.astype(BF)


def rows_of(ref, at, size):
    return ref.at[pl.ds(pl.multiple_of(at, 16), size)]


class Part:
    STAGES = 10

    def __init__(self, own, out, box, send, recv, keep, base, chunk, order, ring=True):
        self.own, self.out, self.box, self.send, self.recv, self.keep = own, out, box, send, recv, keep
        self.axes, self.ring = order, ring
        self.here = [coordinate(a) for a in order]
        self.big, self.mid, self.chunk = 16 * chunk, 4 * chunk, chunk
        self.base = base
        self.first = base + self.here[0] * self.big
        self.second = self.first + self.here[1] * self.mid
        self.third = self.second + self.here[2] * chunk

    def top(self, hops):
        return self.base + lax.rem(self.here[0] + hops, RING) * self.big

    def message(self, n):
        big, mid, chunk = self.big, self.mid, self.chunk
        half = big // 2
        up, down = (self.axes[0], 1), (self.axes[0], RING - 1)
        own, out, box = self.own, self.out, self.box
        after = 3 * big
        if n < 6 and not self.ring:
            hops = (1, 3, 2)[n]
            src, dst, to = rows_of(own, self.top(hops), big), rows_of(box, n * big, big), (self.axes[0], hops)
        elif n == 0:
            src, dst, to = rows_of(own, self.top(2), half), rows_of(box, 0, half), up
        elif n == 1:
            src, dst, to = rows_of(own, self.top(2) + half, half), rows_of(box, half, half), down
        elif n == 2:
            src, dst, to = rows_of(own, self.top(1) + half, half), rows_of(box, big + half, half), up
        elif n == 3:
            src, dst, to = rows_of(own, self.top(3), half), rows_of(box, 2 * big, half), down
        elif n == 4:
            src, dst, to = rows_of(own, self.top(1), half), rows_of(box, big, half), up
        elif n == 5:
            src, dst, to = rows_of(own, self.top(3) + half, half), rows_of(box, 2 * big + half, half), down
        elif n < 9:
            hops = (1, 3, 2)[n - 6]
            at = self.first + lax.rem(self.here[1] + hops, RING) * mid
            src, dst, to = rows_of(own, at, mid), rows_of(box, after + (n - 6) * mid, mid), (self.axes[1], hops)
        elif n < 12:
            hops = (1, 3, 2)[n - 9]
            at = self.second + lax.rem(self.here[2] + hops, RING) * chunk
            src, to = rows_of(own, at, chunk), (self.axes[2], hops)
            dst = rows_of(box, after + 3 * mid + (n - 9) * chunk, chunk)
        elif n < 15:
            src, dst = rows_of(own, self.third, chunk), rows_of(out, self.third, chunk)
            to = (self.axes[2], (1, 3, 2)[n - 12])
        elif n < 18:
            src = dst = rows_of(out, self.second, mid)
            to = (self.axes[1], (1, 3, 2)[n - 15])
        elif n < 22 and not self.ring:
            src = dst = rows_of(out, self.first, big)
            to = (self.axes[0], (1, 3, 2)[n - 18])
        elif n < 20:
            src = dst = rows_of(out, self.first, big)
            to = (up, down)[n - 18]
        elif n == 20:
            src = dst = rows_of(out, self.top(3), half)
            to = up
        elif n == 21:
            src = dst = rows_of(out, self.top(1) + half, half)
            to = down
        else:
            src = dst = rows_of(out, self.top((0, 3, 1, 2)[n - 22]), big)
            to = None
        return pltpu.make_async_remote_copy(
            src,
            dst,
            self.send.at[n],
            self.recv.at[n],
            device_id=partner() if to is None else along(*to),
            device_id_type=MESH,
        )

    def start(self, *numbers):
        for n in numbers:
            self.message(n).start()

    def wait(self, *numbers):
        for n in numbers:
            self.message(n).wait()

    def kept(self):
        return pltpu.make_async_copy(
            rows_of(self.own, self.third, self.chunk), rows_of(self.out, self.third, self.chunk), self.keep
        )

    def stage(self, k):
        big, mid, chunk, own, box = self.big, self.mid, self.chunk, self.own, self.box
        half, after = big // 2, 3 * big
        if k == 0:
            self.start(*((0, 1, 2, 3) if self.ring else (0, 1, 2)))
        elif k == 1 and self.ring:
            self.wait(0)
            add_rows(own, self.top(1), half, [(box, 0)])
            self.start(4)
            self.wait(1)
            add_rows(own, self.top(3) + half, half, [(box, half)])
            self.start(5)
        elif k == 2:
            if self.ring:
                self.wait(2, 3, 4, 5)
            else:
                self.wait(0, 1, 2)
            add_rows(own, self.first, big, [(box, n * big) for n in ((1, 2) if self.ring else (0, 1, 2))])
            self.start(6, 7, 8)
        elif k == 3:
            self.wait(6, 7, 8)
            add_rows(own, self.second, mid, [(box, after + n * mid) for n in range(3)])
            self.start(9, 10, 11)
        elif k == 4:
            self.wait(9, 10, 11)
            add_rows(own, self.third, chunk, [(box, after + 3 * mid + n * chunk) for n in range(3)])
            self.kept().start()
            self.start(12, 13, 14)
        elif k == 5:
            self.kept().wait()
            self.wait(12, 13, 14)
            self.start(15, 16, 17)
        elif k == 6:
            self.wait(15, 16, 17)
            self.start(*((18, 19, 22) if self.ring else (18, 19, 20, 22)))
        elif k == 7 and self.ring:
            self.wait(18)
            self.start(20, 23)
            self.wait(19)
            self.start(21, 24)
        elif k == 8:
            if self.ring:
                self.wait(20, 21)
                self.start(25)
            else:
                self.wait(18, 19, 20)
                self.start(23, 24, 25)
        elif k == 9:
            self.wait(22, 23, 24, 25)


def parts_of(chunks, own, out, boxes, sems, ring=True):
    parts, base = [], 0
    for n, chunk in enumerate(chunks):
        send, recv, keep = (sem.at[n] for sem in sems)
        parts.append(Part(own, out, boxes[n], send, recv, keep, base, chunk, ORDERS[n], ring))
        base += 64 * chunk
    return parts


def run(parts, k):
    for part in parts:
        part.stage(k)


def type_picker(kinds, heads, types):
    shape = (heads * types, len(kinds) * heads)
    row = lax.broadcasted_iota(jnp.int32, shape, 0)
    column = lax.broadcasted_iota(jnp.int32, shape, 1)
    kind = jnp.full(shape, kinds[-1], jnp.int32)
    for n in reversed(range(len(kinds) - 1)):
        kind = jnp.where(column < (n + 1) * heads, kinds[n], kind)
    same_head = (row // types) == (column % heads)
    return (same_head & ((row % types) == kind)).astype(F32).astype(BF)


def lay_positions(pos_ref, all_pos):
    keys = pos_ref.shape[0]
    tails = keys - LANES
    all_pos[:keys] = pos_ref[...].astype(F32).T[:, :LANES].astype(jnp.int32)
    all_pos[keys : keys + tails] = pos_ref[LANES:, :LANES]
    all_pos[keys + tails :] = jnp.full((tails, LANES), -1, jnp.int32)
    all_pos[keys + tails :, : keys - LANES] = pos_ref[LANES:, LANES:]


def one_hot_of(pos):
    low = jnp.bitwise_and(pos, SPAN - 1)
    return (lax.broadcasted_iota(jnp.int32, (SPAN, pos.shape[1]), 0) == low).astype(F32).astype(BF)


def spread_table(picker, table_ref, t2):
    rows, count = picker.shape[1], table_ref.shape[1]
    for k in range(t2.shape[0] // rows):
        width = min(SPAN, count - k * SPAN)
        part = table_ref[:, k * SPAN : k * SPAN + width].astype(BF)
        t2[k * rows : (k + 1) * rows, :width] = tn(picker, part).astype(BF)
        if width < SPAN:
            t2[k * rows : (k + 1) * rows, width:] = jnp.zeros((rows, SPAN - width), BF)


def look_up(t2, all_pos, dest, first, last):
    rows = dest.shape[0]
    high = t2.shape[0] // rows

    @pl.loop(first, last)
    def _(i):
        at = pl.multiple_of(i * 8, 8)
        eight = all_pos[pl.ds(at, 8), :]
        for s in range(0, 8, PER):
            pos = jnp.concatenate([eight[s + j : s + j + 1] for j in range(PER)], 1)
            top = jnp.right_shift(pos, 8)
            spread = nn(t2[...], one_hot_of(pos))
            picked = jnp.zeros((rows, PER * LANES), F32)
            for k in range(high):
                picked = jnp.where(top == k, spread[k * rows : (k + 1) * rows], picked)
            for j in range(PER):
                dest[:, pl.ds(at + s + j, 1), :] = picked[:, j * LANES : (j + 1) * LANES].reshape(rows, 1, LANES)


def turn_tails(bias, bias_tail, keys):
    tails = keys - LANES
    per = bias_tail.shape[2] // tails
    for i in range(bias_tail.shape[0]):
        lines = bias[i * per : (i + 1) * per, keys : keys + tails].reshape(per * tails, LANES)
        bias_tail[i, :LANES] = lines.T
        lines = bias[i * per : (i + 1) * per, keys + tails : keys + 2 * tails].reshape(per * tails, LANES)
        bias_tail[i, LANES:] = lines.T[: keys - LANES]


def lay_terms(ds_main, ds_tail, lines):
    rows, keys = ds_main.shape[:2]
    tails = keys - LANES
    per = ds_tail.shape[2] // tails

    @pl.loop(0, ds_tail.shape[0])
    def _(i):
        at = pl.ds(i * per, per)
        lines[at, :keys] = ds_main[at].astype(F32)
        block = ds_tail[i].astype(F32)
        lines[at, keys : keys + tails] = block[:LANES].T.reshape(per, tails, LANES)
        lines[at, keys + tails : keys + 2 * tails] = jnp.zeros((per, tails, LANES), F32)
        lines[at, keys + tails : keys + 2 * tails, : keys - LANES] = block[LANES:].T.reshape(per, tails, keys - LANES)


def add_terms(acc, all_pos, lines, first, last):
    rows = lines.shape[0]
    high = acc.shape[0] // rows

    @pl.loop(first, last)
    def _(i):
        at = pl.multiple_of(i * 8, 8)
        eight = all_pos[pl.ds(at, 8), :]
        total = None
        for s in range(0, 8, PER):
            pos = jnp.concatenate([eight[s + j : s + j + 1] for j in range(PER)], 1)
            terms = jnp.concatenate([lines[:, pl.ds(at + s + j, 1), :].reshape(rows, LANES) for j in range(PER)], 1)
            top = jnp.right_shift(pos, 8)
            parts = jnp.concatenate([jnp.where(top == k, terms, 0.0) for k in range(high)], 0)
            term = nt(parts.astype(BF), one_hot_of(pos))
            total = term if total is None else total + term
        acc[...] += total


def norm(values):
    centred = values - jnp.mean(values, -1, keepdims=True)
    spread = jnp.mean(centred * centred, -1, keepdims=True)
    scale = lax.rsqrt(spread + EPS)
    return centred * scale, scale


def norm_back(grad, gain, unit, scale):
    scaled = grad * gain
    first = jnp.mean(scaled, -1, keepdims=True)
    second = jnp.mean(scaled * unit, -1, keepdims=True)
    return (scaled - first - unit * second) * scale


def gelu_pair(v):
    half = jnp.exp(-0.5 * v * v)
    t = 1.0 / (1.0 + 0.23164189 * jnp.abs(v))
    series = t * (0.127414796 + t * (-0.142248368 + t * (0.7107068705 + t * (-0.7265760135 + t * 0.5307027145))))
    tail = series * half
    phi = jnp.where(v >= 0.0, 1.0 - tail, tail)
    return v * phi, phi + v * half * 0.3989422804014327


def head_masks(width):
    lane = lax.broadcasted_iota(jnp.int32, (1, width), 1)
    return [(lane // HEAD) == h for h in range(width // HEAD)]


def keep(mask, values):
    return jnp.where(mask, values, 0.0)


def put_panels(ref, at, values):
    rows = values.shape[0]
    for j in range(values.shape[1] // LANES):
        ref[at + j * rows : at + (j + 1) * rows] = values[:, j * LANES : (j + 1) * LANES].astype(ref.dtype)


def softmax_rows(scores):
    top = jnp.max(scores, 0, keepdims=True)
    e = jnp.exp(scores - top)
    return e * (1.0 / jnp.sum(e, 0, keepdims=True))


def score_back(prob, grad):
    return prob * (grad - jnp.sum(grad * prob, 0, keepdims=True))


def layer_kernel(
    kinds_ref, tokens_ref,
    e_gain0, e_gain1, e_shift0, e_shift1,
    e_qkv0, e_qkv1, e_out0, e_out1, e_up0, e_up1, e_down0, e_down1, e_lift0, e_lift1,
    f_gain, f_shift, f_qkv, f_out, f_up, f_down,
    table_ref, pos_ref, target_ref, code_ref,
    out_ref, xg_out, e_all, f_all, t_all,
    x_s, xg_s, n1_s, q_s, k_s, v_s, p_s, o_s, n2_s, h_s, act_s, gp_s, res_s,
    win_s, fq, fk, fv, fp, fo, fdq, fdk, fdv, fh, fn2, fdy, fgrad,
    t2, all_pos, bias_main, bias_tail, ds_main, ds_tail, acc_t,
    acc, acc_norm, own_e, own_f, give_f, peer_f, own_t, give_t, peer_t,
    be0, be1, be2, bf0, bf1, bf2, bt0, bt1, bt2,
    se, re, ke, sf, rf, kf, st, rt, kt, misc_send, misc_recv, misc_near,
):
    boxes_e, boxes_f, boxes_t = (be0, be1, be2), (bf0, bf1, bf2), (bt0, bt1, bt2)
    sems_e, sems_f, sems_t = (se, re, ke), (sf, rf, kf), (st, rt, kt)
    step = pl.program_id(0)
    side = lax.axis_index("lvl")
    rows = x_s.shape[2]
    width1 = x_s.shape[3]
    width2 = f_qkv.shape[0]
    half = rows // 2
    keys = rows
    root = HEAD ** (-0.5)
    masks1 = head_masks(width1)
    masks2 = head_masks(LANES)
    picks2 = [m.astype(F32).astype(BF) for m in masks2]
    gains1, shifts1 = (e_gain0, e_gain1), (e_shift0, e_shift1)
    w_qkv, w_out, w_up = (e_qkv0, e_qkv1), (e_out0, e_out1), (e_up0, e_up1)
    w_down, w_lift = (e_down0, e_down1), (e_lift0, e_lift1)

    pairs = x_s.shape[1]
    heads_all = width2 // HEAD
    types = table_ref.shape[0] // heads_all
    all_terms = 2 * pairs * heads_all
    panels = 12 * width2 // LANES
    halves = panels // 2 * width2

    def encoder(q):
        return parts_of(CHUNKS1, own_e.at[q], e_all.at[side, q], [b.at[q] for b in boxes_e], [s.at[q] for s in sems_e])

    def joining():
        return parts_of(CHUNKS2, own_f, f_all.at[side], boxes_f, sems_f)

    def table():
        return parts_of(CHUNKS3, own_t, t_all.at[side], boxes_t, sems_t, ring=False)

    def tick(new=None, old=None):
        if new is not None:

            @pl.when(step >= 1)
            def _():
                run(encoder(step - 1), new)

        if old is not None:

            @pl.when(step == 2)
            def _():
                run(encoder(0), old)

    def remote(src, dst, n):
        return pltpu.make_async_remote_copy(
            src, dst, misc_send.at[n], misc_recv.at[n], device_id=partner(), device_id_type=MESH
        )

    def near(src, dst, n):
        return pltpu.make_async_copy(src, dst, misc_near.at[n])

    def tokens():
        given = remote(tokens_ref.at[0, pl.ds((1 - side) * pairs, pairs)], x_s.at[side], 0)
        taken = near(tokens_ref.at[0, pl.ds(side * pairs, pairs)], x_s.at[side], 0)
        return given, taken

    def tokens_grad(q):
        given = remote(xg_s.at[1 - side, q], xg_out.at[0, side * pairs + q], 1 + q)
        taken = near(xg_s.at[side, q], xg_out.at[0, side * pairs + q], 1 + q)
        return given, taken

    def joining_half():
        return remote(give_f, peer_f, 1 + pairs)

    def table_half():
        return remote(give_t.at[1 - side], peer_t, 2 + pairs)

    @pl.when(step == 0)
    def _():
        barrier = pltpu.get_barrier_semaphore()
        friends = [along(axis, hops) for axis in range(3) for hops in (1, 2, 3)] + [partner()]
        for device in friends:
            pl.semaphore_signal(barrier, inc=1, device_id=device, device_id_type=MESH)
        pl.semaphore_wait(barrier, len(friends))
        for copy in tokens():
            copy.start()
        lay_positions(pos_ref, all_pos)
        for q in range(pairs):
            picker = type_picker([kinds_ref[q, w] for w in range(2)], heads_all, types)
            spread_table(picker, table_ref, t2.at[q])
        acc[...] = jnp.zeros_like(acc)
        acc_norm[...] = jnp.zeros_like(acc_norm)

    eights = (keys + 2 * (keys - LANES)) // 8
    look_up(t2.at[step], all_pos, bias_main, 0, eights // 2)
    tick(new=1, old=7)
    look_up(t2.at[step], all_pos, bias_main, eights // 2, eights)
    turn_tails(bias_main, bias_tail, keys)
    tick(new=2)

    @pl.when(step == 0)
    def _():
        for copy in tokens():
            copy.wait()

    def stack1(values):
        return jnp.concatenate([keep(m, values) for m in masks1], 0).astype(BF)

    def fold1(stacked):
        total = keep(masks1[0], stacked[:half])
        for h in range(1, HEADS1):
            total += keep(masks1[h], stacked[h * half : (h + 1) * half])
        return total

    both = range(2)
    windows = [(l, w, slice(w * half, (w + 1) * half)) for l in both for w in both]
    xs = [x_s[l, step].astype(F32) for l in both]
    for l in both:
        z1, _ = norm(xs[l])
        n1_s[l] = (z1 * gains1[l][0, 0:1] + shifts1[l][0, 0:1]).astype(BF)
    for l in both:
        qkv = nn(n1_s[l], w_qkv[l][0])
        q_s[l] = qkv[:, :width1].astype(BF).astype(F32)
        k_s[l] = qkv[:, width1 : 2 * width1].astype(BF).astype(F32)
        v_s[l] = qkv[:, 2 * width1 :].astype(BF).astype(F32)
    for l, w, part in windows:
        p_s[l, w] = softmax_rows(nt(k_s[l, part].astype(BF), stack1(q_s[l, part])) * root)
    for l, w, part in windows:
        o_s[l, part] = fold1(tn(p_s[l, w].astype(BF), v_s[l, part].astype(BF)))
    tick(old=8)
    for l in both:
        h = x_s[l, step].astype(F32) + nn(o_s[l].astype(BF), w_out[l][0])
        h_s[l] = h
        z2, _ = norm(h)
        n2_s[l] = (z2 * gains1[l][0, 1:2] + shifts1[l][0, 1:2]).astype(BF)
    for l in both:
        act, slope = gelu_pair(nn(n2_s[l], w_up[l][0]))
        act_s[l] = act.astype(BF)
        gp_s[l] = slope
    for l in both:
        res_s[l] = (h_s[l] + nt(act_s[l], w_down[l][0])).astype(BF)
    for l in both:
        lifted = nn(res_s[l], w_lift[l][0]).astype(BF).astype(F32)
        for w in range(2):
            win_s[w * rows + l * half : w * rows + (l + 1) * half] = lifted[w * half : (w + 1) * half]
    tick(new=3, old=9)

    eye = lax.broadcasted_iota(jnp.int32, (rows, rows), 0) == lax.broadcasted_iota(jnp.int32, (rows, rows), 1)
    for l in range(2):
        codes = code_ref[l].astype(F32)
        chosen = lax.broadcasted_iota(jnp.int32, codes.shape, 0) == step
        weight = 0.5 * jnp.exp(0.35 * jnp.sum(jnp.where(chosen, codes, 0.0), 0, keepdims=True))
        column = jnp.sum(jnp.where(eye, weight, 0.0), 1, keepdims=True)
        direction = column * target_ref[l, 0].astype(F32)
        for w in range(2):
            fdy[w * rows + l * half : w * rows + (l + 1) * half] = direction[w * half : (w + 1) * half]

    lane_groups = width2 // LANES
    z1, _ = norm(win_s[...])
    fn1 = (z1 * f_gain[0:1] + f_shift[0:1]).astype(BF)
    for t, dest in enumerate((fq, fk, fv)):
        part = nn(fn1, f_qkv[:, t * width2 : (t + 1) * width2]).astype(BF)
        for w in range(2):
            for g in range(lane_groups):
                dest[w * lane_groups + g] = part[w * rows : (w + 1) * rows, g * LANES : (g + 1) * LANES]
    tails = rows - LANES

    heads = LANES // HEAD
    lanes = heads * LANES + heads * tails
    spans = [slice(j * LANES, min((j + 1) * LANES, lanes)) for j in range(heads + 1)]

    def stack2(values):
        main, tail = values[:LANES], values[LANES:]
        return jnp.concatenate([main * m for m in picks2] + [tail * m for m in picks2], 0)

    def fold2(stacked):
        main = keep(masks2[0], stacked[:LANES])
        tail = keep(masks2[0], stacked[heads * LANES : heads * LANES + tails])
        for h in range(1, heads):
            main += keep(masks2[h], stacked[h * LANES : (h + 1) * LANES])
            tail += keep(masks2[h], stacked[heads * LANES + h * tails : heads * LANES + (h + 1) * tails])
        return jnp.concatenate([main, tail], 0)

    @pl.loop(0, 2 * lane_groups, unroll=UNROLL)
    def _(i):
        scores = nt(fk[i], stack2(fq[i]))
        probs = []
        for j, span in enumerate(spans):
            bias = bias_main[i * heads + j, :keys] if j < heads else bias_tail[i]
            prob = softmax_rows(scores[:, span] * root + bias)
            fp[i, :, span] = prob
            probs.append(prob.astype(BF))
        fo[i] = fold2(tn(jnp.concatenate(probs, 1), fv[i])).astype(BF)

    tick(new=4)

    def joined(ref):
        return jnp.concatenate(
            [jnp.concatenate([ref[w * lane_groups + g] for g in range(lane_groups)], 1) for w in range(2)], 0
        )

    hidden = win_s[...] + nn(joined(fo), f_out[...])
    fh[...] = hidden
    z2, _ = norm(hidden)
    fn2[...] = (z2 * f_gain[1:2] + f_shift[1:2]).astype(BF)

    def add_panels(n, values):
        for j in range(values.shape[1] // LANES):
            panel = values[:, j * LANES : (j + 1) * LANES]
            acc[2 * (n + j) : 2 * (n + j) + 2] += panel.reshape(2, width2 // 2, LANES)

    blocks = f_up.shape[1] // width2
    fgrad[...] = jnp.zeros_like(fgrad)

    per_block = width2 // LANES
    for j in range(blocks):
        up = f_up[:, j * width2 : (j + 1) * width2]
        down = f_down[j * width2 : (j + 1) * width2, :]
        n2 = fn2[...]
        low = fdy[...].astype(BF)
        act, slope = gelu_pair(nn(n2, up))
        act = act.astype(BF)
        fh[...] += nn(act, down)
        inner_grad = (nt(low, down) * slope).astype(BF)
        add_panels((8 + j) * per_block, tn(act, low))
        add_panels((4 + j) * per_block, tn(n2, inner_grad))
        fgrad[...] += nt(inner_grad, up)
        if j == blocks // 2 - 1:
            tick(new=5)

    for l in range(2):
        for w in range(2):
            out_ref[l, 0, w * half : (w + 1) * half] = fh[w * rows + l * half : w * rows + (l + 1) * half].astype(BF)

    hidden = win_s[...] + nn(joined(fo), f_out[...])
    z2, r2 = norm(hidden)
    grad = fgrad[...]
    acc_norm[1:2] += jnp.sum(grad * z2, 0, keepdims=True)
    acc_norm[3:4] += jnp.sum(grad, 0, keepdims=True)
    hidden_grad = fdy[...] + norm_back(grad, f_gain[1:2], z2, r2)
    fgrad[...] = hidden_grad
    low = hidden_grad.astype(BF)
    add_panels(3 * per_block, tn(joined(fo), low))
    att_grad = nt(low, f_out[...]).astype(BF)
    for w in range(2):
        for g in range(lane_groups):
            fo[w * lane_groups + g] = att_grad[w * rows : (w + 1) * rows, g * LANES : (g + 1) * LANES]

    @pl.loop(0, 2 * lane_groups, unroll=UNROLL)
    def _(i):
        queries = stack2(fq[i])
        grads = stack2(fo[i])
        prob_grads = nt(fv[i], grads)
        probs, terms = [], []
        for j, span in enumerate(spans):
            prob = fp[i, :, span]
            probs.append(prob.astype(BF))
            ds = score_back(prob, prob_grads[:, span]).astype(BF)
            terms.append(ds)
            if j < heads:
                ds_main[step * (2 * lane_groups * heads) + i * heads + j] = ds
            else:
                ds_tail[step * (2 * lane_groups) + i] = ds
        probs, terms = jnp.concatenate(probs, 1), jnp.concatenate(terms, 1)
        fdv[i] = nn(probs, grads).astype(BF)
        fdk[i] = (nn(terms, queries) * root).astype(BF)
        fdq[i] = (fold2(tn(terms, fk[i])) * root).astype(BF)

    z1, r1 = norm(win_s[...])
    n1 = (z1 * f_gain[0:1] + f_shift[0:1]).astype(BF)
    first = jnp.zeros((2 * rows, width2), F32)
    for t, src in enumerate((fdq, fdk, fdv)):
        part = joined(src)
        add_panels(t * per_block, tn(n1, part))
        first += nt(part, f_qkv[:, t * width2 : (t + 1) * width2])
    acc_norm[0:1] += jnp.sum(first * z1, 0, keepdims=True)
    acc_norm[2:3] += jnp.sum(first, 0, keepdims=True)
    fgrad[...] += norm_back(first, f_gain[0:1], z1, r1)

    tick(new=6)

    @pl.when(step == 2)
    def _():
        for owner, dest in ((side, own_f), (1 - side, give_f)):

            @pl.loop(0, panels // 2)
            def _(n):
                panel = acc[pl.ds(2 * (owner * (panels // 2) + n), 2)].reshape(width2, LANES)
                dest[pl.ds(pl.multiple_of(n * width2, 16), width2), :] = panel.astype(BF)

            norms = acc_norm[...]
            norms = jnp.concatenate(
                [norms[:, g * LANES : (g + 1) * LANES] for g in range(lane_groups)]
                + [jnp.zeros((EXTRA - 4 * lane_groups, LANES), F32)],
                0,
            )
            dest[halves : halves + EXTRA] = norms.astype(BF)
        own_f[halves + EXTRA :] = jnp.zeros((own_f.shape[0] - halves - EXTRA, LANES), BF)
        joining_half().start()

    packs = [own_e.at[step, l * ROWS1 : (l + 1) * ROWS1] for l in both]
    lift_grads = [
        jnp.concatenate([fgrad[w * rows + l * half : w * rows + (l + 1) * half] for w in both], 0).astype(BF)
        for l in both
    ]
    d_outs = [nt(lift_grads[l], w_lift[l][0]) for l in both]
    for l in both:
        put_panels(packs[l], 12 * width1, tn(res_s[l], lift_grads[l]))
    norm_grads = [[None] * 4 for _ in both]
    hidden_grads, att_grads, mixed, first_grads = [None] * 2, [None] * 2, [None] * 2, [None] * 2
    inner_grads = [(nn(d_outs[l].astype(BF), w_down[l][0]) * gp_s[l]).astype(BF) for l in both]
    for l in both:
        put_panels(packs[l], 15 * width1, tn(d_outs[l].astype(BF), act_s[l]))
        put_panels(packs[l], 6 * width1, tn(n2_s[l], inner_grads[l]))
    for l in both:
        grad = nt(inner_grads[l], w_up[l][0])
        z2, r2 = norm(h_s[l])
        norm_grads[l][1] = jnp.sum(grad * z2, 0, keepdims=True)
        norm_grads[l][3] = jnp.sum(grad, 0, keepdims=True)
        hidden_grads[l] = d_outs[l] + norm_back(grad, gains1[l][0, 1:2], z2, r2)
    for l in both:
        att_grads[l] = nt(hidden_grads[l].astype(BF), w_out[l][0]).astype(BF).astype(F32)
    out_grads = [tn(o_s[l].astype(BF), hidden_grads[l].astype(BF)) for l in both]
    grads = [stack1(att_grads[l][part]) for l, w, part in windows]
    terms = [
        score_back(p_s[l, w], nt(v_s[l, part].astype(BF), grads[n])).astype(BF)
        for n, (l, w, part) in enumerate(windows)
    ]
    dvs = [nn(p_s[l, w].astype(BF), grads[n]) for n, (l, w, part) in enumerate(windows)]
    dks = [nn(terms[n], stack1(q_s[l, part])) * root for n, (l, w, part) in enumerate(windows)]
    dqs = [fold1(tn(terms[n], k_s[l, part].astype(BF))) * root for n, (l, w, part) in enumerate(windows)]
    for l in both:
        mixed[l] = jnp.concatenate(
            [jnp.concatenate([dqs[n], dks[n], dvs[n]], 1) for n in (2 * l, 2 * l + 1)], 0
        ).astype(BF)
    for l in both:
        put_panels(packs[l], 0, jnp.concatenate([tn(n1_s[l], mixed[l]), out_grads[l]], 1))
    for l in both:
        first = nt(mixed[l], w_qkv[l][0])
        z1, r1 = norm(x_s[l, step].astype(F32))
        norm_grads[l][0] = jnp.sum(first * z1, 0, keepdims=True)
        norm_grads[l][2] = jnp.sum(first, 0, keepdims=True)
        norms = jnp.pad(jnp.concatenate(norm_grads[l], 0), ((0, 4), (0, 2 * LANES - width1)))
        norms = jnp.concatenate([norms[:4, :LANES], norms[:4, LANES:], jnp.zeros((8, LANES), F32)], 0)
        packs[l][21 * width1 : 21 * width1 + EXTRA] = norms.astype(BF)
        packs[l][21 * width1 + EXTRA :] = jnp.zeros((ROWS1 - 21 * width1 - EXTRA, LANES), BF)
        xg_s[l, step] = hidden_grads[l] + norm_back(first, gains1[l][0, 0:1], z1, r1)
    run(encoder(step), 0)
    for copy in tokens_grad(step):
        copy.start()

    @pl.when(step == 2)
    def _():
        joining_half().wait()
        add_rows(own_f, 0, halves + EXTRA, [(peer_f, 0)])
        run(joining(), 0)
        lay_terms(ds_main, ds_tail, acc)
        acc_t[...] = jnp.zeros_like(acc_t)
        quarters = [n * eights // 4 for n in range(5)]
        for n in range(4):
            add_terms(acc_t, all_pos, acc, quarters[n], quarters[n + 1])
            if n < 3:
                run(encoder(1), 7 + n)
            run(encoder(2), 1 + n)
            run(joining(), 1 + n)
        kinds = [kinds_ref[n // 2, n % 2] for n in range(2 * pairs)]
        picker = type_picker(kinds, heads_all, types)
        many = heads_all * types
        high = acc_t.shape[0] // all_terms
        for k in range(high):
            part = nn(picker, acc_t[k * all_terms : (k + 1) * all_terms].astype(BF)).astype(BF)
            for j in range(SPAN // LANES):
                n = k * (SPAN // LANES) + j
                at = n % high * many
                give_t[n // high, at : at + many] = part[:, j * LANES : (j + 1) * LANES]
        table_half().start()
        table_rows = high * many
        own_t[table_rows:] = jnp.zeros((own_t.shape[0] - table_rows, LANES), BF)
        for copy in [near(give_t.at[side], own_t.at[:table_rows], 0)]:
            copy.start()
            copy.wait()
        run(encoder(2), 5)
        run(joining(), 5)
        table_half().wait()
        add_rows(own_t, 0, table_rows, [(peer_t, 0)])
        run(table(), 0)
        for n in range(6, Part.STAGES):
            run(encoder(2), n)
            run(joining(), n)
            run(table(), n - 4)
        for n in range(6, Part.STAGES):
            run(table(), n)
        for q in range(pairs):
            for copy in tokens_grad(q):
                copy.wait()


def layer(kinds, tokens, enc, fus, table, pos_index, target, code):
    pairs, rows, width2 = target.shape[1:]
    width1 = tokens.shape[3]
    ff1 = enc[4].shape[2]
    keys = rows
    tails = rows - LANES
    half = rows // 2
    heads, types, count = table.shape
    high = -(-count // SPAN)
    groups = 2 * width2 // LANES
    per = LANES // HEAD
    lanes = per * (LANES + tails)
    panels = 12 * width2 // LANES
    halves = panels // 2 * width2 + EXTRA
    table_rows = high * heads * types
    total1, total2, total3 = (64 * sum(c) for c in (CHUNKS1, CHUNKS2, CHUNKS3))

    def by_row(array, level):
        return pl.BlockSpec((1,) + array.shape[1:], lambda q, level=level: (level * pairs + q, 0, 0))

    def whole(array):
        return pl.BlockSpec(array.shape, lambda q: (0,) * array.ndim, pipeline_mode=pl.Buffered(1))

    anywhere = pl.BlockSpec(memory_space=pl.ANY)
    table = table.reshape(heads * types, count)
    enc_args, enc_specs = [], []
    for array in enc:
        for level in range(2):
            enc_args.append(array)
            enc_specs.append(by_row(array, level))
    moving = pl.BlockSpec((2, 1, rows, width2), lambda q: (0, q, 0, 0))
    dma = pltpu.SemaphoreType.DMA
    vmem = pltpu.VMEM
    return pl.pallas_call(
        layer_kernel,
        grid=(pairs,),
        out_shape=(
            jax.ShapeDtypeStruct((2, pairs, rows, width2), BF),
            jax.ShapeDtypeStruct((1, 2 * pairs, rows, width1), F32),
            jax.ShapeDtypeStruct((2, pairs, total1, LANES), BF),
            jax.ShapeDtypeStruct((2, total2, LANES), BF),
            jax.ShapeDtypeStruct((2, total3, LANES), BF),
        ),
        in_specs=[pl.BlockSpec(memory_space=pltpu.SMEM), anywhere]
        + enc_specs
        + [whole(a) for a in fus]
        + [whole(table), whole(pos_index), moving, whole(code)],
        out_specs=(moving, anywhere, anywhere, anywhere, anywhere),
        scratch_shapes=[
            vmem((2, pairs, rows, width1), BF),
            vmem((2, pairs, rows, width1), F32),
            vmem((2, rows, width1), BF),
            vmem((2, rows, width1), F32),
            vmem((2, rows, width1), F32),
            vmem((2, rows, width1), F32),
            vmem((2, 2, half, HEADS1 * half), F32),
            vmem((2, rows, width1), F32),
            vmem((2, rows, width1), BF),
            vmem((2, rows, width1), F32),
            vmem((2, rows, ff1), BF),
            vmem((2, rows, ff1), F32),
            vmem((2, rows, width1), BF),
            vmem((2 * rows, width2), F32),
            vmem((groups, rows, LANES), BF),
            vmem((groups, rows, LANES), BF),
            vmem((groups, rows, LANES), BF),
            vmem((groups, rows, lanes), F32),
            vmem((groups, rows, LANES), BF),
            vmem((groups, rows, LANES), BF),
            vmem((groups, rows, LANES), BF),
            vmem((groups, rows, LANES), BF),
            vmem((2 * rows, width2), F32),
            vmem((2 * rows, width2), BF),
            vmem((2 * rows, width2), F32),
            vmem((2 * rows, width2), F32),
            vmem((pairs, high * 2 * heads, SPAN), BF),
            vmem((keys + 2 * tails, LANES), jnp.int32),
            vmem((2 * heads, keys + 2 * tails, LANES), F32),
            vmem((groups, keys, per * tails), F32),
            vmem((pairs * 2 * heads, keys, LANES), BF),
            vmem((pairs * groups, keys, per * tails), BF),
            vmem((high * pairs * 2 * heads, SPAN), F32),
            vmem((2 * panels, width2 // 2, LANES), F32),
            vmem((4, width2), F32),
            vmem((pairs, total1, LANES), BF),
            vmem((total2, LANES), BF),
            vmem((halves, LANES), BF),
            vmem((halves, LANES), BF),
            vmem((total3, LANES), BF),
            vmem((2, table_rows, LANES), BF),
            vmem((table_rows, LANES), BF),
        ]
        + [vmem((pairs, 63 * chunk, LANES), BF) for chunk in CHUNKS1]
        + [vmem((63 * chunk, LANES), BF) for chunk in CHUNKS2 + CHUNKS3]
        + [dma((pairs, 3, MESSAGES)), dma((pairs, 3, MESSAGES)), dma((pairs, 3))]
        + [dma((3, MESSAGES)), dma((3, MESSAGES)), dma((3,))] * 2
        + [dma((3 + pairs,)), dma((3 + pairs,)), dma((1 + pairs,))],
        compiler_params=pltpu.CompilerParams(
            vmem_limit_bytes=VMEM_LIMIT, collective_id=0, has_side_effects=True
        ),
        name="layer",
    )(kinds, tokens, *enc_args, *fus, table, pos_index, target, code)


def select_kernel(groups_ref, *refs):
    count = (len(refs) - 2) // 3
    arrays, picked, held = (refs[n * count : (n + 1) * count] for n in range(3))
    into, out_of = refs[-2:]
    rows = picked[0].shape[0]
    side = lax.axis_index("lvl")

    def load(n, row):
        level, pair = row // (rows // 2), row % (rows // 2)
        group = groups_ref[level * rows + side * (rows // 2) + pair]
        return pltpu.make_async_copy(arrays[n].at[group], held[n].at[row], into.at[n, row])

    def store(n, row):
        return pltpu.make_async_copy(held[n].at[row], picked[n].at[row], out_of.at[n, row])

    every = [(n, row) for row in range(rows) for n in range(count)]
    for at in every:
        load(*at).start()
    for at in every:
        load(*at).wait()
        store(*at).start()
    for at in every:
        store(*at).wait()


def select_rows(level_group, arrays):
    count = level_group.shape[0] // 2
    anywhere = pl.BlockSpec(memory_space=pl.ANY)
    return pl.pallas_call(
        select_kernel,
        out_shape=tuple(jax.ShapeDtypeStruct((count,) + a.shape[1:], a.dtype) for a in arrays),
        in_specs=[pl.BlockSpec(memory_space=pltpu.SMEM)] + [anywhere] * len(arrays),
        out_specs=(anywhere,) * len(arrays),
        scratch_shapes=[pltpu.VMEM((count,) + a.shape[1:], a.dtype) for a in arrays]
        + [pltpu.SemaphoreType.DMA((len(arrays), count))] * 2,
        compiler_params=pltpu.CompilerParams(vmem_limit_bytes=VMEM_LIMIT),
        name="select_rows",
    )(level_group, *arrays)


def unpack_kernel(
    groups_ref, enc_ref, fus_ref, fus_extra, table_in,
    gain_ref, shift_ref, qkv_ref, out_ref, up_ref, down_ref, lift_ref,
    fg_ref, fs_ref, fq_ref, fo_ref, fu_ref, fd_ref, table_ref,
):
    width = qkv_ref.shape[1]

    def panel(n):
        return enc_ref[0, n * width : (n + 1) * width].astype(F32)

    half = LANES // 2
    for n in range(4):
        qkv_ref[0, :, n * LANES : (n + 1) * LANES] = panel(n)
    mixed, last = panel(4), panel(5)
    qkv_ref[0, :, 4 * LANES :] = mixed[:, :half]
    out_ref[0] = jnp.concatenate([mixed[:, half:], last], 1)
    for n in range(6):
        up_ref[0, :, n * LANES : (n + 1) * LANES] = panel(6 + n)
        down_ref[0, :, n * LANES : (n + 1) * LANES] = panel(15 + n)
    for n in range(3):
        lift_ref[0, :, n * LANES : (n + 1) * LANES] = panel(12 + n)
    norms = enc_ref[0, 21 * width : 21 * width + EXTRA].astype(F32)
    norms = jnp.concatenate([norms[0:4], norms[4:8]], 1)[:, :width]
    gain_ref[0] = norms[0:2]
    shift_ref[0] = norms[2:4]
    i = pl.program_id(0)
    size = fo_ref.shape[0]

    def joining(dest):
        for n in range(size // LANES):
            dest[:, n * LANES : (n + 1) * LANES] = fus_ref[0, n * size : (n + 1) * size].astype(F32)

    @pl.when(i < 3)
    def _():
        joining(fq_ref)

    @pl.when(i == 3)
    def _():
        joining(fo_ref)

    @pl.when((i >= 4) & (i < 8))
    def _():
        joining(fu_ref)

    @pl.when(i >= 8)
    def _():
        joining(fd_ref)

    heads, types, count = table_ref.shape

    @pl.when(i == 0)
    def _():
        extra = fus_extra[0].astype(F32)
        extra = jnp.concatenate([extra[4 * n : 4 * n + 4] for n in range(size // LANES)], 1)
        fg_ref[...] = extra[0:2]
        fs_ref[...] = extra[2:4]
        each = heads * types
        per = table_in.shape[1] // each
        for n in range(2 * per):
            wide = min(LANES, count - n * LANES)
            if wide > 0:
                at = n % per * each
                block = table_in[n // per, at : at + each].astype(F32).reshape(heads, types, LANES)
                table_ref[:, :, n * LANES : n * LANES + wide] = block[:, :, :wide]


def unpack(level_group, enc, fus, table, width1, width2, table_shape):
    groups = enc.shape[0]
    pairs = groups // 4

    def group_of(i, s):
        return s[i % 2 * (groups // 2) + i // (2 * pairs) * pairs + i // 2 % pairs]

    heads, types, count = table_shape
    table_rows = -(-count // SPAN) * heads * types
    panels = width2 * width2 // LANES
    sizes1 = [(2, width1), (2, width1), (width1, 3 * width1), (width1, width1), (width1, 4 * width1), (width1, 4 * width1), (width1, 2 * width1)]
    sizes2 = [(2, width2), (2, width2), (width2, 3 * width2), (width2, width2), (width2, 4 * width2), (4 * width2, width2)]
    square = (width2, width2)
    return pl.pallas_call(
        unpack_kernel,
        out_shape=tuple(jax.ShapeDtypeStruct((groups,) + s, F32) for s in sizes1)
        + tuple(jax.ShapeDtypeStruct(s, F32) for s in sizes2)
        + (jax.ShapeDtypeStruct(table_shape, F32),),
        grid_spec=pltpu.PrefetchScalarGridSpec(
            num_scalar_prefetch=1,
            grid=(groups,),
            in_specs=[
                pl.BlockSpec((1,) + enc.shape[1:], lambda i, s: (i, 0, 0)),
                pl.BlockSpec((1, panels, LANES), lambda i, s: (i // 6, i % 6, 0)),
                pl.BlockSpec((1, EXTRA, LANES), lambda i, s: (0, 6 * panels // EXTRA, 0)),
                pl.BlockSpec((2, table_rows, LANES), lambda i, s: (0, 0, 0)),
            ],
            out_specs=tuple(pl.BlockSpec((1,) + s, lambda i, s: (group_of(i, s), 0, 0)) for s in sizes1)
            + (
                pl.BlockSpec((2, width2), lambda i, s: (0, 0)),
                pl.BlockSpec((2, width2), lambda i, s: (0, 0)),
                pl.BlockSpec(square, lambda i, s: (0, jnp.minimum(i, 2))),
                pl.BlockSpec(square, lambda i, s: (0, 0)),
                pl.BlockSpec(square, lambda i, s: (0, jnp.clip(i - 4, 0, 3))),
                pl.BlockSpec(square, lambda i, s: (jnp.clip(i - 8, 0, 3), 0)),
                pl.BlockSpec(table_shape, lambda i, s: (0, 0, 0)),
            ),
        ),
        compiler_params=pltpu.CompilerParams(vmem_limit_bytes=VMEM_LIMIT),
        name="unpack",
    )(level_group, enc, fus, fus, table)


def shards(
    tokens_in,
    enc_gains,
    enc_shifts,
    enc_qkv,
    enc_out,
    enc_up,
    enc_down,
    enc_lift,
    fus_gains,
    fus_shifts,
    fus_qkv,
    fus_out,
    fus_up,
    fus_down,
    fus_table,
    target,
    loss_code,
    level_group,
    window_type,
    pos_index,
):
    enc = select_rows(
        level_group, (enc_gains, enc_shifts, enc_qkv, enc_out, enc_up, jnp.swapaxes(enc_down, 1, 2), enc_lift)
    )
    output, x_grad, enc_sums, fus_sums, table_sums = layer(
        window_type,
        tokens_in,
        enc,
        (fus_gains, fus_shifts, fus_qkv, fus_out, fus_up, fus_down),
        fus_table,
        pos_index,
        target,
        loss_code,
    )
    grads = unpack(
        level_group,
        enc_sums.reshape(level_group.shape[0], ROWS1, LANES),
        fus_sums,
        table_sums,
        enc_out.shape[1],
        fus_out.shape[0],
        fus_table.shape,
    )
    return (output, x_grad, *grads[:5], jnp.swapaxes(grads[5], 1, 2), *grads[6:])


def solution(mesh):
    copied = P()
    in_specs = (
        (P("lvl", None, "win", None),)
        + (copied,) * 14
        + (P(None, "lvl", "win", None), P(None, "lvl", "win"), copied, P("lvl", "win"), copied)
    )
    out_specs = (P(None, "lvl", "win", None), P("lvl", None, "win", None)) + (copied,) * 14
    return jax.shard_map(shards, mesh=mesh, in_specs=in_specs, out_specs=out_specs, check_vma=False)
```

```python
import functools

import jax
import jax.numpy as jnp
from jax import lax
from jax.experimental import pallas as pl
from jax.experimental.pallas import tpu as pltpu
from jax.sharding import PartitionSpec as P

HEADS1 = 6
HEADS2 = 12
HEAD = 32
EPS = 1e-05
LANES = 128
SPAN = 256
PER = 4
UNROLL = 6
ROWS1 = 4096
CHUNKS1 = (48, 48, 32)
CHUNKS2 = (48, 32, 32)
CHUNKS3 = (16, 16, 16)
EXTRA = 16
VMEM_LIMIT = 60 * 1024 * 1024

BF = jnp.bfloat16
F32 = jnp.float32


def nn(a, b):
    return lax.dot_general(a, b, (((1,), (0,)), ((), ())), preferred_element_type=F32)


def nt(a, b):
    return lax.dot_general(a, b, (((1,), (1,)), ((), ())), preferred_element_type=F32)


def tn(a, b):
    return lax.dot_general(a, b, (((0,), (0,)), ((), ())), preferred_element_type=F32)


RING = 4
STRIDES = (16, 4, 1)
ORDERS = ((0, 1, 2), (1, 2, 0), (2, 0, 1))
MESH = pl.DeviceIdType.MESH
MESSAGES = 22


def coordinate(axis):
    return lax.rem(lax.axis_index("win") // STRIDES[axis], RING)


def along(axis, hops):
    place = lax.axis_index("win")
    mine = coordinate(axis)
    other = lax.rem(mine + hops, RING)
    return (lax.axis_index("lvl"), place + (other - mine) * STRIDES[axis])


def partner():
    return (1 - lax.axis_index("lvl"), lax.axis_index("win"))


def add_rows(dest, at, rows, others):
    step = max(s for s in (128, 112, 96, 64, 48, 32, 16) if rows % s == 0)

    @pl.loop(0, rows // step)
    def _(i):
        here = pl.ds(pl.multiple_of(at + i * step, 16), step)
        total = dest[here, :].astype(F32)
        for ref, start in others:
            total += ref[pl.ds(pl.multiple_of(start + i * step, 16), step), :].astype(F32)
        dest[here, :] = total.astype(BF)


def rows_of(ref, at, size):
    return ref.at[pl.ds(pl.multiple_of(at, 16), size)]


class Place:
    def __init__(self):
        self.here = [coordinate(axis) for axis in range(3)]
        self.chips = {(axis, hops): along(axis, hops) for axis in range(3) for hops in (1, 2, 3)}
        self.partner = partner()


class Part:
    def __init__(self, place, own, out, box, send, recv, keep, base, chunk, order, ring):
        self.own, self.out, self.box, self.send, self.recv, self.keep = own, out, box, send, recv, keep
        self.place, self.axes, self.ring = place, order, ring
        self.here = [place.here[a] for a in order]
        self.big, self.mid, self.chunk = 16 * chunk, 4 * chunk, chunk
        self.base = base
        self.first = base + self.here[0] * self.big
        self.second = self.first + self.here[1] * self.mid
        self.third = self.second + self.here[2] * chunk

    def top(self, hops):
        return self.base + jnp.bitwise_and(self.here[0] + hops, RING - 1) * self.big

    def message(self, n):
        big, mid, chunk = self.big, self.mid, self.chunk
        half = big // 2
        up, down = (0, 1), (0, RING - 1)
        own, out, box = self.own, self.out, self.box
        after = 3 * big
        if n < 6 and not self.ring:
            hops = (1, 3, 2)[n]
            src, dst, to = rows_of(own, self.top(hops), big), rows_of(box, n * big, big), (0, hops)
        elif n == 0:
            src, dst, to = rows_of(own, self.top(2), half), rows_of(box, 0, half), up
        elif n == 1:
            src, dst, to = rows_of(own, self.top(2) + half, half), rows_of(box, half, half), down
        elif n == 2:
            src, dst, to = rows_of(own, self.top(1) + half, half), rows_of(box, big + half, half), up
        elif n == 3:
            src, dst, to = rows_of(own, self.top(3), half), rows_of(box, 2 * big, half), down
        elif n == 4:
            src, dst, to = rows_of(own, self.top(1), half), rows_of(box, big, half), up
        elif n == 5:
            src, dst, to = rows_of(own, self.top(3) + half, half), rows_of(box, 2 * big + half, half), down
        elif n < 9:
            hops = (1, 3, 2)[n - 6]
            at = self.first + jnp.bitwise_and(self.here[1] + hops, RING - 1) * mid
            src, dst, to = rows_of(own, at, mid), rows_of(box, after + (n - 6) * mid, mid), (1, hops)
        elif n < 12:
            hops = (1, 3, 2)[n - 9]
            at = self.second + jnp.bitwise_and(self.here[2] + hops, RING - 1) * chunk
            src, to = rows_of(own, at, chunk), (2, hops)
            dst = rows_of(box, after + 3 * mid + (n - 9) * chunk, chunk)
        elif n < 15:
            src, dst = rows_of(own, self.third, chunk), rows_of(out, self.third, chunk)
            to = (2, (1, 3, 2)[n - 12])
        elif n < 18:
            src = dst = rows_of(out, self.second, mid)
            to = (1, (1, 3, 2)[n - 15])
        elif not self.ring:
            src = dst = rows_of(out, self.first, big)
            to = (0, (1, 3, 2)[n - 18])
        elif n < 20:
            src = dst = rows_of(out, self.first, big)
            to = (up, down)[n - 18]
        elif n == 20:
            src = dst = rows_of(out, self.top(3), half)
            to = up
        else:
            src = dst = rows_of(out, self.top(1) + half, half)
            to = down
        device = self.place.chips[self.axes[to[0]], to[1]]
        return pltpu.make_async_remote_copy(
            src, dst, self.send.at[n], self.recv.at[n], device_id=device, device_id_type=MESH
        )

    def start(self, *numbers):
        for n in numbers:
            self.message(n).start()

    def wait(self, *numbers):
        for n in numbers:
            self.message(n).wait()

    def kept(self):
        return pltpu.make_async_copy(
            rows_of(self.own, self.third, self.chunk), rows_of(self.out, self.third, self.chunk), self.keep
        )

    def stage(self, k):
        big, mid, chunk, own, box = self.big, self.mid, self.chunk, self.own, self.box
        half, after = big // 2, 3 * big
        if k == 0:
            self.start(*((0, 1, 2, 3) if self.ring else (2, 0, 1)))
        elif k == 1 and self.ring:
            self.wait(0)
            add_rows(own, self.top(1), half, [(box, 0)])
            self.start(4)
            self.wait(1)
            add_rows(own, self.top(3) + half, half, [(box, half)])
            self.start(5)
        elif k == 2:
            if self.ring:
                self.wait(2, 3, 4, 5)
            else:
                self.wait(0, 1, 2)
            add_rows(own, self.first, big, [(box, n * big) for n in ((1, 2) if self.ring else (0, 1, 2))])
            self.start(6, 7, 8)
        elif k == 3:
            self.wait(6, 7, 8)
            add_rows(own, self.second, mid, [(box, after + n * mid) for n in range(3)])
            self.start(9, 10, 11)
        elif k == 4:
            self.wait(9, 10, 11)
            add_rows(own, self.third, chunk, [(box, after + 3 * mid + n * chunk) for n in range(3)])
            self.kept().start()
            self.start(12, 13, 14)
        elif k == 5:
            self.kept().wait()
            self.wait(12, 13, 14)
            self.start(15, 16, 17)
        elif k == 6:
            self.wait(15, 16, 17)
            self.start(*((18, 19) if self.ring else (20, 18, 19)))
        elif k == 7 and self.ring:
            self.wait(18)
            self.start(20)
            self.wait(19)
            self.start(21)
        elif k == 8:
            self.wait(*((20, 21) if self.ring else (18, 19, 20)))


def parts_of(place, chunks, own, out, boxes, sems, ring):
    parts, base = [], 0
    for n, chunk in enumerate(chunks):
        send, recv, keep = (sem.at[n] for sem in sems)
        parts.append(Part(place, own, out, boxes[n], send, recv, keep, base, chunk, ORDERS[n], ring))
        base += 64 * chunk
    return parts


def run(parts, k):
    for part in parts:
        part.stage(k)


def type_picker(kinds, heads, types):
    shape = (heads * types, len(kinds) * heads)
    row = lax.broadcasted_iota(jnp.int32, shape, 0)
    column = lax.broadcasted_iota(jnp.int32, shape, 1)
    kind = jnp.full(shape, kinds[-1], jnp.int32)
    for n in reversed(range(len(kinds) - 1)):
        kind = jnp.where(column < (n + 1) * heads, kinds[n], kind)
    same_head = (row // types) == (column % heads)
    return (same_head & ((row % types) == kind)).astype(F32).astype(BF)


def lay_positions(pos_ref, all_pos):
    keys = pos_ref.shape[0]
    tails = keys - LANES
    all_pos[:keys] = pos_ref[...].astype(F32).T[:, :LANES].astype(jnp.int32)
    all_pos[keys : keys + tails] = pos_ref[LANES:, :LANES]
    all_pos[keys + tails :] = jnp.full((tails, LANES), -1, jnp.int32)
    all_pos[keys + tails :, : keys - LANES] = pos_ref[LANES:, LANES:]


def one_hot_of(pos):
    low = jnp.bitwise_and(pos, SPAN - 1)
    return (lax.broadcasted_iota(jnp.int32, (SPAN, pos.shape[1]), 0) == low).astype(F32).astype(BF)


def spread_table(picker, table_ref, t2):
    rows, count = picker.shape[1], table_ref.shape[1]
    for k in range(t2.shape[0] // rows):
        width = min(SPAN, count - k * SPAN)
        part = table_ref[:, k * SPAN : k * SPAN + width].astype(BF)
        t2[k * rows : (k + 1) * rows, :width] = tn(picker, part).astype(BF)
        if width < SPAN:
            t2[k * rows : (k + 1) * rows, width:] = jnp.zeros((rows, SPAN - width), BF)


def look_up(t2, all_pos, dest, first, last):
    rows = dest.shape[0]
    high = t2.shape[0] // rows

    @pl.loop(first, last)
    def _(i):
        at = pl.multiple_of(i * 8, 8)
        eight = all_pos[pl.ds(at, 8), :]
        for s in range(0, 8, PER):
            pos = jnp.concatenate([eight[s + j : s + j + 1] for j in range(PER)], 1)
            top = jnp.right_shift(pos, 8)
            spread = nn(t2[...], one_hot_of(pos))
            picked = jnp.zeros((rows, PER * LANES), F32)
            for k in range(high):
                picked = jnp.where(top == k, spread[k * rows : (k + 1) * rows], picked)
            for j in range(PER):
                dest[:, pl.ds(at + s + j, 1), :] = picked[:, j * LANES : (j + 1) * LANES].reshape(rows, 1, LANES)


def turn_tails(bias, bias_tail, keys):
    tails = keys - LANES
    per = bias_tail.shape[2] // tails
    for i in range(bias_tail.shape[0]):
        lines = bias[i * per : (i + 1) * per, keys : keys + tails].reshape(per * tails, LANES)
        bias_tail[i, :LANES] = lines.T
        lines = bias[i * per : (i + 1) * per, keys + tails : keys + 2 * tails].reshape(per * tails, LANES)
        bias_tail[i, LANES:] = lines.T[: keys - LANES]


def lay_terms(ds_main, ds_tail, lines):
    rows, keys = ds_main.shape[:2]
    tails = keys - LANES
    per = ds_tail.shape[2] // tails

    @pl.loop(0, ds_tail.shape[0])
    def _(i):
        at = pl.ds(i * per, per)
        lines[at, :keys] = ds_main[at].astype(F32)
        block = ds_tail[i].astype(F32)
        lines[at, keys : keys + tails] = block[:LANES].T.reshape(per, tails, LANES)
        lines[at, keys + tails : keys + 2 * tails] = jnp.zeros((per, tails, LANES), F32)
        lines[at, keys + tails : keys + 2 * tails, : keys - LANES] = block[LANES:].T.reshape(per, tails, keys - LANES)


def add_terms(acc, all_pos, lines, first, last):
    rows = lines.shape[0]
    high = acc.shape[0] // rows

    @pl.loop(first, last)
    def _(i):
        at = pl.multiple_of(i * 8, 8)
        eight = all_pos[pl.ds(at, 8), :]
        total = None
        for s in range(0, 8, PER):
            pos = jnp.concatenate([eight[s + j : s + j + 1] for j in range(PER)], 1)
            terms = jnp.concatenate([lines[:, pl.ds(at + s + j, 1), :].reshape(rows, LANES) for j in range(PER)], 1)
            top = jnp.right_shift(pos, 8)
            parts = jnp.concatenate([jnp.where(top == k, terms, 0.0) for k in range(high)], 0)
            term = nt(parts.astype(BF), one_hot_of(pos))
            total = term if total is None else total + term
        acc[...] += total


def norm(values):
    centred = values - jnp.mean(values, -1, keepdims=True)
    spread = jnp.mean(centred * centred, -1, keepdims=True)
    scale = lax.rsqrt(spread + EPS)
    return centred * scale, scale


def norm_back(grad, gain, unit, scale):
    scaled = grad * gain
    first = jnp.mean(scaled, -1, keepdims=True)
    second = jnp.mean(scaled * unit, -1, keepdims=True)
    return (scaled - first - unit * second) * scale


def gelu_pair(v):
    half = jnp.exp(-0.5 * v * v)
    t = 1.0 / (1.0 + 0.23164189 * jnp.abs(v))
    series = t * (0.127414796 + t * (-0.142248368 + t * (0.7107068705 + t * (-0.7265760135 + t * 0.5307027145))))
    tail = series * half
    phi = jnp.where(v >= 0.0, 1.0 - tail, tail)
    return v * phi, phi + v * half * 0.3989422804014327


def head_masks(width):
    lane = lax.broadcasted_iota(jnp.int32, (1, width), 1)
    return [(lane // HEAD) == h for h in range(width // HEAD)]


def keep(mask, values):
    return jnp.where(mask, values, 0.0)


def put_panels(ref, at, values):
    rows = values.shape[0]
    for j in range(values.shape[1] // LANES):
        ref[at + j * rows : at + (j + 1) * rows] = values[:, j * LANES : (j + 1) * LANES].astype(ref.dtype)


def softmax_rows(scores):
    top = jnp.max(scores, 0, keepdims=True)
    e = jnp.exp(scores - top)
    return e * (1.0 / jnp.sum(e, 0, keepdims=True))


def score_back(prob, grad):
    return prob * (grad - jnp.sum(grad * prob, 0, keepdims=True))


def layer_kernel(
    kinds_ref, tokens_ref,
    e_gain0, e_gain1, e_shift0, e_shift1,
    e_qkv0, e_qkv1, e_out0, e_out1, e_up0, e_up1, e_down0, e_down1, e_lift0, e_lift1,
    f_gain, f_shift, f_qkv, f_out, f_up, f_down,
    table_ref, pos_ref, target_ref, code_ref,
    out_ref, xg_out, e_all, f_all, t_all,
    x_s, xg_s, n1_s, q_s, k_s, v_s, p_s, o_s, n2_s, h_s, act_s, gp_s, res_s,
    win_s, fq, fk, fv, fp, fo, fdq, fdk, fdv, fh, fn2, fdy, fgrad,
    t2, all_pos, bias_main, bias_tail, ds_main, ds_tail, acc_t,
    acc, acc_norm, own_e, own_f, give_f, peer_f, own_t, give_t, peer_t,
    be0, be1, be2, bf0, bf1, bf2, bt0, bt1, bt2,
    se, re, ke, sf, rf, kf, st, rt, kt, misc_send, misc_recv, misc_near,
):
    boxes_e, boxes_f, boxes_t = (be0, be1, be2), (bf0, bf1, bf2), (bt0, bt1, bt2)
    sems_e, sems_f, sems_t = (se, re, ke), (sf, rf, kf), (st, rt, kt)
    step = pl.program_id(0)
    side = lax.axis_index("lvl")
    rows = x_s.shape[2]
    width1 = x_s.shape[3]
    width2 = f_qkv.shape[0]
    half = rows // 2
    keys = rows
    root = HEAD ** (-0.5)
    masks1 = head_masks(width1)
    masks2 = head_masks(LANES)
    picks2 = [m.astype(F32).astype(BF) for m in masks2]
    gains1, shifts1 = (e_gain0, e_gain1), (e_shift0, e_shift1)
    w_qkv, w_out, w_up = (e_qkv0, e_qkv1), (e_out0, e_out1), (e_up0, e_up1)
    w_down, w_lift = (e_down0, e_down1), (e_lift0, e_lift1)

    pairs = x_s.shape[1]
    heads_all = width2 // HEAD
    types = table_ref.shape[0] // heads_all
    all_terms = 2 * pairs * heads_all
    panels = 12 * width2 // LANES
    halves = panels // 2 * width2

    place = Place()

    def encoder(q, ring=False):
        return parts_of(
            place, CHUNKS1, own_e.at[q], e_all.at[side, q], [b.at[q] for b in boxes_e], [s.at[q] for s in sems_e], ring
        )

    def joining():
        return parts_of(place, CHUNKS2, own_f, f_all.at[side], boxes_f, sems_f, True)

    def table():
        return parts_of(place, CHUNKS3, own_t, t_all.at[side], boxes_t, sems_t, False)

    def hand_over(ref, n):
        return remote(ref.at[side], ref.at[side], 3 + pairs + n)

    def hand_encoder(q):
        return remote(e_all.at[side, q], e_all.at[side, q], 5 + pairs + q)

    def tick(new=None, old=None):
        if new is not None:

            @pl.when(step >= 1)
            def _():
                run(encoder(step - 1), new)

        if old is not None:

            @pl.when(step == 2)
            def _():
                if old < 9:
                    run(encoder(0), old)
                if old == 8:
                    hand_encoder(0).start()

    def remote(src, dst, n):
        return pltpu.make_async_remote_copy(
            src, dst, misc_send.at[n], misc_recv.at[n], device_id=place.partner, device_id_type=MESH
        )

    def near(src, dst, n):
        return pltpu.make_async_copy(src, dst, misc_near.at[n])

    def tokens():
        given = remote(tokens_ref.at[0, pl.ds((1 - side) * pairs, pairs)], x_s.at[side], 0)
        taken = near(tokens_ref.at[0, pl.ds(side * pairs, pairs)], x_s.at[side], 0)
        return given, taken

    def tokens_grad(q):
        given = remote(xg_s.at[1 - side, q], xg_out.at[0, side * pairs + q], 1 + q)
        taken = near(xg_s.at[side, q], xg_out.at[0, side * pairs + q], 1 + q)
        return given, taken

    def joining_half():
        return remote(give_f, peer_f, 1 + pairs)

    def table_half():
        return remote(give_t.at[1 - side], peer_t, 2 + pairs)

    @pl.when(step == 0)
    def _():
        barrier = pltpu.get_barrier_semaphore()
        friends = list(place.chips.values()) + [place.partner]
        for device in friends:
            pl.semaphore_signal(barrier, inc=1, device_id=device, device_id_type=MESH)
        pl.semaphore_wait(barrier, len(friends))
        for copy in tokens():
            copy.start()
        lay_positions(pos_ref, all_pos)
        for q in range(pairs):
            picker = type_picker([kinds_ref[w, q] for w in range(2)], heads_all, types)
            spread_table(picker, table_ref, t2.at[q])
        acc[...] = jnp.zeros_like(acc)
        acc_norm[...] = jnp.zeros_like(acc_norm)

    eights = (keys + 2 * (keys - LANES)) // 8
    look_up(t2.at[step], all_pos, bias_main, 0, eights)
    turn_tails(bias_main, bias_tail, keys)

    @pl.when(step == 0)
    def _():
        for copy in tokens():
            copy.wait()

    def stack1(values):
        return jnp.concatenate([keep(m, values) for m in masks1], 0).astype(BF)

    def fold1(stacked):
        total = keep(masks1[0], stacked[:half])
        for h in range(1, HEADS1):
            total += keep(masks1[h], stacked[h * half : (h + 1) * half])
        return total

    both = range(2)
    windows = [(l, w, slice(w * half, (w + 1) * half)) for l in both for w in both]
    xs = [x_s[l, step].astype(F32) for l in both]
    for l in both:
        z1, _ = norm(xs[l])
        n1_s[l] = (z1 * gains1[l][0, 0:1] + shifts1[l][0, 0:1]).astype(BF)
    for l in both:
        qkv = nn(n1_s[l], w_qkv[l][0])
        q_s[l] = qkv[:, :width1].astype(BF).astype(F32)
        k_s[l] = qkv[:, width1 : 2 * width1].astype(BF).astype(F32)
        v_s[l] = qkv[:, 2 * width1 :].astype(BF).astype(F32)
    for l, w, part in windows:
        p_s[l, w] = softmax_rows(nt(k_s[l, part].astype(BF), stack1(q_s[l, part])) * root)
    for l, w, part in windows:
        o_s[l, part] = fold1(tn(p_s[l, w].astype(BF), v_s[l, part].astype(BF)))
    for l in both:
        h = x_s[l, step].astype(F32) + nn(o_s[l].astype(BF), w_out[l][0])
        h_s[l] = h
        z2, _ = norm(h)
        n2_s[l] = (z2 * gains1[l][0, 1:2] + shifts1[l][0, 1:2]).astype(BF)
    for l in both:
        act, slope = gelu_pair(nn(n2_s[l], w_up[l][0]))
        act_s[l] = act.astype(BF)
        gp_s[l] = slope
    for l in both:
        res_s[l] = (h_s[l] + nt(act_s[l], w_down[l][0])).astype(BF)
    for l in both:
        lifted = nn(res_s[l], w_lift[l][0]).astype(BF).astype(F32)
        for w in range(2):
            win_s[w * rows + l * half : w * rows + (l + 1) * half] = lifted[w * half : (w + 1) * half]
    tick(new=2, old=8)

    eye = lax.broadcasted_iota(jnp.int32, (rows, rows), 0) == lax.broadcasted_iota(jnp.int32, (rows, rows), 1)
    for l in range(2):
        codes = code_ref[:, l].astype(F32)
        chosen = lax.broadcasted_iota(jnp.int32, codes.shape, 0) == step
        weight = 0.5 * jnp.exp(0.35 * jnp.sum(jnp.where(chosen, codes, 0.0), 0, keepdims=True))
        column = jnp.sum(jnp.where(eye, weight, 0.0), 1, keepdims=True)
        direction = column * target_ref[l, 0].astype(F32)
        for w in range(2):
            fdy[w * rows + l * half : w * rows + (l + 1) * half] = direction[w * half : (w + 1) * half]

    lane_groups = width2 // LANES
    z1, _ = norm(win_s[...])
    fn1 = (z1 * f_gain[0:1] + f_shift[0:1]).astype(BF)
    for t, dest in enumerate((fq, fk, fv)):
        part = nn(fn1, f_qkv[:, t * width2 : (t + 1) * width2]).astype(BF)
        for w in range(2):
            for g in range(lane_groups):
                dest[w * lane_groups + g] = part[w * rows : (w + 1) * rows, g * LANES : (g + 1) * LANES]
    tails = rows - LANES

    heads = LANES // HEAD
    lanes = heads * LANES + heads * tails
    spans = [slice(j * LANES, min((j + 1) * LANES, lanes)) for j in range(heads + 1)]

    def stack2(values):
        main, tail = values[:LANES], values[LANES:]
        return jnp.concatenate([main * m for m in picks2] + [tail * m for m in picks2], 0)

    def fold2(stacked):
        main = keep(masks2[0], stacked[:LANES])
        tail = keep(masks2[0], stacked[heads * LANES : heads * LANES + tails])
        for h in range(1, heads):
            main += keep(masks2[h], stacked[h * LANES : (h + 1) * LANES])
            tail += keep(masks2[h], stacked[heads * LANES + h * tails : heads * LANES + (h + 1) * tails])
        return jnp.concatenate([main, tail], 0)

    @pl.loop(0, 2 * lane_groups, unroll=UNROLL)
    def _(i):
        scores = nt(fk[i], stack2(fq[i]))
        probs = []
        for j, span in enumerate(spans):
            bias = bias_main[i * heads + j, :keys] if j < heads else bias_tail[i]
            prob = softmax_rows(scores[:, span] * root + bias)
            fp[i, :, span] = prob
            probs.append(prob.astype(BF))
        fo[i] = fold2(tn(jnp.concatenate(probs, 1), fv[i])).astype(BF)

    tick(new=3)

    def joined(ref):
        return jnp.concatenate(
            [jnp.concatenate([ref[w * lane_groups + g] for g in range(lane_groups)], 1) for w in range(2)], 0
        )

    hidden = win_s[...] + nn(joined(fo), f_out[...])
    fh[...] = hidden
    z2, _ = norm(hidden)
    fn2[...] = (z2 * f_gain[1:2] + f_shift[1:2]).astype(BF)

    def add_panels(n, values):
        for j in range(values.shape[1] // LANES):
            panel = values[:, j * LANES : (j + 1) * LANES]
            acc[2 * (n + j) : 2 * (n + j) + 2] += panel.reshape(2, width2 // 2, LANES)

    blocks = f_up.shape[1] // width2
    fgrad[...] = jnp.zeros_like(fgrad)

    per_block = width2 // LANES
    for j in range(blocks):
        up = f_up[:, j * width2 : (j + 1) * width2]
        down = f_down[j * width2 : (j + 1) * width2, :]
        n2 = fn2[...]
        low = fdy[...].astype(BF)
        act, slope = gelu_pair(nn(n2, up))
        act = act.astype(BF)
        fh[...] += nn(act, down)
        inner_grad = (nt(low, down) * slope).astype(BF)
        add_panels((8 + j) * per_block, tn(act, low))
        add_panels((4 + j) * per_block, tn(n2, inner_grad))
        fgrad[...] += nt(inner_grad, up)
        if j == blocks // 2 - 1:
            tick(new=4)

    for l in range(2):
        for w in range(2):
            out_ref[l, 0, w * half : (w + 1) * half] = fh[w * rows + l * half : w * rows + (l + 1) * half].astype(BF)

    hidden = win_s[...] + nn(joined(fo), f_out[...])
    z2, r2 = norm(hidden)
    grad = fgrad[...]
    acc_norm[1:2] += jnp.sum(grad * z2, 0, keepdims=True)
    acc_norm[3:4] += jnp.sum(grad, 0, keepdims=True)
    hidden_grad = fdy[...] + norm_back(grad, f_gain[1:2], z2, r2)
    fgrad[...] = hidden_grad
    low = hidden_grad.astype(BF)
    add_panels(3 * per_block, tn(joined(fo), low))
    att_grad = nt(low, f_out[...]).astype(BF)
    tick(new=5)
    for w in range(2):
        for g in range(lane_groups):
            fo[w * lane_groups + g] = att_grad[w * rows : (w + 1) * rows, g * LANES : (g + 1) * LANES]

    @pl.loop(0, 2 * lane_groups, unroll=UNROLL)
    def _(i):
        queries = stack2(fq[i])
        grads = stack2(fo[i])
        prob_grads = nt(fv[i], grads)
        probs, terms = [], []
        for j, span in enumerate(spans):
            prob = fp[i, :, span]
            probs.append(prob.astype(BF))
            ds = score_back(prob, prob_grads[:, span]).astype(BF)
            terms.append(ds)
            if j < heads:
                ds_main[step * (2 * lane_groups * heads) + i * heads + j] = ds
            else:
                ds_tail[step * (2 * lane_groups) + i] = ds
        probs, terms = jnp.concatenate(probs, 1), jnp.concatenate(terms, 1)
        fdv[i] = nn(probs, grads).astype(BF)
        fdk[i] = (nn(terms, queries) * root).astype(BF)
        fdq[i] = (fold2(tn(terms, fk[i])) * root).astype(BF)

    z1, r1 = norm(win_s[...])
    n1 = (z1 * f_gain[0:1] + f_shift[0:1]).astype(BF)
    first = jnp.zeros((2 * rows, width2), F32)
    for t, src in enumerate((fdq, fdk, fdv)):
        part = joined(src)
        add_panels(t * per_block, tn(n1, part))
        first += nt(part, f_qkv[:, t * width2 : (t + 1) * width2])
    acc_norm[0:1] += jnp.sum(first * z1, 0, keepdims=True)
    acc_norm[2:3] += jnp.sum(first, 0, keepdims=True)
    fgrad[...] += norm_back(first, f_gain[0:1], z1, r1)

    tick(new=6)

    @pl.when(step == 2)
    def _():
        for owner, dest in ((side, own_f), (1 - side, give_f)):

            @pl.loop(0, panels // 2)
            def _(n):
                panel = acc[pl.ds(2 * (owner * (panels // 2) + n), 2)].reshape(width2, LANES)
                dest[pl.ds(pl.multiple_of(n * width2, 16), width2), :] = panel.astype(BF)

            norms = acc_norm[...]
            norms = jnp.concatenate(
                [norms[:, g * LANES : (g + 1) * LANES] for g in range(lane_groups)]
                + [jnp.zeros((EXTRA - 4 * lane_groups, LANES), F32)],
                0,
            )
            dest[halves : halves + EXTRA] = norms.astype(BF)
        own_f[halves + EXTRA :] = jnp.zeros((own_f.shape[0] - halves - EXTRA, LANES), BF)
        joining_half().start()

    packs = [own_e.at[step, l * ROWS1 : (l + 1) * ROWS1] for l in both]
    lift_grads = [
        jnp.concatenate([fgrad[w * rows + l * half : w * rows + (l + 1) * half] for w in both], 0).astype(BF)
        for l in both
    ]
    d_outs = [nt(lift_grads[l], w_lift[l][0]) for l in both]
    for l in both:
        put_panels(packs[l], 12 * width1, tn(res_s[l], lift_grads[l]))
    norm_grads = [[None] * 4 for _ in both]
    hidden_grads, att_grads, mixed, first_grads = [None] * 2, [None] * 2, [None] * 2, [None] * 2
    inner_grads = [(nn(d_outs[l].astype(BF), w_down[l][0]) * gp_s[l]).astype(BF) for l in both]
    for l in both:
        put_panels(packs[l], 15 * width1, tn(d_outs[l].astype(BF), act_s[l]))
        put_panels(packs[l], 6 * width1, tn(n2_s[l], inner_grads[l]))
    for l in both:
        grad = nt(inner_grads[l], w_up[l][0])
        z2, r2 = norm(h_s[l])
        norm_grads[l][1] = jnp.sum(grad * z2, 0, keepdims=True)
        norm_grads[l][3] = jnp.sum(grad, 0, keepdims=True)
        hidden_grads[l] = d_outs[l] + norm_back(grad, gains1[l][0, 1:2], z2, r2)
    for l in both:
        att_grads[l] = nt(hidden_grads[l].astype(BF), w_out[l][0]).astype(BF).astype(F32)
    out_grads = [tn(o_s[l].astype(BF), hidden_grads[l].astype(BF)) for l in both]
    grads = [stack1(att_grads[l][part]) for l, w, part in windows]
    terms = [
        score_back(p_s[l, w], nt(v_s[l, part].astype(BF), grads[n])).astype(BF)
        for n, (l, w, part) in enumerate(windows)
    ]
    dvs = [nn(p_s[l, w].astype(BF), grads[n]) for n, (l, w, part) in enumerate(windows)]
    dks = [nn(terms[n], stack1(q_s[l, part])) * root for n, (l, w, part) in enumerate(windows)]
    dqs = [fold1(tn(terms[n], k_s[l, part].astype(BF))) * root for n, (l, w, part) in enumerate(windows)]
    for l in both:
        mixed[l] = jnp.concatenate(
            [jnp.concatenate([dqs[n], dks[n], dvs[n]], 1) for n in (2 * l, 2 * l + 1)], 0
        ).astype(BF)
    for l in both:
        put_panels(packs[l], 0, jnp.concatenate([tn(n1_s[l], mixed[l]), out_grads[l]], 1))
    for l in both:
        first = nt(mixed[l], w_qkv[l][0])
        z1, r1 = norm(x_s[l, step].astype(F32))
        norm_grads[l][0] = jnp.sum(first * z1, 0, keepdims=True)
        norm_grads[l][2] = jnp.sum(first, 0, keepdims=True)
        norms = jnp.pad(jnp.concatenate(norm_grads[l], 0), ((0, 4), (0, 2 * LANES - width1)))
        norms = jnp.concatenate([norms[:4, :LANES], norms[:4, LANES:], jnp.zeros((8, LANES), F32)], 0)
        packs[l][21 * width1 : 21 * width1 + EXTRA] = norms.astype(BF)
        packs[l][21 * width1 + EXTRA :] = jnp.zeros((ROWS1 - 21 * width1 - EXTRA, LANES), BF)
        xg_s[l, step] = hidden_grads[l] + norm_back(first, gains1[l][0, 0:1], z1, r1)
    for copy in tokens_grad(step):
        copy.start()

    @pl.when(step < 2)
    def _():
        run(encoder(step), 0)

    @pl.when(step == 2)
    def _():
        last = encoder(2, ring=True)
        run(last, 0)
        joining_half().wait()
        add_rows(own_f, 0, halves + EXTRA, [(peer_f, 0)])
        run(joining(), 0)
        lay_terms(ds_main, ds_tail, acc)
        acc_t[...] = jnp.zeros_like(acc_t)
        quarters = [n * eights // 4 for n in range(5)]
        for n in range(4):
            add_terms(acc_t, all_pos, acc, quarters[n], quarters[n + 1])
            if n == 1:
                run(encoder(1), 8)
                hand_encoder(1).start()
            run(last, 1 + n)
            run(joining(), 1 + n)
        kinds = [kinds_ref[n % 2, n // 2] for n in range(2 * pairs)]
        picker = type_picker(kinds, heads_all, types)
        many = heads_all * types
        high = acc_t.shape[0] // all_terms
        for k in range(high):
            part = nn(picker, acc_t[k * all_terms : (k + 1) * all_terms].astype(BF)).astype(BF)
            for j in range(SPAN // LANES):
                n = k * (SPAN // LANES) + j
                at = n % high * many
                give_t[n // high, at : at + many] = part[:, j * LANES : (j + 1) * LANES]
        table_half().start()
        table_rows = high * many
        own_t[table_rows:] = jnp.zeros((own_t.shape[0] - table_rows, LANES), BF)
        for copy in [near(give_t.at[side], own_t.at[:table_rows], 0)]:
            copy.start()
            copy.wait()
        run(last, 5)
        run(joining(), 5)
        table_half().wait()
        add_rows(own_t, 0, table_rows, [(peer_t, 0)])
        run(table(), 0)
        run(last, 6)
        run(joining(), 6)
        run(table(), 2)
        run(last, 7)
        run(joining(), 7)
        run(table(), 3)
        run(last, 8)
        hand_encoder(2).start()
        run(joining(), 8)
        hand_over(f_all, 0).start()
        for n in (4, 5, 6, 8):
            run(table(), n)
        hand_over(t_all, 1).start()
        for q in range(pairs):
            hand_encoder(q).wait()
            for copy in tokens_grad(q):
                copy.wait()
        hand_over(f_all, 0).wait()
        hand_over(t_all, 1).wait()


def layer(kinds, tokens, enc, fus, table, pos_index, target, code):
    pairs, rows, width2 = target.shape[1:]
    width1 = tokens.shape[3]
    ff1 = enc[4].shape[2]
    keys = rows
    tails = rows - LANES
    half = rows // 2
    heads, types, count = table.shape
    high = -(-count // SPAN)
    groups = 2 * width2 // LANES
    per = LANES // HEAD
    lanes = per * (LANES + tails)
    panels = 12 * width2 // LANES
    halves = panels // 2 * width2 + EXTRA
    table_rows = high * heads * types
    total1, total2, total3 = (64 * sum(c) for c in (CHUNKS1, CHUNKS2, CHUNKS3))

    def by_row(array, level):
        return pl.BlockSpec((1,) + array.shape[1:], lambda q, level=level: (level * pairs + q, 0, 0))

    def whole(array):
        return pl.BlockSpec(array.shape, lambda q: (0,) * array.ndim, pipeline_mode=pl.Buffered(1))

    anywhere = pl.BlockSpec(memory_space=pl.ANY)
    table = table.reshape(heads * types, count)
    enc_args, enc_specs = [], []
    for array in enc:
        for level in range(2):
            enc_args.append(array)
            enc_specs.append(by_row(array, level))
    moving = pl.BlockSpec((2, 1, rows, width2), lambda q: (0, q, 0, 0))
    dma = pltpu.SemaphoreType.DMA
    vmem = pltpu.VMEM
    return pl.pallas_call(
        layer_kernel,
        grid=(pairs,),
        out_shape=(
            jax.ShapeDtypeStruct((2, pairs, rows, width2), BF),
            jax.ShapeDtypeStruct((1, 2 * pairs, rows, width1), F32),
            jax.ShapeDtypeStruct((2, pairs, total1, LANES), BF),
            jax.ShapeDtypeStruct((2, total2, LANES), BF),
            jax.ShapeDtypeStruct((2, total3, LANES), BF),
        ),
        in_specs=[pl.BlockSpec(memory_space=pltpu.SMEM), anywhere]
        + enc_specs
        + [whole(a) for a in fus]
        + [whole(table), whole(pos_index), moving, whole(code)],
        out_specs=(moving, anywhere, anywhere, anywhere, anywhere),
        scratch_shapes=[
            vmem((2, pairs, rows, width1), BF),
            vmem((2, pairs, rows, width1), F32),
            vmem((2, rows, width1), BF),
            vmem((2, rows, width1), F32),
            vmem((2, rows, width1), F32),
            vmem((2, rows, width1), F32),
            vmem((2, 2, half, HEADS1 * half), F32),
            vmem((2, rows, width1), F32),
            vmem((2, rows, width1), BF),
            vmem((2, rows, width1), F32),
            vmem((2, rows, ff1), BF),
            vmem((2, rows, ff1), F32),
            vmem((2, rows, width1), BF),
            vmem((2 * rows, width2), F32),
            vmem((groups, rows, LANES), BF),
            vmem((groups, rows, LANES), BF),
            vmem((groups, rows, LANES), BF),
            vmem((groups, rows, lanes), F32),
            vmem((groups, rows, LANES), BF),
            vmem((groups, rows, LANES), BF),
            vmem((groups, rows, LANES), BF),
            vmem((groups, rows, LANES), BF),
            vmem((2 * rows, width2), F32),
            vmem((2 * rows, width2), BF),
            vmem((2 * rows, width2), F32),
            vmem((2 * rows, width2), F32),
            vmem((pairs, high * 2 * heads, SPAN), BF),
            vmem((keys + 2 * tails, LANES), jnp.int32),
            vmem((2 * heads, keys + 2 * tails, LANES), F32),
            vmem((groups, keys, per * tails), F32),
            vmem((pairs * 2 * heads, keys, LANES), BF),
            vmem((pairs * groups, keys, per * tails), BF),
            vmem((high * pairs * 2 * heads, SPAN), F32),
            vmem((2 * panels, width2 // 2, LANES), F32),
            vmem((4, width2), F32),
            vmem((pairs, total1, LANES), BF),
            vmem((total2, LANES), BF),
            vmem((halves, LANES), BF),
            vmem((halves, LANES), BF),
            vmem((total3, LANES), BF),
            vmem((2, table_rows, LANES), BF),
            vmem((table_rows, LANES), BF),
        ]
        + [vmem((pairs, 63 * chunk, LANES), BF) for chunk in CHUNKS1]
        + [vmem((63 * chunk, LANES), BF) for chunk in CHUNKS2 + CHUNKS3]
        + [dma((pairs, 3, MESSAGES)), dma((pairs, 3, MESSAGES)), dma((pairs, 3))]
        + [dma((3, MESSAGES)), dma((3, MESSAGES)), dma((3,))] * 2
        + [dma((5 + 2 * pairs,)), dma((5 + 2 * pairs,)), dma((1 + pairs,))],
        compiler_params=pltpu.CompilerParams(
            vmem_limit_bytes=VMEM_LIMIT, collective_id=0, has_side_effects=True
        ),
        name="layer",
    )(kinds, tokens, *enc_args, *fus, table, pos_index, target, code)


def select_kernel(groups_ref, *refs):
    count = (len(refs) - 2) // 3
    arrays, picked, held = (refs[n * count : (n + 1) * count] for n in range(3))
    into, out_of = refs[-2:]
    rows = picked[0].shape[0]
    side = lax.axis_index("lvl")

    def load(n, row):
        level, pair = row // (rows // 2), row % (rows // 2)
        group = groups_ref[level * rows + side * (rows // 2) + pair]
        return pltpu.make_async_copy(arrays[n].at[group], held[n].at[row], into.at[n, row])

    def store(n, row):
        return pltpu.make_async_copy(held[n].at[row], picked[n].at[row], out_of.at[n, row])

    every = [(n, row) for row in range(rows) for n in range(count)]
    for at in every:
        load(*at).start()
    for at in every:
        load(*at).wait()
        store(*at).start()
    for at in every:
        store(*at).wait()


def select_rows(level_group, arrays):
    count = level_group.shape[0] // 2
    anywhere = pl.BlockSpec(memory_space=pl.ANY)
    return pl.pallas_call(
        select_kernel,
        out_shape=tuple(jax.ShapeDtypeStruct((count,) + a.shape[1:], a.dtype) for a in arrays),
        in_specs=[pl.BlockSpec(memory_space=pltpu.SMEM)] + [anywhere] * len(arrays),
        out_specs=(anywhere,) * len(arrays),
        scratch_shapes=[pltpu.VMEM((count,) + a.shape[1:], a.dtype) for a in arrays]
        + [pltpu.SemaphoreType.DMA((len(arrays), count))] * 2,
        compiler_params=pltpu.CompilerParams(vmem_limit_bytes=VMEM_LIMIT),
        name="select_rows",
    )(level_group, *arrays)


def unpack_kernel(
    groups_ref, enc_ref, fus_ref, fus_extra, table_in,
    gain_ref, shift_ref, qkv_ref, out_ref, up_ref, down_ref, lift_ref,
    fg_ref, fs_ref, fq_ref, fo_ref, fu_ref, fd_ref, table_ref,
):
    width = qkv_ref.shape[1]

    def panel(n):
        return enc_ref[0, n * width : (n + 1) * width].astype(F32)

    half = LANES // 2
    for n in range(4):
        qkv_ref[0, :, n * LANES : (n + 1) * LANES] = panel(n)
    mixed, last = panel(4), panel(5)
    qkv_ref[0, :, 4 * LANES :] = mixed[:, :half]
    out_ref[0] = jnp.concatenate([mixed[:, half:], last], 1)
    for n in range(6):
        up_ref[0, :, n * LANES : (n + 1) * LANES] = panel(6 + n)
        down_ref[0, :, n * LANES : (n + 1) * LANES] = panel(15 + n)
    for n in range(3):
        lift_ref[0, :, n * LANES : (n + 1) * LANES] = panel(12 + n)
    norms = enc_ref[0, 21 * width : 21 * width + EXTRA].astype(F32)
    norms = jnp.concatenate([norms[0:4], norms[4:8]], 1)[:, :width]
    gain_ref[0] = norms[0:2]
    shift_ref[0] = norms[2:4]
    i = pl.program_id(0)
    size = fo_ref.shape[0]

    def joining(dest):
        for n in range(size // LANES):
            dest[:, n * LANES : (n + 1) * LANES] = fus_ref[0, n * size : (n + 1) * size].astype(F32)

    @pl.when(i < 3)
    def _():
        joining(fq_ref)

    @pl.when(i == 3)
    def _():
        joining(fo_ref)

    @pl.when((i >= 4) & (i < 8))
    def _():
        joining(fu_ref)

    @pl.when(i >= 8)
    def _():
        joining(fd_ref)

    heads, types, count = table_ref.shape

    @pl.when(i == 0)
    def _():
        extra = fus_extra[0].astype(F32)
        extra = jnp.concatenate([extra[4 * n : 4 * n + 4] for n in range(size // LANES)], 1)
        fg_ref[...] = extra[0:2]
        fs_ref[...] = extra[2:4]
        each = heads * types
        per = table_in.shape[1] // each
        for n in range(2 * per):
            wide = min(LANES, count - n * LANES)
            if wide > 0:
                at = n % per * each
                block = table_in[n // per, at : at + each].astype(F32).reshape(heads, types, LANES)
                table_ref[:, :, n * LANES : n * LANES + wide] = block[:, :, :wide]


def unpack(level_group, enc, fus, table, width1, width2, table_shape):
    groups = enc.shape[0]
    pairs = groups // 4

    def group_of(i, s):
        return s[i % 2 * (groups // 2) + i // (2 * pairs) * pairs + i // 2 % pairs]

    heads, types, count = table_shape
    table_rows = -(-count // SPAN) * heads * types
    panels = width2 * width2 // LANES
    sizes1 = [(2, width1), (2, width1), (width1, 3 * width1), (width1, width1), (width1, 4 * width1), (width1, 4 * width1), (width1, 2 * width1)]
    sizes2 = [(2, width2), (2, width2), (width2, 3 * width2), (width2, width2), (width2, 4 * width2), (4 * width2, width2)]
    square = (width2, width2)
    return pl.pallas_call(
        unpack_kernel,
        out_shape=tuple(jax.ShapeDtypeStruct((groups,) + s, F32) for s in sizes1)
        + tuple(jax.ShapeDtypeStruct(s, F32) for s in sizes2)
        + (jax.ShapeDtypeStruct(table_shape, F32),),
        grid_spec=pltpu.PrefetchScalarGridSpec(
            num_scalar_prefetch=1,
            grid=(groups,),
            in_specs=[
                pl.BlockSpec((1,) + enc.shape[1:], lambda i, s: (i, 0, 0)),
                pl.BlockSpec((1, panels, LANES), lambda i, s: (i // 6, i % 6, 0)),
                pl.BlockSpec((1, EXTRA, LANES), lambda i, s: (0, 6 * panels // EXTRA, 0)),
                pl.BlockSpec((2, table_rows, LANES), lambda i, s: (0, 0, 0)),
            ],
            out_specs=tuple(pl.BlockSpec((1,) + s, lambda i, s: (group_of(i, s), 0, 0)) for s in sizes1)
            + (
                pl.BlockSpec((2, width2), lambda i, s: (0, 0)),
                pl.BlockSpec((2, width2), lambda i, s: (0, 0)),
                pl.BlockSpec(square, lambda i, s: (0, jnp.minimum(i, 2))),
                pl.BlockSpec(square, lambda i, s: (0, 0)),
                pl.BlockSpec(square, lambda i, s: (0, jnp.clip(i - 4, 0, 3))),
                pl.BlockSpec(square, lambda i, s: (jnp.clip(i - 8, 0, 3), 0)),
                pl.BlockSpec(table_shape, lambda i, s: (0, 0, 0)),
            ),
        ),
        compiler_params=pltpu.CompilerParams(vmem_limit_bytes=VMEM_LIMIT),
        name="unpack",
    )(level_group, enc, fus, fus, table)


def shards(
    tokens_in,
    enc_gains,
    enc_shifts,
    enc_qkv,
    enc_out,
    enc_up,
    enc_down,
    enc_lift,
    fus_gains,
    fus_shifts,
    fus_qkv,
    fus_out,
    fus_up,
    fus_down,
    fus_table,
    target,
    loss_code,
    level_group,
    window_type,
    pos_index,
):
    enc = select_rows(
        level_group, (enc_gains, enc_shifts, enc_qkv, enc_out, enc_up, jnp.swapaxes(enc_down, 1, 2), enc_lift)
    )
    output, x_grad, enc_sums, fus_sums, table_sums = layer(
        window_type.T,
        tokens_in,
        enc,
        (fus_gains, fus_shifts, fus_qkv, fus_out, fus_up, fus_down),
        fus_table,
        pos_index,
        target,
        jnp.swapaxes(loss_code, 0, 1),
    )
    grads = unpack(
        level_group,
        enc_sums.reshape(level_group.shape[0], ROWS1, LANES),
        fus_sums,
        table_sums,
        enc_out.shape[1],
        fus_out.shape[0],
        fus_table.shape,
    )
    return (output, x_grad, *grads[:5], jnp.swapaxes(grads[5], 1, 2), *grads[6:])


def solution(mesh):
    copied = P()
    in_specs = (
        (P("lvl", None, "win", None),)
        + (copied,) * 14
        + (P(None, "lvl", "win", None), P(None, "lvl", "win"), copied, P("lvl", "win"), copied)
    )
    out_specs = (P(None, "lvl", "win", None), P("lvl", None, "win", None)) + (copied,) * 14
    return jax.shard_map(shards, mesh=mesh, in_specs=in_specs, out_specs=out_specs, check_vma=False)
```

```python
import functools

import jax
import jax.numpy as jnp
from jax import lax
from jax.experimental import pallas as pl
from jax.experimental.pallas import tpu as pltpu
from jax.sharding import PartitionSpec as P

HEADS1 = 6
HEADS2 = 12
HEAD = 32
EPS = 1e-05
LANES = 128
SPAN = 256
PER = 4
UNROLL = 6
ROWS1 = 4096
CHUNKS1 = (48, 48, 32)
CHUNKS2 = (32, 32, 48)
CHUNKS3 = (16, 16, 16)
EXTRA = 16
VMEM_LIMIT = 60 * 1024 * 1024

BF = jnp.bfloat16
F32 = jnp.float32


def nn(a, b):
    return lax.dot_general(a, b, (((1,), (0,)), ((), ())), preferred_element_type=F32)


def nt(a, b):
    return lax.dot_general(a, b, (((1,), (1,)), ((), ())), preferred_element_type=F32)


def tn(a, b):
    return lax.dot_general(a, b, (((0,), (0,)), ((), ())), preferred_element_type=F32)


RING = 4
STRIDES = (16, 4, 1)
ORDERS = ((0, 1, 2), (1, 2, 0), (2, 0, 1))
MESH = pl.DeviceIdType.MESH
MESSAGES = 22


def coordinate(axis):
    return lax.rem(lax.axis_index("win") // STRIDES[axis], RING)


def along(axis, hops):
    place = lax.axis_index("win")
    mine = coordinate(axis)
    other = lax.rem(mine + hops, RING)
    return (lax.axis_index("lvl"), place + (other - mine) * STRIDES[axis])


def partner():
    return (1 - lax.axis_index("lvl"), lax.axis_index("win"))


def add_rows(dest, at, rows, others):
    step = max(s for s in (128, 112, 96, 64, 48, 32, 16) if rows % s == 0)

    @pl.loop(0, rows // step)
    def _(i):
        here = pl.ds(pl.multiple_of(at + i * step, 16), step)
        total = dest[here, :].astype(F32)
        for ref, start in others:
            total += ref[pl.ds(pl.multiple_of(start + i * step, 16), step), :].astype(F32)
        dest[here, :] = total.astype(BF)


def rows_of(ref, at, size):
    return ref.at[pl.ds(pl.multiple_of(at, 16), size)]


class Place:
    def __init__(self):
        self.here = [coordinate(axis) for axis in range(3)]
        self.chips = {(axis, hops): along(axis, hops) for axis in range(3) for hops in (1, 2, 3)}
        self.partner = partner()


class Part:
    def __init__(self, place, own, out, box, send, recv, keep, base, chunk, order, ring):
        self.own, self.out, self.box, self.send, self.recv, self.keep = own, out, box, send, recv, keep
        self.place, self.axes, self.ring = place, order, ring
        self.here = [place.here[a] for a in order]
        self.big, self.mid, self.chunk = 16 * chunk, 4 * chunk, chunk
        self.base = base
        self.first = base + self.here[0] * self.big
        self.second = self.first + self.here[1] * self.mid
        self.third = self.second + self.here[2] * chunk

    def top(self, hops):
        return self.base + jnp.bitwise_and(self.here[0] + hops, RING - 1) * self.big

    def message(self, n):
        big, mid, chunk = self.big, self.mid, self.chunk
        half = big // 2
        up, down = (0, 1), (0, RING - 1)
        own, out, box = self.own, self.out, self.box
        after = 3 * big
        if n < 6 and not self.ring:
            hops = (1, 3, 2)[n]
            src, dst, to = rows_of(own, self.top(hops), big), rows_of(box, n * big, big), (0, hops)
        elif n == 0:
            src, dst, to = rows_of(own, self.top(2), half), rows_of(box, 0, half), up
        elif n == 1:
            src, dst, to = rows_of(own, self.top(2) + half, half), rows_of(box, half, half), down
        elif n == 2:
            src, dst, to = rows_of(own, self.top(1) + half, half), rows_of(box, big + half, half), up
        elif n == 3:
            src, dst, to = rows_of(own, self.top(3), half), rows_of(box, 2 * big, half), down
        elif n == 4:
            src, dst, to = rows_of(own, self.top(1), half), rows_of(box, big, half), up
        elif n == 5:
            src, dst, to = rows_of(own, self.top(3) + half, half), rows_of(box, 2 * big + half, half), down
        elif n < 9:
            hops = (1, 3, 2)[n - 6]
            at = self.first + jnp.bitwise_and(self.here[1] + hops, RING - 1) * mid
            src, dst, to = rows_of(own, at, mid), rows_of(box, after + (n - 6) * mid, mid), (1, hops)
        elif n < 12:
            hops = (1, 3, 2)[n - 9]
            at = self.second + jnp.bitwise_and(self.here[2] + hops, RING - 1) * chunk
            src, to = rows_of(own, at, chunk), (2, hops)
            dst = rows_of(box, after + 3 * mid + (n - 9) * chunk, chunk)
        elif n < 15:
            src, dst = rows_of(own, self.third, chunk), rows_of(out, self.third, chunk)
            to = (2, (1, 3, 2)[n - 12])
        elif n < 18:
            src = dst = rows_of(out, self.second, mid)
            to = (1, (1, 3, 2)[n - 15])
        elif not self.ring:
            src = dst = rows_of(out, self.first, big)
            to = (0, (1, 3, 2)[n - 18])
        elif n < 20:
            src = dst = rows_of(out, self.first, big)
            to = (up, down)[n - 18]
        elif n == 20:
            src = dst = rows_of(out, self.top(3), half)
            to = up
        else:
            src = dst = rows_of(out, self.top(1) + half, half)
            to = down
        device = self.place.chips[self.axes[to[0]], to[1]]
        return pltpu.make_async_remote_copy(
            src, dst, self.send.at[n], self.recv.at[n], device_id=device, device_id_type=MESH
        )

    def start(self, *numbers):
        for n in numbers:
            self.message(n).start()

    def wait(self, *numbers):
        for n in numbers:
            self.message(n).wait()

    def kept(self):
        return pltpu.make_async_copy(
            rows_of(self.own, self.third, self.chunk), rows_of(self.out, self.third, self.chunk), self.keep
        )

    def stage(self, k):
        big, mid, chunk, own, box = self.big, self.mid, self.chunk, self.own, self.box
        half, after = big // 2, 3 * big
        if k == 0:
            self.start(*((0, 1, 2, 3) if self.ring else (2, 0, 1)))
        elif k == 1 and self.ring:
            self.wait(0)
            add_rows(own, self.top(1), half, [(box, 0)])
            self.start(4)
            self.wait(1)
            add_rows(own, self.top(3) + half, half, [(box, half)])
            self.start(5)
        elif k == 2:
            if self.ring:
                self.wait(2, 3, 4, 5)
            else:
                self.wait(0, 1, 2)
            add_rows(own, self.first, big, [(box, n * big) for n in ((1, 2) if self.ring else (0, 1, 2))])
            self.start(6, 7, 8)
        elif k == 3:
            self.wait(6, 7, 8)
            add_rows(own, self.second, mid, [(box, after + n * mid) for n in range(3)])
            self.start(9, 10, 11)
        elif k == 4:
            self.wait(9, 10, 11)
            add_rows(own, self.third, chunk, [(box, after + 3 * mid + n * chunk) for n in range(3)])
            self.kept().start()
            self.start(12, 13, 14)
        elif k == 5:
            self.kept().wait()
            self.wait(12, 13, 14)
            self.start(15, 16, 17)
        elif k == 6:
            self.wait(15, 16, 17)
            self.start(*((18, 19) if self.ring else (20, 18, 19)))
        elif k == 7 and self.ring:
            self.wait(18)
            self.start(20)
            self.wait(19)
            self.start(21)
        elif k == 8:
            self.wait(*((20, 21) if self.ring else (18, 19, 20)))


def parts_of(place, chunks, own, out, boxes, sems, ring):
    parts, base = [], 0
    for n, chunk in enumerate(chunks):
        send, recv, keep = (sem.at[n] for sem in sems)
        parts.append(Part(place, own, out, boxes[n], send, recv, keep, base, chunk, ORDERS[n], ring))
        base += 64 * chunk
    return parts


def run(parts, k):
    for part in parts:
        part.stage(k)


def type_picker(kinds, heads, types):
    shape = (heads * types, len(kinds) * heads)
    row = lax.broadcasted_iota(jnp.int32, shape, 0)
    column = lax.broadcasted_iota(jnp.int32, shape, 1)
    kind = jnp.full(shape, kinds[-1], jnp.int32)
    for n in reversed(range(len(kinds) - 1)):
        kind = jnp.where(column < (n + 1) * heads, kinds[n], kind)
    same_head = (row // types) == (column % heads)
    return (same_head & ((row % types) == kind)).astype(F32).astype(BF)


def lay_positions(pos_ref, all_pos):
    keys = pos_ref.shape[0]
    tails = keys - LANES
    all_pos[:keys] = pos_ref[...].astype(F32).T[:, :LANES].astype(jnp.int32)
    all_pos[keys : keys + tails] = pos_ref[LANES:, :LANES]
    all_pos[keys + tails :] = jnp.full((tails, LANES), -1, jnp.int32)
    all_pos[keys + tails :, : keys - LANES] = pos_ref[LANES:, LANES:]


def one_hot_of(pos):
    low = jnp.bitwise_and(pos, SPAN - 1)
    return (lax.broadcasted_iota(jnp.int32, (SPAN, pos.shape[1]), 0) == low).astype(F32).astype(BF)


def spread_table(picker, table_ref, t2):
    rows, count = picker.shape[1], table_ref.shape[1]
    for k in range(t2.shape[0] // rows):
        width = min(SPAN, count - k * SPAN)
        part = table_ref[:, k * SPAN : k * SPAN + width].astype(BF)
        t2[k * rows : (k + 1) * rows, :width] = tn(picker, part).astype(BF)
        if width < SPAN:
            t2[k * rows : (k + 1) * rows, width:] = jnp.zeros((rows, SPAN - width), BF)


def look_up(t2, all_pos, dest, first, last):
    rows = dest.shape[0]
    high = t2.shape[0] // rows

    @pl.loop(first, last, unroll=2)
    def _(i):
        at = pl.multiple_of(i * 8, 8)
        eight = all_pos[pl.ds(at, 8), :]
        for s in range(0, 8, PER):
            pos = jnp.concatenate([eight[s + j : s + j + 1] for j in range(PER)], 1)
            top = jnp.right_shift(pos, 8)
            spread = nn(t2[...], one_hot_of(pos))
            picked = jnp.zeros((rows, PER * LANES), F32)
            for k in range(high):
                picked = jnp.where(top == k, spread[k * rows : (k + 1) * rows], picked)
            for j in range(PER):
                dest[:, pl.ds(at + s + j, 1), :] = picked[:, j * LANES : (j + 1) * LANES].reshape(rows, 1, LANES)


def turn_tails(bias, bias_tail, keys):
    tails = keys - LANES
    per = bias_tail.shape[2] // tails
    for i in range(bias_tail.shape[0]):
        lines = bias[i * per : (i + 1) * per, keys : keys + tails].reshape(per * tails, LANES)
        bias_tail[i, :LANES] = lines.T
        lines = bias[i * per : (i + 1) * per, keys + tails : keys + 2 * tails].reshape(per * tails, LANES)
        bias_tail[i, LANES:] = lines.T[: keys - LANES]


def lay_terms(ds_main, ds_tail, lines):
    rows, keys = ds_main.shape[:2]
    tails = keys - LANES
    per = ds_tail.shape[2] // tails

    @pl.loop(0, ds_tail.shape[0])
    def _(i):
        at = pl.ds(i * per, per)
        lines[at, :keys] = ds_main[at].astype(F32)
        block = ds_tail[i].astype(F32)
        lines[at, keys : keys + tails] = block[:LANES].T.reshape(per, tails, LANES)
        lines[at, keys + tails : keys + 2 * tails] = jnp.zeros((per, tails, LANES), F32)
        lines[at, keys + tails : keys + 2 * tails, : keys - LANES] = block[LANES:].T.reshape(per, tails, keys - LANES)


def add_terms(acc, all_pos, lines, first, last):
    rows = lines.shape[0]
    high = acc.shape[0] // rows

    @pl.loop(first, last, unroll=2)
    def _(i):
        at = pl.multiple_of(i * 8, 8)
        eight = all_pos[pl.ds(at, 8), :]
        total = None
        for s in range(0, 8, PER):
            pos = jnp.concatenate([eight[s + j : s + j + 1] for j in range(PER)], 1)
            terms = jnp.concatenate([lines[:, pl.ds(at + s + j, 1), :].reshape(rows, LANES) for j in range(PER)], 1)
            top = jnp.right_shift(pos, 8)
            parts = jnp.concatenate([jnp.where(top == k, terms, 0.0) for k in range(high)], 0)
            term = nt(parts.astype(BF), one_hot_of(pos))
            total = term if total is None else total + term
        acc[...] += total


def norm(values):
    centred = values - jnp.mean(values, -1, keepdims=True)
    spread = jnp.mean(centred * centred, -1, keepdims=True)
    scale = lax.rsqrt(spread + EPS)
    return centred * scale, scale


def norm_back(grad, gain, unit, scale):
    scaled = grad * gain
    first = jnp.mean(scaled, -1, keepdims=True)
    second = jnp.mean(scaled * unit, -1, keepdims=True)
    return (scaled - first - unit * second) * scale


def gelu_pair(v):
    half = jnp.exp(-0.5 * v * v)
    t = 1.0 / (1.0 + 0.23164189 * jnp.abs(v))
    series = t * (0.127414796 + t * (-0.142248368 + t * (0.7107068705 + t * (-0.7265760135 + t * 0.5307027145))))
    tail = series * half
    phi = jnp.where(v >= 0.0, 1.0 - tail, tail)
    return v * phi, phi + v * half * 0.3989422804014327


def head_masks(width):
    lane = lax.broadcasted_iota(jnp.int32, (1, width), 1)
    return [(lane // HEAD) == h for h in range(width // HEAD)]


def keep(mask, values):
    return jnp.where(mask, values, 0.0)


def put_panels(ref, at, values):
    rows = values.shape[0]
    for j in range(values.shape[1] // LANES):
        ref[at + j * rows : at + (j + 1) * rows] = values[:, j * LANES : (j + 1) * LANES].astype(ref.dtype)


def softmax_rows(scores):
    top = jnp.max(scores, 0, keepdims=True)
    e = jnp.exp(scores - top)
    return e * (1.0 / jnp.sum(e, 0, keepdims=True))


def score_back(prob, grad):
    return prob * (grad - jnp.sum(grad * prob, 0, keepdims=True))


def layer_kernel(
    kinds_ref, tokens_ref,
    e_gain0, e_gain1, e_shift0, e_shift1,
    e_qkv0, e_qkv1, e_out0, e_out1, e_up0, e_up1, e_down0, e_down1, e_lift0, e_lift1,
    f_gain, f_shift, f_qkv, f_out, f_up, f_down,
    table_ref, pos_ref, target_ref, code_ref,
    out_ref, xg_out, e_all, f_all, t_all,
    x_s, xg_s, n1_s, q_s, k_s, v_s, p_s, o_s, n2_s, h_s, act_s, gp_s, res_s,
    win_s, fq, fk, fv, fp, fo, fdq, fdk, fdv, fh, fn2, fdy, fgrad,
    t2, all_pos, bias_main, bias_tail, ds_main, ds_tail, acc_t,
    acc, acc_norm, own_e, own_f, give_f, peer_f, own_t, give_t, peer_t,
    be0, be1, be2, bf0, bf1, bf2, bt0, bt1, bt2,
    se, re, ke, sf, rf, kf, st, rt, kt, misc_send, misc_recv, misc_near,
):
    boxes_e, boxes_f, boxes_t = (be0, be1, be2), (bf0, bf1, bf2), (bt0, bt1, bt2)
    sems_e, sems_f, sems_t = (se, re, ke), (sf, rf, kf), (st, rt, kt)
    step = pl.program_id(0)
    side = lax.axis_index("lvl")
    rows = x_s.shape[2]
    width1 = x_s.shape[3]
    width2 = f_qkv.shape[0]
    half = rows // 2
    keys = rows
    root = HEAD ** (-0.5)
    masks1 = head_masks(width1)
    masks2 = head_masks(LANES)
    picks2 = [m.astype(F32).astype(BF) for m in masks2]
    gains1, shifts1 = (e_gain0, e_gain1), (e_shift0, e_shift1)
    w_qkv, w_out, w_up = (e_qkv0, e_qkv1), (e_out0, e_out1), (e_up0, e_up1)
    w_down, w_lift = (e_down0, e_down1), (e_lift0, e_lift1)

    pairs = x_s.shape[1]
    heads_all = width2 // HEAD
    types = table_ref.shape[0] // heads_all
    terms_each = 2 * heads_all
    panels = 12 * width2 // LANES
    halves = panels // 2 * width2

    place = Place()

    def encoder(q, ring=False):
        return parts_of(
            place, CHUNKS1, own_e.at[q], e_all.at[side, q], [b.at[q] for b in boxes_e], [s.at[q] for s in sems_e], ring
        )

    def joining():
        return parts_of(place, CHUNKS2, own_f, f_all.at[side], boxes_f, sems_f, True)

    def table():
        return parts_of(place, CHUNKS3, own_t, t_all.at[side], boxes_t, sems_t, False)

    def hand_over(ref, n):
        return remote(ref.at[side], ref.at[side], 3 + pairs + n)

    def hand_encoder(q):
        return remote(e_all.at[side, q], e_all.at[side, q], 5 + pairs + q)

    def hand_last(quarters, what):
        for k, part in enumerate(encoder(2, ring=True)):
            for hops in quarters:
                rows = rows_of(part.out, part.top(hops), part.big)
                getattr(remote(rows, rows, 4 + 2 * pairs + 4 * k + hops), what)()

    def tick(new=None, old=None):
        if new is not None:

            @pl.when(step >= 1)
            def _():
                run(encoder(step - 1), new)

        if old is not None:

            @pl.when(step == 2)
            def _():
                if old < 9:
                    run(encoder(0), old)
                if old == 8:
                    hand_encoder(0).start()

    def remote(src, dst, n):
        return pltpu.make_async_remote_copy(
            src, dst, misc_send.at[n], misc_recv.at[n], device_id=place.partner, device_id_type=MESH
        )

    def near(src, dst, n):
        return pltpu.make_async_copy(src, dst, misc_near.at[n])

    def tokens():
        given = remote(tokens_ref.at[0, pl.ds((1 - side) * pairs, pairs)], x_s.at[side], 0)
        taken = near(tokens_ref.at[0, pl.ds(side * pairs, pairs)], x_s.at[side], 0)
        return given, taken

    def tokens_grad(q):
        given = remote(xg_s.at[1 - side, q], xg_out.at[0, side * pairs + q], 1 + q)
        taken = near(xg_s.at[side, q], xg_out.at[0, side * pairs + q], 1 + q)
        return given, taken

    def joining_half():
        return remote(give_f, peer_f, 1 + pairs)

    def table_half():
        return remote(give_t.at[1 - side], peer_t, 2 + pairs)

    @pl.when(step == 0)
    def _():
        barrier = pltpu.get_barrier_semaphore()
        friends = list(place.chips.values()) + [place.partner]
        for device in friends:
            pl.semaphore_signal(barrier, inc=1, device_id=device, device_id_type=MESH)
        pl.semaphore_wait(barrier, len(friends))
        for copy in tokens():
            copy.start()
        lay_positions(pos_ref, all_pos)
        for q in range(pairs):
            picker = type_picker([kinds_ref[w, q] for w in range(2)], heads_all, types)
            spread_table(picker, table_ref, t2.at[q])
        acc[...] = jnp.zeros_like(acc)
        acc_norm[...] = jnp.zeros_like(acc_norm)

    eights = (keys + 2 * (keys - LANES)) // 8
    look_up(t2.at[step], all_pos, bias_main, 0, eights // 2)
    tick(new=2)
    look_up(t2.at[step], all_pos, bias_main, eights // 2, eights)
    turn_tails(bias_main, bias_tail, keys)
    tick(old=8)

    @pl.when(step == 0)
    def _():
        for copy in tokens():
            copy.wait()

    def stack1(values):
        return jnp.concatenate([keep(m, values) for m in masks1], 0).astype(BF)

    def fold1(stacked):
        total = keep(masks1[0], stacked[:half])
        for h in range(1, HEADS1):
            total += keep(masks1[h], stacked[h * half : (h + 1) * half])
        return total

    both = range(2)
    windows = [(l, w, slice(w * half, (w + 1) * half)) for l in both for w in both]
    xs = [x_s[l, step].astype(F32) for l in both]
    for l in both:
        z1, _ = norm(xs[l])
        n1_s[l] = (z1 * gains1[l][0, 0:1] + shifts1[l][0, 0:1]).astype(BF)
    for l in both:
        qkv = nn(n1_s[l], w_qkv[l][0])
        q_s[l] = qkv[:, :width1].astype(BF).astype(F32)
        k_s[l] = qkv[:, width1 : 2 * width1].astype(BF).astype(F32)
        v_s[l] = qkv[:, 2 * width1 :].astype(BF).astype(F32)
    for l, w, part in windows:
        p_s[l, w] = softmax_rows(nt(k_s[l, part].astype(BF), stack1(q_s[l, part])) * root)
    for l, w, part in windows:
        o_s[l, part] = fold1(tn(p_s[l, w].astype(BF), v_s[l, part].astype(BF)))
    for l in both:
        h = x_s[l, step].astype(F32) + nn(o_s[l].astype(BF), w_out[l][0])
        h_s[l] = h
        z2, _ = norm(h)
        n2_s[l] = (z2 * gains1[l][0, 1:2] + shifts1[l][0, 1:2]).astype(BF)
    for l in both:
        act, slope = gelu_pair(nn(n2_s[l], w_up[l][0]))
        act_s[l] = act.astype(BF)
        gp_s[l] = slope
    for l in both:
        res_s[l] = (h_s[l] + nt(act_s[l], w_down[l][0])).astype(BF)
    for l in both:
        lifted = nn(res_s[l], w_lift[l][0]).astype(BF).astype(F32)
        for w in range(2):
            win_s[w * rows + l * half : w * rows + (l + 1) * half] = lifted[w * half : (w + 1) * half]

    eye = lax.broadcasted_iota(jnp.int32, (rows, rows), 0) == lax.broadcasted_iota(jnp.int32, (rows, rows), 1)
    for l in range(2):
        codes = code_ref[:, l].astype(F32)
        chosen = lax.broadcasted_iota(jnp.int32, codes.shape, 0) == step
        weight = 0.5 * jnp.exp(0.35 * jnp.sum(jnp.where(chosen, codes, 0.0), 0, keepdims=True))
        column = jnp.sum(jnp.where(eye, weight, 0.0), 1, keepdims=True)
        direction = column * target_ref[l, 0].astype(F32)
        for w in range(2):
            fdy[w * rows + l * half : w * rows + (l + 1) * half] = direction[w * half : (w + 1) * half]

    lane_groups = width2 // LANES
    z1, _ = norm(win_s[...])
    fn1 = (z1 * f_gain[0:1] + f_shift[0:1]).astype(BF)
    for t, dest in enumerate((fq, fk, fv)):
        part = nn(fn1, f_qkv[:, t * width2 : (t + 1) * width2]).astype(BF)
        for w in range(2):
            for g in range(lane_groups):
                dest[w * lane_groups + g] = part[w * rows : (w + 1) * rows, g * LANES : (g + 1) * LANES]
    tails = rows - LANES
    tick(new=3)

    heads = LANES // HEAD
    lanes = heads * LANES + heads * tails
    spans = [slice(j * LANES, min((j + 1) * LANES, lanes)) for j in range(heads + 1)]

    def stack2(values):
        main, tail = values[:LANES], values[LANES:]
        return jnp.concatenate([main * m for m in picks2] + [tail * m for m in picks2], 0)

    def fold2(stacked):
        main = keep(masks2[0], stacked[:LANES])
        tail = keep(masks2[0], stacked[heads * LANES : heads * LANES + tails])
        for h in range(1, heads):
            main += keep(masks2[h], stacked[h * LANES : (h + 1) * LANES])
            tail += keep(masks2[h], stacked[heads * LANES + h * tails : heads * LANES + (h + 1) * tails])
        return jnp.concatenate([main, tail], 0)

    @pl.loop(0, 2 * lane_groups, unroll=UNROLL)
    def _(i):
        scores = nt(fk[i], stack2(fq[i]))
        probs = []
        for j, span in enumerate(spans):
            bias = bias_main[i * heads + j, :keys] if j < heads else bias_tail[i]
            prob = softmax_rows(scores[:, span] * root + bias)
            fp[i, :, span] = prob
            probs.append(prob.astype(BF))
        fo[i] = fold2(tn(jnp.concatenate(probs, 1), fv[i])).astype(BF)


    def joined(ref):
        return jnp.concatenate(
            [jnp.concatenate([ref[w * lane_groups + g] for g in range(lane_groups)], 1) for w in range(2)], 0
        )

    hidden = win_s[...] + nn(joined(fo), f_out[...])
    fh[...] = hidden
    z2, _ = norm(hidden)
    fn2[...] = (z2 * f_gain[1:2] + f_shift[1:2]).astype(BF)

    def add_panels(n, values):
        for j in range(values.shape[1] // LANES):
            panel = values[:, j * LANES : (j + 1) * LANES]
            acc[2 * (n + j) : 2 * (n + j) + 2] += panel.reshape(2, width2 // 2, LANES)

    blocks = f_up.shape[1] // width2
    fgrad[...] = jnp.zeros_like(fgrad)

    per_block = width2 // LANES
    wide = 2 * width2
    for j in range(blocks // 2):
        up = f_up[:, j * wide : (j + 1) * wide]
        down = f_down[j * wide : (j + 1) * wide, :]
        n2 = fn2[...]
        low = fdy[...].astype(BF)
        act, slope = gelu_pair(nn(n2, up))
        act = act.astype(BF)
        fh[...] += nn(act, down)
        inner_grad = (nt(low, down) * slope).astype(BF)
        down_grad = tn(act, low)
        add_panels((8 + 2 * j) * per_block, down_grad[:width2])
        add_panels((9 + 2 * j) * per_block, down_grad[width2:])
        add_panels((4 + 2 * j) * per_block, tn(n2, inner_grad))
        fgrad[...] += nt(inner_grad, up)
        if j == 0:
            tick(new=4)

    for l in range(2):
        for w in range(2):
            out_ref[l, 0, w * half : (w + 1) * half] = fh[w * rows + l * half : w * rows + (l + 1) * half].astype(BF)

    hidden = win_s[...] + nn(joined(fo), f_out[...])
    z2, r2 = norm(hidden)
    grad = fgrad[...]
    acc_norm[1:2] += jnp.sum(grad * z2, 0, keepdims=True)
    acc_norm[3:4] += jnp.sum(grad, 0, keepdims=True)
    hidden_grad = fdy[...] + norm_back(grad, f_gain[1:2], z2, r2)
    fgrad[...] = hidden_grad
    low = hidden_grad.astype(BF)
    add_panels(3 * per_block, tn(joined(fo), low))
    att_grad = nt(low, f_out[...]).astype(BF)
    tick(new=5)
    for w in range(2):
        for g in range(lane_groups):
            fo[w * lane_groups + g] = att_grad[w * rows : (w + 1) * rows, g * LANES : (g + 1) * LANES]

    @pl.loop(0, 2 * lane_groups, unroll=UNROLL)
    def _(i):
        queries = stack2(fq[i])
        grads = stack2(fo[i])
        prob_grads = nt(fv[i], grads)
        probs, terms = [], []
        for j, span in enumerate(spans):
            prob = fp[i, :, span]
            probs.append(prob.astype(BF))
            ds = score_back(prob, prob_grads[:, span]).astype(BF)
            terms.append(ds)
            if j < heads:
                ds_main[i * heads + j] = ds
            else:
                ds_tail[i] = ds
        probs, terms = jnp.concatenate(probs, 1), jnp.concatenate(terms, 1)
        fdv[i] = nn(probs, grads).astype(BF)
        fdk[i] = (nn(terms, queries) * root).astype(BF)
        fdq[i] = (fold2(tn(terms, fk[i])) * root).astype(BF)

    z1, r1 = norm(win_s[...])
    n1 = (z1 * f_gain[0:1] + f_shift[0:1]).astype(BF)
    first = jnp.zeros((2 * rows, width2), F32)
    for t, src in enumerate((fdq, fdk, fdv)):
        part = joined(src)
        add_panels(t * per_block, tn(n1, part))
        first += nt(part, f_qkv[:, t * width2 : (t + 1) * width2])
    acc_norm[0:1] += jnp.sum(first * z1, 0, keepdims=True)
    acc_norm[2:3] += jnp.sum(first, 0, keepdims=True)
    fgrad[...] += norm_back(first, f_gain[0:1], z1, r1)

    tick(new=6)

    @pl.when(step == 2)
    def _():
        for owner, dest in ((side, own_f), (1 - side, give_f)):

            @pl.loop(0, panels // 2)
            def _(n):
                panel = acc[pl.ds(2 * (owner * (panels // 2) + n), 2)].reshape(width2, LANES)
                dest[pl.ds(pl.multiple_of(n * width2, 16), width2), :] = panel.astype(BF)

            norms = acc_norm[...]
            norms = jnp.concatenate(
                [norms[:, g * LANES : (g + 1) * LANES] for g in range(lane_groups)]
                + [jnp.zeros((EXTRA - 4 * lane_groups, LANES), F32)],
                0,
            )
            dest[halves : halves + EXTRA] = norms.astype(BF)
        own_f[halves + EXTRA :] = jnp.zeros((own_f.shape[0] - halves - EXTRA, LANES), BF)
        joining_half().start()

    packs = [own_e.at[step, l * ROWS1 : (l + 1) * ROWS1] for l in both]
    lift_grads = [
        jnp.concatenate([fgrad[w * rows + l * half : w * rows + (l + 1) * half] for w in both], 0).astype(BF)
        for l in both
    ]
    d_outs = [nt(lift_grads[l], w_lift[l][0]) for l in both]
    for l in both:
        put_panels(packs[l], 12 * width1, tn(res_s[l], lift_grads[l]))
    norm_grads = [[None] * 4 for _ in both]
    hidden_grads, att_grads, mixed, first_grads = [None] * 2, [None] * 2, [None] * 2, [None] * 2
    inner_grads = [(nn(d_outs[l].astype(BF), w_down[l][0]) * gp_s[l]).astype(BF) for l in both]
    for l in both:
        put_panels(packs[l], 15 * width1, tn(d_outs[l].astype(BF), act_s[l]))
        put_panels(packs[l], 6 * width1, tn(n2_s[l], inner_grads[l]))
    for l in both:
        grad = nt(inner_grads[l], w_up[l][0])
        z2, r2 = norm(h_s[l])
        norm_grads[l][1] = jnp.sum(grad * z2, 0, keepdims=True)
        norm_grads[l][3] = jnp.sum(grad, 0, keepdims=True)
        hidden_grads[l] = d_outs[l] + norm_back(grad, gains1[l][0, 1:2], z2, r2)
    for l in both:
        att_grads[l] = nt(hidden_grads[l].astype(BF), w_out[l][0]).astype(BF).astype(F32)
    out_grads = [tn(o_s[l].astype(BF), hidden_grads[l].astype(BF)) for l in both]
    for l in both:
        h_s[l] = hidden_grads[l]

    @pl.when(step == 2)
    def _():
        joining_half().wait()
        add_rows(own_f, 0, halves + EXTRA, [(peer_f, 0)])
        run(joining(), 0)

    grads = [stack1(att_grads[l][part]) for l, w, part in windows]
    terms = [
        score_back(p_s[l, w], nt(v_s[l, part].astype(BF), grads[n])).astype(BF)
        for n, (l, w, part) in enumerate(windows)
    ]
    dvs = [nn(p_s[l, w].astype(BF), grads[n]) for n, (l, w, part) in enumerate(windows)]
    dks = [nn(terms[n], stack1(q_s[l, part])) * root for n, (l, w, part) in enumerate(windows)]
    dqs = [fold1(tn(terms[n], k_s[l, part].astype(BF))) * root for n, (l, w, part) in enumerate(windows)]
    for l in both:
        mixed[l] = jnp.concatenate(
            [jnp.concatenate([dqs[n], dks[n], dvs[n]], 1) for n in (2 * l, 2 * l + 1)], 0
        ).astype(BF)
    for l in both:
        put_panels(packs[l], 0, jnp.concatenate([tn(n1_s[l], mixed[l]), out_grads[l]], 1))
    for l in both:
        first = nt(mixed[l], w_qkv[l][0])
        z1, r1 = norm(x_s[l, step].astype(F32))
        norm_grads[l][0] = jnp.sum(first * z1, 0, keepdims=True)
        norm_grads[l][2] = jnp.sum(first, 0, keepdims=True)
        norms = jnp.pad(jnp.concatenate(norm_grads[l], 0), ((0, 4), (0, 2 * LANES - width1)))
        norms = jnp.concatenate([norms[:4, :LANES], norms[:4, LANES:], jnp.zeros((8, LANES), F32)], 0)
        packs[l][21 * width1 : 21 * width1 + EXTRA] = norms.astype(BF)
        packs[l][21 * width1 + EXTRA :] = jnp.zeros((ROWS1 - 21 * width1 - EXTRA, LANES), BF)
        xg_s[l, step] = h_s[l] + norm_back(first, gains1[l][0, 0:1], z1, r1)
    for copy in tokens_grad(step):
        copy.start()

    @pl.when(step < 2)
    def _():
        run(encoder(step), 0)

    last = encoder(2, ring=True)

    @pl.when(step == 2)
    def _():
        run(last, 0)

    lay_terms(ds_main, ds_tail, bias_main)
    acc_t[step] = jnp.zeros(acc_t.shape[1:], F32)
    add_terms(acc_t.at[step], all_pos, bias_main, 0, eights // 2)

    @pl.when(step == 2)
    def _():
        run(last, 1)
        run(joining(), 1)

    add_terms(acc_t.at[step], all_pos, bias_main, eights // 2, eights)

    @pl.when(step == 2)
    def _():
        kinds = [kinds_ref[n % 2, n // 2] for n in range(2 * pairs)]
        picker = type_picker(kinds, heads_all, types)
        many = heads_all * types
        high = acc_t.shape[1] // terms_each
        for k in range(high):
            part = jnp.concatenate([acc_t[q, k * terms_each : (k + 1) * terms_each] for q in range(pairs)], 0)
            part = nn(picker, part.astype(BF)).astype(BF)
            for j in range(SPAN // LANES):
                n = k * (SPAN // LANES) + j
                at = n % high * many
                give_t[n // high, at : at + many] = part[:, j * LANES : (j + 1) * LANES]
        table_half().start()
        table_rows = high * many
        own_t[table_rows:] = jnp.zeros((own_t.shape[0] - table_rows, LANES), BF)
        for copy in [near(give_t.at[side], own_t.at[:table_rows], 0)]:
            copy.start()
            copy.wait()
        run(last, 2)
        run(joining(), 2)
        table_half().wait()
        add_rows(own_t, 0, table_rows, [(peer_t, 0)])
        run(table(), 0)
        run(last, 3)
        run(joining(), 3)
        run(table(), 2)
        run(encoder(1), 8)
        hand_encoder(1).start()
        run(last, 4)
        run(joining(), 4)
        run(table(), 3)
        run(last, 5)
        run(joining(), 5)
        run(table(), 4)
        run(last, 6)
        hand_last((0,), "start")
        run(joining(), 6)
        run(table(), 5)
        run(last, 7)
        hand_last((3, 1), "start")
        run(joining(), 7)
        run(table(), 6)
        run(last, 8)
        hand_last((2,), "start")
        run(joining(), 8)
        hand_over(f_all, 0).start()
        run(table(), 8)
        hand_over(t_all, 1).start()
        hand_last((0, 3, 1, 2), "wait")
        for q in range(pairs - 1):
            hand_encoder(q).wait()
        for q in range(pairs):
            for copy in tokens_grad(q):
                copy.wait()
        hand_over(f_all, 0).wait()
        hand_over(t_all, 1).wait()


def layer(kinds, tokens, enc, fus, table, pos_index, target, code):
    pairs, rows, width2 = target.shape[1:]
    width1 = tokens.shape[3]
    ff1 = enc[4].shape[2]
    keys = rows
    tails = rows - LANES
    half = rows // 2
    heads, types, count = table.shape
    high = -(-count // SPAN)
    groups = 2 * width2 // LANES
    per = LANES // HEAD
    lanes = per * (LANES + tails)
    panels = 12 * width2 // LANES
    halves = panels // 2 * width2 + EXTRA
    table_rows = high * heads * types
    total1, total2, total3 = (64 * sum(c) for c in (CHUNKS1, CHUNKS2, CHUNKS3))

    def by_row(array, level):
        return pl.BlockSpec((1,) + array.shape[1:], lambda q, level=level: (level * pairs + q, 0, 0))

    def whole(array):
        return pl.BlockSpec(array.shape, lambda q: (0,) * array.ndim, pipeline_mode=pl.Buffered(1))

    anywhere = pl.BlockSpec(memory_space=pl.ANY)
    table = table.reshape(heads * types, count)
    enc_args, enc_specs = [], []
    for array in enc:
        for level in range(2):
            enc_args.append(array)
            enc_specs.append(by_row(array, level))
    moving = pl.BlockSpec((2, 1, rows, width2), lambda q: (0, q, 0, 0))
    dma = pltpu.SemaphoreType.DMA
    vmem = pltpu.VMEM
    return pl.pallas_call(
        layer_kernel,
        grid=(pairs,),
        out_shape=(
            jax.ShapeDtypeStruct((2, pairs, rows, width2), BF),
            jax.ShapeDtypeStruct((1, 2 * pairs, rows, width1), F32),
            jax.ShapeDtypeStruct((2, pairs, total1, LANES), BF),
            jax.ShapeDtypeStruct((2, total2, LANES), BF),
            jax.ShapeDtypeStruct((2, total3, LANES), BF),
        ),
        in_specs=[pl.BlockSpec(memory_space=pltpu.SMEM), anywhere]
        + enc_specs
        + [whole(a) for a in fus]
        + [whole(table), whole(pos_index), moving, whole(code)],
        out_specs=(moving, anywhere, anywhere, anywhere, anywhere),
        scratch_shapes=[
            vmem((2, pairs, rows, width1), BF),
            vmem((2, pairs, rows, width1), F32),
            vmem((2, rows, width1), BF),
            vmem((2, rows, width1), F32),
            vmem((2, rows, width1), F32),
            vmem((2, rows, width1), F32),
            vmem((2, 2, half, HEADS1 * half), F32),
            vmem((2, rows, width1), F32),
            vmem((2, rows, width1), BF),
            vmem((2, rows, width1), F32),
            vmem((2, rows, ff1), BF),
            vmem((2, rows, ff1), F32),
            vmem((2, rows, width1), BF),
            vmem((2 * rows, width2), F32),
            vmem((groups, rows, LANES), BF),
            vmem((groups, rows, LANES), BF),
            vmem((groups, rows, LANES), BF),
            vmem((groups, rows, lanes), F32),
            vmem((groups, rows, LANES), BF),
            vmem((groups, rows, LANES), BF),
            vmem((groups, rows, LANES), BF),
            vmem((groups, rows, LANES), BF),
            vmem((2 * rows, width2), F32),
            vmem((2 * rows, width2), BF),
            vmem((2 * rows, width2), F32),
            vmem((2 * rows, width2), F32),
            vmem((pairs, high * 2 * heads, SPAN), BF),
            vmem((keys + 2 * tails, LANES), jnp.int32),
            vmem((2 * heads, keys + 2 * tails, LANES), F32),
            vmem((groups, keys, per * tails), F32),
            vmem((2 * heads, keys, LANES), BF),
            vmem((groups, keys, per * tails), BF),
            vmem((pairs, high * 2 * heads, SPAN), F32),
            vmem((2 * panels, width2 // 2, LANES), F32),
            vmem((4, width2), F32),
            vmem((pairs, total1, LANES), BF),
            vmem((total2, LANES), BF),
            vmem((halves, LANES), BF),
            vmem((halves, LANES), BF),
            vmem((total3, LANES), BF),
            vmem((2, table_rows, LANES), BF),
            vmem((table_rows, LANES), BF),
        ]
        + [vmem((pairs, 63 * chunk, LANES), BF) for chunk in CHUNKS1]
        + [vmem((63 * chunk, LANES), BF) for chunk in CHUNKS2 + CHUNKS3]
        + [dma((pairs, 3, MESSAGES)), dma((pairs, 3, MESSAGES)), dma((pairs, 3))]
        + [dma((3, MESSAGES)), dma((3, MESSAGES)), dma((3,))] * 2
        + [dma((16 + 2 * pairs,)), dma((16 + 2 * pairs,)), dma((1 + pairs,))],
        compiler_params=pltpu.CompilerParams(
            vmem_limit_bytes=VMEM_LIMIT + 2 * 1024 * 1024, collective_id=0, has_side_effects=True
        ),
        name="layer",
    )(kinds, tokens, *enc_args, *fus, table, pos_index, target, code)


def select_kernel(groups_ref, *refs):
    count = (len(refs) - 2) // 3
    arrays, picked, held = (refs[n * count : (n + 1) * count] for n in range(3))
    into, out_of = refs[-2:]
    rows = picked[0].shape[0]
    side = lax.axis_index("lvl")

    def load(n, row):
        level, pair = row // (rows // 2), row % (rows // 2)
        group = groups_ref[level * rows + side * (rows // 2) + pair]
        return pltpu.make_async_copy(arrays[n].at[group], held[n].at[row], into.at[n, row])

    def store(n, row):
        return pltpu.make_async_copy(held[n].at[row], picked[n].at[row], out_of.at[n, row])

    every = [(n, row) for row in range(rows) for n in range(count)]
    for at in every:
        load(*at).start()
    for at in every:
        load(*at).wait()
        store(*at).start()
    for at in every:
        store(*at).wait()


def select_rows(level_group, arrays):
    count = level_group.shape[0] // 2
    anywhere = pl.BlockSpec(memory_space=pl.ANY)
    return pl.pallas_call(
        select_kernel,
        out_shape=tuple(jax.ShapeDtypeStruct((count,) + a.shape[1:], a.dtype) for a in arrays),
        in_specs=[pl.BlockSpec(memory_space=pltpu.SMEM)] + [anywhere] * len(arrays),
        out_specs=(anywhere,) * len(arrays),
        scratch_shapes=[pltpu.VMEM((count,) + a.shape[1:], a.dtype) for a in arrays]
        + [pltpu.SemaphoreType.DMA((len(arrays), count))] * 2,
        compiler_params=pltpu.CompilerParams(vmem_limit_bytes=VMEM_LIMIT),
        name="select_rows",
    )(level_group, *arrays)


def unpack_kernel(
    groups_ref, enc_ref, fus_ref, fus_extra, table_in,
    gain_ref, shift_ref, qkv_ref, out_ref, up_ref, down_ref, lift_ref,
    fg_ref, fs_ref, fq_ref, fo_ref, fu_ref, fd_ref, table_ref,
):
    width = qkv_ref.shape[1]

    def panel(n):
        return enc_ref[0, n * width : (n + 1) * width].astype(F32)

    half = LANES // 2
    for n in range(4):
        qkv_ref[0, :, n * LANES : (n + 1) * LANES] = panel(n)
    mixed, last = panel(4), panel(5)
    qkv_ref[0, :, 4 * LANES :] = mixed[:, :half]
    out_ref[0] = jnp.concatenate([mixed[:, half:], last], 1)
    for n in range(6):
        up_ref[0, :, n * LANES : (n + 1) * LANES] = panel(6 + n)
        down_ref[0, :, n * LANES : (n + 1) * LANES] = panel(15 + n)
    for n in range(3):
        lift_ref[0, :, n * LANES : (n + 1) * LANES] = panel(12 + n)
    norms = enc_ref[0, 21 * width : 21 * width + EXTRA].astype(F32)
    norms = jnp.concatenate([norms[0:4], norms[4:8]], 1)[:, :width]
    gain_ref[0] = norms[0:2]
    shift_ref[0] = norms[2:4]
    i = pl.program_id(0)
    size = fo_ref.shape[0]

    def joining(dest):
        for n in range(size // LANES):
            dest[:, n * LANES : (n + 1) * LANES] = fus_ref[0, n * size : (n + 1) * size].astype(F32)

    @pl.when(i < 3)
    def _():
        joining(fq_ref)

    @pl.when(i == 3)
    def _():
        joining(fo_ref)

    @pl.when((i >= 4) & (i < 8))
    def _():
        joining(fu_ref)

    @pl.when(i >= 8)
    def _():
        joining(fd_ref)

    heads, types, count = table_ref.shape

    @pl.when(i == 0)
    def _():
        extra = fus_extra[0].astype(F32)
        extra = jnp.concatenate([extra[4 * n : 4 * n + 4] for n in range(size // LANES)], 1)
        fg_ref[...] = extra[0:2]
        fs_ref[...] = extra[2:4]
        each = heads * types
        per = table_in.shape[1] // each
        for n in range(2 * per):
            wide = min(LANES, count - n * LANES)
            if wide > 0:
                at = n % per * each
                block = table_in[n // per, at : at + each].astype(F32).reshape(heads, types, LANES)
                table_ref[:, :, n * LANES : n * LANES + wide] = block[:, :, :wide]


def unpack(level_group, enc, fus, table, width1, width2, table_shape):
    groups = enc.shape[0]
    pairs = groups // 4

    def group_of(i, s):
        return s[i % 2 * (groups // 2) + i // (2 * pairs) * pairs + i // 2 % pairs]

    heads, types, count = table_shape
    table_rows = -(-count // SPAN) * heads * types
    panels = width2 * width2 // LANES
    sizes1 = [(2, width1), (2, width1), (width1, 3 * width1), (width1, width1), (width1, 4 * width1), (width1, 4 * width1), (width1, 2 * width1)]
    sizes2 = [(2, width2), (2, width2), (width2, 3 * width2), (width2, width2), (width2, 4 * width2), (4 * width2, width2)]
    square = (width2, width2)
    return pl.pallas_call(
        unpack_kernel,
        out_shape=tuple(jax.ShapeDtypeStruct((groups,) + s, F32) for s in sizes1)
        + tuple(jax.ShapeDtypeStruct(s, F32) for s in sizes2)
        + (jax.ShapeDtypeStruct(table_shape, F32),),
        grid_spec=pltpu.PrefetchScalarGridSpec(
            num_scalar_prefetch=1,
            grid=(groups,),
            in_specs=[
                pl.BlockSpec((1,) + enc.shape[1:], lambda i, s: (i, 0, 0)),
                pl.BlockSpec((1, panels, LANES), lambda i, s: (i // 6, i % 6, 0)),
                pl.BlockSpec((1, EXTRA, LANES), lambda i, s: (0, 6 * panels // EXTRA, 0)),
                pl.BlockSpec((2, table_rows, LANES), lambda i, s: (0, 0, 0)),
            ],
            out_specs=tuple(pl.BlockSpec((1,) + s, lambda i, s: (group_of(i, s), 0, 0)) for s in sizes1)
            + (
                pl.BlockSpec((2, width2), lambda i, s: (0, 0)),
                pl.BlockSpec((2, width2), lambda i, s: (0, 0)),
                pl.BlockSpec(square, lambda i, s: (0, jnp.minimum(i, 2))),
                pl.BlockSpec(square, lambda i, s: (0, 0)),
                pl.BlockSpec(square, lambda i, s: (0, jnp.clip(i - 4, 0, 3))),
                pl.BlockSpec(square, lambda i, s: (jnp.clip(i - 8, 0, 3), 0)),
                pl.BlockSpec(table_shape, lambda i, s: (0, 0, 0)),
            ),
        ),
        compiler_params=pltpu.CompilerParams(vmem_limit_bytes=VMEM_LIMIT),
        name="unpack",
    )(level_group, enc, fus, fus, table)


def shards(
    tokens_in,
    enc_gains,
    enc_shifts,
    enc_qkv,
    enc_out,
    enc_up,
    enc_down,
    enc_lift,
    fus_gains,
    fus_shifts,
    fus_qkv,
    fus_out,
    fus_up,
    fus_down,
    fus_table,
    target,
    loss_code,
    level_group,
    window_type,
    pos_index,
):
    enc = select_rows(
        level_group, (enc_gains, enc_shifts, enc_qkv, enc_out, enc_up, jnp.swapaxes(enc_down, 1, 2), enc_lift)
    )
    output, x_grad, enc_sums, fus_sums, table_sums = layer(
        window_type.T,
        tokens_in,
        enc,
        (fus_gains, fus_shifts, fus_qkv, fus_out, fus_up, fus_down),
        fus_table,
        pos_index,
        target,
        jnp.swapaxes(loss_code, 0, 1),
    )
    grads = unpack(
        level_group,
        enc_sums.reshape(level_group.shape[0], ROWS1, LANES),
        fus_sums,
        table_sums,
        enc_out.shape[1],
        fus_out.shape[0],
        fus_table.shape,
    )
    return (output, x_grad, *grads[:5], jnp.swapaxes(grads[5], 1, 2), *grads[6:])


def solution(mesh):
    copied = P()
    in_specs = (
        (P("lvl", None, "win", None),)
        + (copied,) * 14
        + (P(None, "lvl", "win", None), P(None, "lvl", "win"), copied, P("lvl", "win"), copied)
    )
    out_specs = (P(None, "lvl", "win", None), P("lvl", None, "win", None)) + (copied,) * 14
    return jax.shard_map(shards, mesh=mesh, in_specs=in_specs, out_specs=out_specs, check_vma=False)
```

```python
import functools

import jax
import jax.numpy as jnp
from jax import lax
from jax.experimental import pallas as pl
from jax.experimental.pallas import tpu as pltpu
from jax.sharding import PartitionSpec as P

HEADS1 = 6
HEADS2 = 12
HEAD = 32
EPS = 1e-05
LANES = 128
SPAN = 256
PER = 4
UNROLL = 6
ROWS1 = 4096
CHUNKS1 = (48, 48, 32)
CHUNKS2 = (32, 32, 48)
CHUNKS3 = (16, 16, 16)
EXTRA = 16
VMEM_LIMIT = 60 * 1024 * 1024

BF = jnp.bfloat16
F32 = jnp.float32


def nn(a, b):
    return lax.dot_general(a, b, (((1,), (0,)), ((), ())), preferred_element_type=F32)


def nt(a, b):
    return lax.dot_general(a, b, (((1,), (1,)), ((), ())), preferred_element_type=F32)


def tn(a, b):
    return lax.dot_general(a, b, (((0,), (0,)), ((), ())), preferred_element_type=F32)


RING = 4
STRIDES = (16, 4, 1)
ORDERS = ((0, 1, 2), (1, 2, 0), (2, 0, 1))
MESH = pl.DeviceIdType.MESH
MESSAGES = 22


def coordinate(axis):
    return lax.rem(lax.axis_index("win") // STRIDES[axis], RING)


def along(axis, hops):
    place = lax.axis_index("win")
    mine = coordinate(axis)
    other = lax.rem(mine + hops, RING)
    return (lax.axis_index("lvl"), place + (other - mine) * STRIDES[axis])


def partner():
    return (1 - lax.axis_index("lvl"), lax.axis_index("win"))


def add_rows(dest, at, rows, others):
    step = max(s for s in (128, 112, 96, 64, 48, 32, 16) if rows % s == 0)

    @pl.loop(0, rows // step)
    def _(i):
        here = pl.ds(pl.multiple_of(at + i * step, 16), step)
        total = dest[here, :].astype(F32)
        for ref, start in others:
            total += ref[pl.ds(pl.multiple_of(start + i * step, 16), step), :].astype(F32)
        dest[here, :] = total.astype(BF)


def rows_of(ref, at, size):
    return ref.at[pl.ds(pl.multiple_of(at, 16), size)]


class Place:
    def __init__(self):
        self.here = [coordinate(axis) for axis in range(3)]
        self.chips = {(axis, hops): along(axis, hops) for axis in range(3) for hops in (1, 2, 3)}
        self.partner = partner()


class Part:
    def __init__(self, place, own, out, box, send, recv, keep, base, chunk, order, ring):
        self.own, self.out, self.box, self.send, self.recv, self.keep = own, out, box, send, recv, keep
        self.place, self.axes, self.ring = place, order, ring
        self.here = [place.here[a] for a in order]
        self.big, self.mid, self.chunk = 16 * chunk, 4 * chunk, chunk
        self.base = base
        self.first = base + self.here[0] * self.big
        self.second = self.first + self.here[1] * self.mid
        self.third = self.second + self.here[2] * chunk

    def top(self, hops):
        return self.base + jnp.bitwise_and(self.here[0] + hops, RING - 1) * self.big

    def message(self, n):
        big, mid, chunk = self.big, self.mid, self.chunk
        half = big // 2
        up, down = (0, 1), (0, RING - 1)
        own, out, box = self.own, self.out, self.box
        after = 3 * big
        if n < 6 and not self.ring:
            hops = (1, 3, 2)[n]
            src, dst, to = rows_of(own, self.top(hops), big), rows_of(box, n * big, big), (0, hops)
        elif n == 0:
            src, dst, to = rows_of(own, self.top(2), half), rows_of(box, 0, half), up
        elif n == 1:
            src, dst, to = rows_of(own, self.top(2) + half, half), rows_of(box, half, half), down
        elif n == 2:
            src, dst, to = rows_of(own, self.top(1) + half, half), rows_of(box, big + half, half), up
        elif n == 3:
            src, dst, to = rows_of(own, self.top(3), half), rows_of(box, 2 * big, half), down
        elif n == 4:
            src, dst, to = rows_of(own, self.top(1), half), rows_of(box, big, half), up
        elif n == 5:
            src, dst, to = rows_of(own, self.top(3) + half, half), rows_of(box, 2 * big + half, half), down
        elif n < 9:
            hops = (1, 3, 2)[n - 6]
            at = self.first + jnp.bitwise_and(self.here[1] + hops, RING - 1) * mid
            src, dst, to = rows_of(own, at, mid), rows_of(box, after + (n - 6) * mid, mid), (1, hops)
        elif n < 12:
            hops = (1, 3, 2)[n - 9]
            at = self.second + jnp.bitwise_and(self.here[2] + hops, RING - 1) * chunk
            src, to = rows_of(own, at, chunk), (2, hops)
            dst = rows_of(box, after + 3 * mid + (n - 9) * chunk, chunk)
        elif n < 15:
            src, dst = rows_of(own, self.third, chunk), rows_of(out, self.third, chunk)
            to = (2, (1, 3, 2)[n - 12])
        elif n < 18:
            src = dst = rows_of(out, self.second, mid)
            to = (1, (1, 3, 2)[n - 15])
        elif not self.ring:
            src = dst = rows_of(out, self.first, big)
            to = (0, (1, 3, 2)[n - 18])
        elif n < 20:
            src = dst = rows_of(out, self.first, big)
            to = (up, down)[n - 18]
        elif n == 20:
            src = dst = rows_of(out, self.top(3), half)
            to = up
        else:
            src = dst = rows_of(out, self.top(1) + half, half)
            to = down
        device = self.place.chips[self.axes[to[0]], to[1]]
        return pltpu.make_async_remote_copy(
            src, dst, self.send.at[n], self.recv.at[n], device_id=device, device_id_type=MESH
        )

    def start(self, *numbers):
        for n in numbers:
            self.message(n).start()

    def wait(self, *numbers):
        for n in numbers:
            self.message(n).wait()

    def kept(self):
        return pltpu.make_async_copy(
            rows_of(self.own, self.third, self.chunk), rows_of(self.out, self.third, self.chunk), self.keep
        )

    def stage(self, k):
        big, mid, chunk, own, box = self.big, self.mid, self.chunk, self.own, self.box
        half, after = big // 2, 3 * big
        if k == 0:
            self.start(*((0, 1, 2, 3) if self.ring else (2, 0, 1)))
        elif k == 1 and self.ring:
            self.wait(0)
            add_rows(own, self.top(1), half, [(box, 0)])
            self.start(4)
            self.wait(1)
            add_rows(own, self.top(3) + half, half, [(box, half)])
            self.start(5)
        elif k == 2:
            if self.ring:
                self.wait(2, 3, 4, 5)
            else:
                self.wait(0, 1, 2)
            add_rows(own, self.first, big, [(box, n * big) for n in ((1, 2) if self.ring else (0, 1, 2))])
            self.start(6, 7, 8)
        elif k == 3:
            self.wait(6, 7, 8)
            add_rows(own, self.second, mid, [(box, after + n * mid) for n in range(3)])
            self.start(9, 10, 11)
        elif k == 4:
            self.wait(9, 10, 11)
            add_rows(own, self.third, chunk, [(box, after + 3 * mid + n * chunk) for n in range(3)])
            self.kept().start()
            self.start(12, 13, 14)
        elif k == 5:
            self.kept().wait()
            self.wait(12, 13, 14)
            self.start(15, 16, 17)
        elif k == 6:
            self.wait(15, 16, 17)
            self.start(*((18, 19) if self.ring else (20, 18, 19)))
        elif k == 7 and self.ring:
            self.wait(18)
            self.start(20)
            self.wait(19)
            self.start(21)
        elif k == 8:
            self.wait(*((20, 21) if self.ring else (18, 19, 20)))


def parts_of(place, chunks, own, out, boxes, sems, ring):
    parts, base = [], 0
    for n, chunk in enumerate(chunks):
        send, recv, keep = (sem.at[n] for sem in sems)
        parts.append(Part(place, own, out, boxes[n], send, recv, keep, base, chunk, ORDERS[n], ring))
        base += 64 * chunk
    return parts


def run(parts, k):
    for part in parts:
        part.stage(k)


def type_picker(kinds, heads, types):
    shape = (heads * types, len(kinds) * heads)
    row = lax.broadcasted_iota(jnp.int32, shape, 0)
    column = lax.broadcasted_iota(jnp.int32, shape, 1)
    kind = jnp.full(shape, kinds[-1], jnp.int32)
    for n in reversed(range(len(kinds) - 1)):
        kind = jnp.where(column < (n + 1) * heads, kinds[n], kind)
    same_head = (row // types) == (column % heads)
    return (same_head & ((row % types) == kind)).astype(F32).astype(BF)


def lay_positions(pos_ref, all_pos):
    keys = pos_ref.shape[0]
    tails = keys - LANES
    all_pos[:keys] = pos_ref[...].astype(F32).T[:, :LANES].astype(jnp.int32)
    all_pos[keys : keys + tails] = pos_ref[LANES:, :LANES]
    all_pos[keys + tails :] = jnp.full((tails, LANES), -1, jnp.int32)
    all_pos[keys + tails :, : keys - LANES] = pos_ref[LANES:, LANES:]


def one_hot_of(pos):
    low = jnp.bitwise_and(pos, SPAN - 1).astype(F32).astype(BF)
    line = lax.broadcasted_iota(jnp.int32, (SPAN, pos.shape[1]), 0).astype(F32).astype(BF)
    return jnp.where(line == low, jnp.ones((), BF), jnp.zeros((), BF))


def spread_table(picker, table_ref, t2):
    rows, count = picker.shape[1], table_ref.shape[1]
    for k in range(t2.shape[0] // rows):
        width = min(SPAN, count - k * SPAN)
        part = table_ref[:, k * SPAN : k * SPAN + width].astype(BF)
        t2[k * rows : (k + 1) * rows, :width] = tn(picker, part).astype(BF)
        if width < SPAN:
            t2[k * rows : (k + 1) * rows, width:] = jnp.zeros((rows, SPAN - width), BF)


def look_up(t2, all_pos, dest, first, last):
    rows = dest.shape[0]
    high = t2.shape[0] // rows

    @pl.loop(first, last, unroll=2)
    def _(i):
        at = pl.multiple_of(i * 8, 8)
        eight = all_pos[pl.ds(at, 8), :]
        for s in range(0, 8, PER):
            pos = jnp.concatenate([eight[s + j : s + j + 1] for j in range(PER)], 1)
            top = jnp.right_shift(pos, 8)
            spread = nn(t2[...], one_hot_of(pos))
            picked = jnp.zeros((rows, PER * LANES), F32)
            for k in range(high):
                picked = jnp.where(top == k, spread[k * rows : (k + 1) * rows], picked)
            for j in range(PER):
                dest[:, pl.ds(at + s + j, 1), :] = picked[:, j * LANES : (j + 1) * LANES].reshape(rows, 1, LANES)


def turn_tails(bias, bias_tail, keys):
    tails = keys - LANES
    per = bias_tail.shape[2] // tails
    for i in range(bias_tail.shape[0]):
        lines = bias[i * per : (i + 1) * per, keys : keys + tails].reshape(per * tails, LANES)
        bias_tail[i, :LANES] = lines.T
        lines = bias[i * per : (i + 1) * per, keys + tails : keys + 2 * tails].reshape(per * tails, LANES)
        bias_tail[i, LANES:] = lines.T[: keys - LANES]


def lay_terms(ds_main, ds_tail, lines):
    rows, keys = ds_main.shape[:2]
    tails = keys - LANES
    per = ds_tail.shape[2] // tails

    @pl.loop(0, ds_tail.shape[0])
    def _(i):
        at = pl.ds(i * per, per)
        lines[at, :keys] = ds_main[at].astype(F32)
        block = ds_tail[i].astype(F32)
        lines[at, keys : keys + tails] = block[:LANES].T.reshape(per, tails, LANES)
        lines[at, keys + tails : keys + 2 * tails] = jnp.zeros((per, tails, LANES), F32)
        lines[at, keys + tails : keys + 2 * tails, : keys - LANES] = block[LANES:].T.reshape(per, tails, keys - LANES)


def add_terms(acc, all_pos, lines, first, last):
    rows = lines.shape[0]
    high = acc.shape[0] // rows

    @pl.loop(first, last, unroll=2)
    def _(i):
        at = pl.multiple_of(i * 8, 8)
        eight = all_pos[pl.ds(at, 8), :]
        total = None
        for s in range(0, 8, PER):
            pos = jnp.concatenate([eight[s + j : s + j + 1] for j in range(PER)], 1)
            terms = jnp.concatenate([lines[:, pl.ds(at + s + j, 1), :].reshape(rows, LANES) for j in range(PER)], 1)
            top = jnp.right_shift(pos, 8)
            parts = jnp.concatenate([jnp.where(top == k, terms, 0.0) for k in range(high)], 0)
            term = nt(parts.astype(BF), one_hot_of(pos))
            total = term if total is None else total + term
        acc[...] += total


def norm(values):
    centred = values - jnp.mean(values, -1, keepdims=True)
    spread = jnp.mean(centred * centred, -1, keepdims=True)
    scale = lax.rsqrt(spread + EPS)
    return centred * scale, scale


def norm_back(grad, gain, unit, scale):
    scaled = grad * gain
    first = jnp.mean(scaled, -1, keepdims=True)
    second = jnp.mean(scaled * unit, -1, keepdims=True)
    return (scaled - first - unit * second) * scale


def gelu_pair(v):
    half = jnp.exp(-0.5 * v * v)
    t = 1.0 / (1.0 + 0.23164189 * jnp.abs(v))
    series = t * (0.127414796 + t * (-0.142248368 + t * (0.7107068705 + t * (-0.7265760135 + t * 0.5307027145))))
    tail = series * half
    phi = jnp.where(v >= 0.0, 1.0 - tail, tail)
    return v * phi, phi + v * half * 0.3989422804014327


def head_masks(width):
    lane = lax.broadcasted_iota(jnp.int32, (1, width), 1)
    return [(lane // HEAD) == h for h in range(width // HEAD)]


def keep(mask, values):
    return jnp.where(mask, values, 0.0)


def put_panels(ref, at, values):
    rows = values.shape[0]
    for j in range(values.shape[1] // LANES):
        ref[at + j * rows : at + (j + 1) * rows] = values[:, j * LANES : (j + 1) * LANES].astype(ref.dtype)


def softmax_rows(scores):
    top = jnp.max(scores, 0, keepdims=True)
    e = jnp.exp(scores - top)
    return e * (1.0 / jnp.sum(e, 0, keepdims=True))


def score_back(prob, grad):
    return prob * (grad - jnp.sum(grad * prob, 0, keepdims=True))


def layer_kernel(
    kinds_ref, tokens_ref,
    e_gain0, e_gain1, e_shift0, e_shift1,
    e_qkv0, e_qkv1, e_out0, e_out1, e_up0, e_up1, e_down0, e_down1, e_lift0, e_lift1,
    f_gain, f_shift, f_qkv_ref, f_out_ref, f_up_ref, f_down_ref,
    table_ref, pos_ref, target_ref, code_ref,
    out_ref, xg_out, e_all, f_all, t_all,
    f_qkv, f_out, f_up, f_down,
    x_s, xg_s, n1_s, q_s, k_s, v_s, p_s, o_s, n2_s, h_s, act_s, gp_s, res_s,
    win_s, fq, fk, fv, fp, fo, fdq, fdk, fdv, fh, fn2, fdy, fgrad,
    t2, all_pos, bias_main, bias_tail, ds_main, ds_tail, acc_t,
    acc, acc_norm, own_e, own_f, give_f, peer_f, own_t, give_t, peer_t,
    be0, be1, be2, bf0, bf1, bf2, bt0, bt1, bt2,
    se, re, ke, sf, rf, kf, st, rt, kt, misc_send, misc_recv, misc_near,
):
    boxes_e, boxes_f, boxes_t = (be0, be1, be2), (bf0, bf1, bf2), (bt0, bt1, bt2)
    sems_e, sems_f, sems_t = (se, re, ke), (sf, rf, kf), (st, rt, kt)
    step = pl.program_id(0)
    side = lax.axis_index("lvl")
    rows = x_s.shape[2]
    width1 = x_s.shape[3]
    width2 = f_qkv.shape[0]
    half = rows // 2
    keys = rows
    root = HEAD ** (-0.5)
    masks1 = head_masks(width1)
    masks2 = head_masks(LANES)
    picks2 = [m.astype(F32).astype(BF) for m in masks2]
    gains1, shifts1 = (e_gain0, e_gain1), (e_shift0, e_shift1)
    w_qkv, w_out, w_up = (e_qkv0, e_qkv1), (e_out0, e_out1), (e_up0, e_up1)
    w_down, w_lift = (e_down0, e_down1), (e_lift0, e_lift1)

    pairs = x_s.shape[1]
    heads_all = width2 // HEAD
    types = table_ref.shape[0] // heads_all
    terms_each = 2 * heads_all
    panels = 12 * width2 // LANES
    halves = panels // 2 * width2

    place = Place()

    def encoder(q, ring=False):
        return parts_of(
            place, CHUNKS1, own_e.at[q], e_all.at[side, q], [b.at[q] for b in boxes_e], [s.at[q] for s in sems_e], ring
        )

    def joining():
        return parts_of(place, CHUNKS2, own_f, f_all.at[side], boxes_f, sems_f, True)

    def table():
        return parts_of(place, CHUNKS3, own_t, t_all.at[side], boxes_t, sems_t, False)

    def hand_over(ref, n):
        return remote(ref.at[side], ref.at[side], 3 + pairs + n)

    def hand_encoder(q):
        return remote(e_all.at[side, q], e_all.at[side, q], 5 + pairs + q)

    def hand_quarters(parts, first, quarters, what):
        for k, part in enumerate(parts):
            for hops in quarters:
                rows = rows_of(part.out, part.top(hops), part.big)
                getattr(remote(rows, rows, first + 4 * k + hops), what)()

    def hand_last(quarters, what):
        hand_quarters(encoder(2, ring=True), 4 + 2 * pairs, quarters, what)

    def hand_joining(quarters, what):
        hand_quarters(joining(), 16 + 2 * pairs, quarters, what)

    def tick(new=None, old=None):
        if new is not None:

            @pl.when(step >= 1)
            def _():
                run(encoder(step - 1), new)

        if old is not None:

            @pl.when(step == 2)
            def _():
                if old < 9:
                    run(encoder(0), old)
                if old == 8:
                    hand_encoder(0).start()

    def remote(src, dst, n):
        return pltpu.make_async_remote_copy(
            src, dst, misc_send.at[n], misc_recv.at[n], device_id=place.partner, device_id_type=MESH
        )

    def near(src, dst, n):
        return pltpu.make_async_copy(src, dst, misc_near.at[n])

    def tokens():
        given = remote(tokens_ref.at[0, pl.ds((1 - side) * pairs, pairs)], x_s.at[side], 0)
        taken = near(tokens_ref.at[0, pl.ds(side * pairs, pairs)], x_s.at[side], 0)
        return given, taken

    def joining_weights():
        pairs_of = ((f_qkv_ref, f_qkv), (f_out_ref, f_out), (f_up_ref, f_up), (f_down_ref, f_down))
        return tuple(near(src, dst, 1 + pairs + n) for n, (src, dst) in enumerate(pairs_of))

    def tokens_grad(q):
        given = remote(xg_s.at[1 - side, q], xg_out.at[0, side * pairs + q], 1 + q)
        taken = near(xg_s.at[side, q], xg_out.at[0, side * pairs + q], 1 + q)
        return given, taken

    def joining_half():
        return remote(give_f, peer_f, 1 + pairs)

    def table_half():
        return remote(give_t.at[1 - side], peer_t, 2 + pairs)

    @pl.when(step == 0)
    def _():
        barrier = pltpu.get_barrier_semaphore()
        friends = list(place.chips.values()) + [place.partner]
        for device in friends:
            pl.semaphore_signal(barrier, inc=1, device_id=device, device_id_type=MESH)
        pl.semaphore_wait(barrier, len(friends))
        for copy in tokens() + joining_weights():
            copy.start()
        lay_positions(pos_ref, all_pos)
        for q in range(pairs):
            picker = type_picker([kinds_ref[w, q] for w in range(2)], heads_all, types)
            spread_table(picker, table_ref, t2.at[q])
        acc[...] = jnp.zeros_like(acc)
        acc_norm[...] = jnp.zeros_like(acc_norm)

    eights = (keys + 2 * (keys - LANES)) // 8
    look_up(t2.at[step], all_pos, bias_main, 0, eights)
    turn_tails(bias_main, bias_tail, keys)
    tick(new=2, old=8)

    @pl.when(step == 0)
    def _():
        for copy in tokens():
            copy.wait()

    def stack1(values):
        return jnp.concatenate([keep(m, values) for m in masks1], 0).astype(BF)

    def fold1(stacked):
        total = keep(masks1[0], stacked[:half])
        for h in range(1, HEADS1):
            total += keep(masks1[h], stacked[h * half : (h + 1) * half])
        return total

    both = range(2)
    windows = [(l, w, slice(w * half, (w + 1) * half)) for l in both for w in both]
    xs = [x_s[l, step].astype(F32) for l in both]
    for l in both:
        z1, _ = norm(xs[l])
        n1_s[l] = (z1 * gains1[l][0, 0:1] + shifts1[l][0, 0:1]).astype(BF)
    for l in both:
        qkv = nn(n1_s[l], w_qkv[l][0])
        q_s[l] = qkv[:, :width1].astype(BF).astype(F32)
        k_s[l] = qkv[:, width1 : 2 * width1].astype(BF).astype(F32)
        v_s[l] = qkv[:, 2 * width1 :].astype(BF).astype(F32)
    for l, w, part in windows:
        p_s[l, w] = softmax_rows(nt(k_s[l, part].astype(BF), stack1(q_s[l, part])) * root)
    for l, w, part in windows:
        o_s[l, part] = fold1(tn(p_s[l, w].astype(BF), v_s[l, part].astype(BF)))
    for l in both:
        h = x_s[l, step].astype(F32) + nn(o_s[l].astype(BF), w_out[l][0])
        h_s[l] = h
        z2, _ = norm(h)
        n2_s[l] = (z2 * gains1[l][0, 1:2] + shifts1[l][0, 1:2]).astype(BF)
    for l in both:
        act, slope = gelu_pair(nn(n2_s[l], w_up[l][0]))
        act_s[l] = act.astype(BF)
        gp_s[l] = slope
    for l in both:
        res_s[l] = (h_s[l] + nt(act_s[l], w_down[l][0])).astype(BF)
    for l in both:
        lifted = nn(res_s[l], w_lift[l][0]).astype(BF).astype(F32)
        for w in range(2):
            win_s[w * rows + l * half : w * rows + (l + 1) * half] = lifted[w * half : (w + 1) * half]

    eye = lax.broadcasted_iota(jnp.int32, (rows, rows), 0) == lax.broadcasted_iota(jnp.int32, (rows, rows), 1)
    for l in range(2):
        codes = code_ref[:, l].astype(F32)
        chosen = lax.broadcasted_iota(jnp.int32, codes.shape, 0) == step
        weight = 0.5 * jnp.exp(0.35 * jnp.sum(jnp.where(chosen, codes, 0.0), 0, keepdims=True))
        column = jnp.sum(jnp.where(eye, weight, 0.0), 1, keepdims=True)
        direction = column * target_ref[l, 0].astype(F32)
        for w in range(2):
            fdy[w * rows + l * half : w * rows + (l + 1) * half] = direction[w * half : (w + 1) * half]

    @pl.when(step == 0)
    def _():
        for copy in joining_weights():
            copy.wait()

    lane_groups = width2 // LANES
    z1, _ = norm(win_s[...])
    fn1 = (z1 * f_gain[0:1] + f_shift[0:1]).astype(BF)
    for t, dest in enumerate((fq, fk, fv)):
        part = nn(fn1, f_qkv[:, t * width2 : (t + 1) * width2]).astype(BF)
        for w in range(2):
            for g in range(lane_groups):
                dest[w * lane_groups + g] = part[w * rows : (w + 1) * rows, g * LANES : (g + 1) * LANES]
    tails = rows - LANES
    tick(new=3)

    heads = LANES // HEAD
    lanes = heads * LANES + heads * tails
    spans = [slice(j * LANES, min((j + 1) * LANES, lanes)) for j in range(heads + 1)]

    def stack2(values):
        main, tail = values[:LANES], values[LANES:]
        return jnp.concatenate([main * m for m in picks2] + [tail * m for m in picks2], 0)

    def fold2(stacked):
        main = keep(masks2[0], stacked[:LANES])
        tail = keep(masks2[0], stacked[heads * LANES : heads * LANES + tails])
        for h in range(1, heads):
            main += keep(masks2[h], stacked[h * LANES : (h + 1) * LANES])
            tail += keep(masks2[h], stacked[heads * LANES + h * tails : heads * LANES + (h + 1) * tails])
        return jnp.concatenate([main, tail], 0)

    @pl.loop(0, 2 * lane_groups, unroll=UNROLL)
    def _(i):
        scores = nt(fk[i], stack2(fq[i]))
        probs = []
        for j, span in enumerate(spans):
            bias = bias_main[i * heads + j, :keys] if j < heads else bias_tail[i]
            prob = softmax_rows(scores[:, span] * root + bias)
            fp[i, :, span] = prob
            probs.append(prob.astype(BF))
        fo[i] = fold2(tn(jnp.concatenate(probs, 1), fv[i])).astype(BF)


    def joined(ref):
        return jnp.concatenate(
            [jnp.concatenate([ref[w * lane_groups + g] for g in range(lane_groups)], 1) for w in range(2)], 0
        )

    hidden = win_s[...] + nn(joined(fo), f_out[...])
    fh[...] = hidden
    z2, _ = norm(hidden)
    fn2[...] = (z2 * f_gain[1:2] + f_shift[1:2]).astype(BF)

    def add_panels(n, values):
        for j in range(values.shape[1] // LANES):
            panel = values[:, j * LANES : (j + 1) * LANES]
            acc[2 * (n + j) : 2 * (n + j) + 2] += panel.reshape(2, width2 // 2, LANES)

    blocks = f_up.shape[1] // width2
    fgrad[...] = jnp.zeros_like(fgrad)

    per_block = width2 // LANES
    wide = 2 * width2
    for j in range(blocks // 2):
        up = f_up[:, j * wide : (j + 1) * wide]
        down = f_down[j * wide : (j + 1) * wide, :]
        n2 = fn2[...]
        low = fdy[...].astype(BF)
        act, slope = gelu_pair(nn(n2, up))
        act = act.astype(BF)
        fh[...] += nn(act, down)
        inner_grad = (nt(low, down) * slope).astype(BF)
        down_grad = tn(act, low)
        add_panels((8 + 2 * j) * per_block, down_grad[:width2])
        add_panels((9 + 2 * j) * per_block, down_grad[width2:])
        add_panels((4 + 2 * j) * per_block, tn(n2, inner_grad))
        fgrad[...] += nt(inner_grad, up)
        if j == 0:
            tick(new=4)

    for l in range(2):
        for w in range(2):
            out_ref[l, 0, w * half : (w + 1) * half] = fh[w * rows + l * half : w * rows + (l + 1) * half].astype(BF)

    hidden = win_s[...] + nn(joined(fo), f_out[...])
    z2, r2 = norm(hidden)
    grad = fgrad[...]
    acc_norm[1:2] += jnp.sum(grad * z2, 0, keepdims=True)
    acc_norm[3:4] += jnp.sum(grad, 0, keepdims=True)
    hidden_grad = fdy[...] + norm_back(grad, f_gain[1:2], z2, r2)
    fgrad[...] = hidden_grad
    low = hidden_grad.astype(BF)
    add_panels(3 * per_block, tn(joined(fo), low))
    att_grad = nt(low, f_out[...]).astype(BF)
    tick(new=5)
    for w in range(2):
        for g in range(lane_groups):
            fo[w * lane_groups + g] = att_grad[w * rows : (w + 1) * rows, g * LANES : (g + 1) * LANES]

    @pl.loop(0, 2 * lane_groups, unroll=UNROLL)
    def _(i):
        queries = stack2(fq[i])
        grads = stack2(fo[i])
        prob_grads = nt(fv[i], grads)
        probs, terms = [], []
        for j, span in enumerate(spans):
            prob = fp[i, :, span]
            probs.append(prob.astype(BF))
            ds = score_back(prob, prob_grads[:, span]).astype(BF)
            terms.append(ds)
            if j < heads:
                ds_main[i * heads + j] = ds
            else:
                ds_tail[i] = ds
        probs, terms = jnp.concatenate(probs, 1), jnp.concatenate(terms, 1)
        fdv[i] = nn(probs, grads).astype(BF)
        fdk[i] = (nn(terms, queries) * root).astype(BF)
        fdq[i] = (fold2(tn(terms, fk[i])) * root).astype(BF)

    z1, r1 = norm(win_s[...])
    n1 = (z1 * f_gain[0:1] + f_shift[0:1]).astype(BF)
    first = jnp.zeros((2 * rows, width2), F32)
    for t, src in enumerate((fdq, fdk, fdv)):
        part = joined(src)
        add_panels(t * per_block, tn(n1, part))
        first += nt(part, f_qkv[:, t * width2 : (t + 1) * width2])
    acc_norm[0:1] += jnp.sum(first * z1, 0, keepdims=True)
    acc_norm[2:3] += jnp.sum(first, 0, keepdims=True)
    fgrad[...] += norm_back(first, f_gain[0:1], z1, r1)

    tick(new=6)

    @pl.when(step == 2)
    def _():
        for owner, dest in ((side, own_f), (1 - side, give_f)):

            @pl.loop(0, panels // 2)
            def _(n):
                panel = acc[pl.ds(2 * (owner * (panels // 2) + n), 2)].reshape(width2, LANES)
                dest[pl.ds(pl.multiple_of(n * width2, 16), width2), :] = panel.astype(BF)

            norms = acc_norm[...]
            norms = jnp.concatenate(
                [norms[:, g * LANES : (g + 1) * LANES] for g in range(lane_groups)]
                + [jnp.zeros((EXTRA - 4 * lane_groups, LANES), F32)],
                0,
            )
            dest[halves : halves + EXTRA] = norms.astype(BF)
        own_f[halves + EXTRA :] = jnp.zeros((own_f.shape[0] - halves - EXTRA, LANES), BF)
        joining_half().start()

    packs = [own_e.at[step, l * ROWS1 : (l + 1) * ROWS1] for l in both]
    lift_grads = [
        jnp.concatenate([fgrad[w * rows + l * half : w * rows + (l + 1) * half] for w in both], 0).astype(BF)
        for l in both
    ]
    d_outs = [nt(lift_grads[l], w_lift[l][0]) for l in both]
    for l in both:
        put_panels(packs[l], 12 * width1, tn(res_s[l], lift_grads[l]))
    norm_grads = [[None] * 4 for _ in both]
    hidden_grads, att_grads, mixed, first_grads = [None] * 2, [None] * 2, [None] * 2, [None] * 2
    inner_grads = [(nn(d_outs[l].astype(BF), w_down[l][0]) * gp_s[l]).astype(BF) for l in both]
    for l in both:
        put_panels(packs[l], 15 * width1, tn(d_outs[l].astype(BF), act_s[l]))
        put_panels(packs[l], 6 * width1, tn(n2_s[l], inner_grads[l]))
    for l in both:
        grad = nt(inner_grads[l], w_up[l][0])
        z2, r2 = norm(h_s[l])
        norm_grads[l][1] = jnp.sum(grad * z2, 0, keepdims=True)
        norm_grads[l][3] = jnp.sum(grad, 0, keepdims=True)
        hidden_grads[l] = d_outs[l] + norm_back(grad, gains1[l][0, 1:2], z2, r2)
    for l in both:
        att_grads[l] = nt(hidden_grads[l].astype(BF), w_out[l][0]).astype(BF).astype(F32)
    out_grads = [tn(o_s[l].astype(BF), hidden_grads[l].astype(BF)) for l in both]
    for l in both:
        h_s[l] = hidden_grads[l]

    @pl.when(step == 2)
    def _():
        joining_half().wait()
        add_rows(own_f, 0, halves + EXTRA, [(peer_f, 0)])
        run(joining(), 0)

    grads = [stack1(att_grads[l][part]) for l, w, part in windows]
    terms = [
        score_back(p_s[l, w], nt(v_s[l, part].astype(BF), grads[n])).astype(BF)
        for n, (l, w, part) in enumerate(windows)
    ]
    dvs = [nn(p_s[l, w].astype(BF), grads[n]) for n, (l, w, part) in enumerate(windows)]
    dks = [nn(terms[n], stack1(q_s[l, part])) * root for n, (l, w, part) in enumerate(windows)]
    dqs = [fold1(tn(terms[n], k_s[l, part].astype(BF))) * root for n, (l, w, part) in enumerate(windows)]
    for l in both:
        mixed[l] = jnp.concatenate(
            [jnp.concatenate([dqs[n], dks[n], dvs[n]], 1) for n in (2 * l, 2 * l + 1)], 0
        ).astype(BF)
    for l in both:
        put_panels(packs[l], 0, jnp.concatenate([tn(n1_s[l], mixed[l]), out_grads[l]], 1))
    for l in both:
        first = nt(mixed[l], w_qkv[l][0])
        z1, r1 = norm(x_s[l, step].astype(F32))
        norm_grads[l][0] = jnp.sum(first * z1, 0, keepdims=True)
        norm_grads[l][2] = jnp.sum(first, 0, keepdims=True)
        norms = jnp.pad(jnp.concatenate(norm_grads[l], 0), ((0, 4), (0, 2 * LANES - width1)))
        norms = jnp.concatenate([norms[:4, :LANES], norms[:4, LANES:], jnp.zeros((8, LANES), F32)], 0)
        packs[l][21 * width1 : 21 * width1 + EXTRA] = norms.astype(BF)
        packs[l][21 * width1 + EXTRA :] = jnp.zeros((ROWS1 - 21 * width1 - EXTRA, LANES), BF)
        xg_s[l, step] = h_s[l] + norm_back(first, gains1[l][0, 0:1], z1, r1)
    for copy in tokens_grad(step):
        copy.start()

    @pl.when(step < 2)
    def _():
        run(encoder(step), 0)

    last = encoder(2, ring=True)

    @pl.when(step == 2)
    def _():
        run(last, 0)

    lay_terms(ds_main, ds_tail, bias_main)
    acc_t[step] = jnp.zeros(acc_t.shape[1:], F32)
    add_terms(acc_t.at[step], all_pos, bias_main, 0, eights // 2)

    @pl.when(step == 2)
    def _():
        run(last, 1)
        run(joining(), 1)

    add_terms(acc_t.at[step], all_pos, bias_main, eights // 2, eights)

    @pl.when(step == 2)
    def _():
        kinds = [kinds_ref[n % 2, n // 2] for n in range(2 * pairs)]
        picker = type_picker(kinds, heads_all, types)
        many = heads_all * types
        high = acc_t.shape[1] // terms_each
        for k in range(high):
            part = jnp.concatenate([acc_t[q, k * terms_each : (k + 1) * terms_each] for q in range(pairs)], 0)
            part = nn(picker, part.astype(BF)).astype(BF)
            for j in range(SPAN // LANES):
                n = k * (SPAN // LANES) + j
                at = n % high * many
                give_t[n // high, at : at + many] = part[:, j * LANES : (j + 1) * LANES]
        table_half().start()
        table_rows = high * many
        own_t[table_rows:] = jnp.zeros((own_t.shape[0] - table_rows, LANES), BF)
        for copy in [near(give_t.at[side], own_t.at[:table_rows], 0)]:
            copy.start()
            copy.wait()
        run(last, 2)
        run(joining(), 2)
        table_half().wait()
        add_rows(own_t, 0, table_rows, [(peer_t, 0)])
        run(table(), 0)
        run(last, 3)
        run(joining(), 3)
        run(encoder(1), 8)
        hand_encoder(1).start()
        run(table(), 2)
        run(last, 4)
        run(joining(), 4)
        run(table(), 3)
        run(last, 5)
        run(table(), 4)
        run(joining(), 5)
        run(last, 6)
        hand_last((0,), "start")
        run(table(), 5)
        run(joining(), 6)
        hand_joining((0,), "start")
        run(table(), 6)
        run(last, 7)
        hand_last((3, 1), "start")
        run(joining(), 7)
        hand_joining((3, 1), "start")
        run(table(), 8)
        hand_over(t_all, 1).start()
        run(last, 8)
        hand_last((2,), "start")
        run(joining(), 8)
        hand_joining((2,), "start")
        hand_last((0, 3, 1, 2), "wait")
        hand_joining((0, 3, 1, 2), "wait")
        for q in range(pairs - 1):
            hand_encoder(q).wait()
        for q in range(pairs):
            for copy in tokens_grad(q):
                copy.wait()
        hand_over(t_all, 1).wait()


def layer(kinds, tokens, enc, fus, table, pos_index, target, code):
    pairs, rows, width2 = target.shape[1:]
    width1 = tokens.shape[3]
    ff1 = enc[4].shape[2]
    keys = rows
    tails = rows - LANES
    half = rows // 2
    heads, types, count = table.shape
    high = -(-count // SPAN)
    groups = 2 * width2 // LANES
    per = LANES // HEAD
    lanes = per * (LANES + tails)
    panels = 12 * width2 // LANES
    halves = panels // 2 * width2 + EXTRA
    table_rows = high * heads * types
    total1, total2, total3 = (64 * sum(c) for c in (CHUNKS1, CHUNKS2, CHUNKS3))

    def by_row(array, level):
        return pl.BlockSpec((1,) + array.shape[1:], lambda q, level=level: (level * pairs + q, 0, 0))

    def whole(array):
        return pl.BlockSpec(array.shape, lambda q: (0,) * array.ndim, pipeline_mode=pl.Buffered(1))

    anywhere = pl.BlockSpec(memory_space=pl.ANY)
    table = table.reshape(heads * types, count)
    enc_args, enc_specs = [], []
    for array in enc:
        for level in range(2):
            enc_args.append(array)
            enc_specs.append(by_row(array, level))
    moving = pl.BlockSpec((2, 1, rows, width2), lambda q: (0, q, 0, 0))
    dma = pltpu.SemaphoreType.DMA
    vmem = pltpu.VMEM
    return pl.pallas_call(
        layer_kernel,
        grid=(pairs,),
        out_shape=(
            jax.ShapeDtypeStruct((2, pairs, rows, width2), BF),
            jax.ShapeDtypeStruct((1, 2 * pairs, rows, width1), F32),
            jax.ShapeDtypeStruct((2, pairs, total1, LANES), BF),
            jax.ShapeDtypeStruct((2, total2, LANES), BF),
            jax.ShapeDtypeStruct((2, total3, LANES), BF),
        ),
        in_specs=[pl.BlockSpec(memory_space=pltpu.SMEM), anywhere]
        + enc_specs
        + [whole(a) for a in fus[:2]]
        + [anywhere] * 4
        + [whole(table), whole(pos_index), moving, whole(code)],
        out_specs=(moving, anywhere, anywhere, anywhere, anywhere),
        scratch_shapes=[vmem(a.shape, a.dtype) for a in fus[2:]]
        + [
            vmem((2, pairs, rows, width1), BF),
            vmem((2, pairs, rows, width1), F32),
            vmem((2, rows, width1), BF),
            vmem((2, rows, width1), F32),
            vmem((2, rows, width1), F32),
            vmem((2, rows, width1), F32),
            vmem((2, 2, half, HEADS1 * half), F32),
            vmem((2, rows, width1), F32),
            vmem((2, rows, width1), BF),
            vmem((2, rows, width1), F32),
            vmem((2, rows, ff1), BF),
            vmem((2, rows, ff1), F32),
            vmem((2, rows, width1), BF),
            vmem((2 * rows, width2), F32),
            vmem((groups, rows, LANES), BF),
            vmem((groups, rows, LANES), BF),
            vmem((groups, rows, LANES), BF),
            vmem((groups, rows, lanes), F32),
            vmem((groups, rows, LANES), BF),
            vmem((groups, rows, LANES), BF),
            vmem((groups, rows, LANES), BF),
            vmem((groups, rows, LANES), BF),
            vmem((2 * rows, width2), F32),
            vmem((2 * rows, width2), BF),
            vmem((2 * rows, width2), F32),
            vmem((2 * rows, width2), F32),
            vmem((pairs, high * 2 * heads, SPAN), BF),
            vmem((keys + 2 * tails, LANES), jnp.int32),
            vmem((2 * heads, keys + 2 * tails, LANES), F32),
            vmem((groups, keys, per * tails), F32),
            vmem((2 * heads, keys, LANES), BF),
            vmem((groups, keys, per * tails), BF),
            vmem((pairs, high * 2 * heads, SPAN), F32),
            vmem((2 * panels, width2 // 2, LANES), F32),
            vmem((4, width2), F32),
            vmem((pairs, total1, LANES), BF),
            vmem((total2, LANES), BF),
            vmem((halves, LANES), BF),
            vmem((halves, LANES), BF),
            vmem((total3, LANES), BF),
            vmem((2, table_rows, LANES), BF),
            vmem((table_rows, LANES), BF),
        ]
        + [vmem((pairs, 63 * chunk, LANES), BF) for chunk in CHUNKS1]
        + [vmem((63 * chunk, LANES), BF) for chunk in CHUNKS2 + CHUNKS3]
        + [dma((pairs, 3, MESSAGES)), dma((pairs, 3, MESSAGES)), dma((pairs, 3))]
        + [dma((3, MESSAGES)), dma((3, MESSAGES)), dma((3,))] * 2
        + [dma((28 + 2 * pairs,)), dma((28 + 2 * pairs,)), dma((5 + pairs,))],
        compiler_params=pltpu.CompilerParams(
            vmem_limit_bytes=VMEM_LIMIT + 2 * 1024 * 1024, collective_id=0, has_side_effects=True
        ),
        name="layer",
    )(kinds, tokens, *enc_args, *fus, table, pos_index, target, code)


def select_kernel(groups_ref, *refs):
    count = (len(refs) - 2) // 3
    arrays, picked, held = (refs[n * count : (n + 1) * count] for n in range(3))
    into, out_of = refs[-2:]
    rows = picked[0].shape[0]
    side = lax.axis_index("lvl")

    def load(n, row):
        level, pair = row // (rows // 2), row % (rows // 2)
        group = groups_ref[level * rows + side * (rows // 2) + pair]
        return pltpu.make_async_copy(arrays[n].at[group], held[n].at[row], into.at[n, row])

    def store(n, row):
        return pltpu.make_async_copy(held[n].at[row], picked[n].at[row], out_of.at[n, row])

    every = [(n, row) for row in range(rows) for n in range(count)]
    for at in every:
        load(*at).start()
    for at in every:
        load(*at).wait()
        store(*at).start()
    for at in every:
        store(*at).wait()


def select_rows(level_group, arrays):
    count = level_group.shape[0] // 2
    anywhere = pl.BlockSpec(memory_space=pl.ANY)
    return pl.pallas_call(
        select_kernel,
        out_shape=tuple(jax.ShapeDtypeStruct((count,) + a.shape[1:], a.dtype) for a in arrays),
        in_specs=[pl.BlockSpec(memory_space=pltpu.SMEM)] + [anywhere] * len(arrays),
        out_specs=(anywhere,) * len(arrays),
        scratch_shapes=[pltpu.VMEM((count,) + a.shape[1:], a.dtype) for a in arrays]
        + [pltpu.SemaphoreType.DMA((len(arrays), count))] * 2,
        compiler_params=pltpu.CompilerParams(vmem_limit_bytes=VMEM_LIMIT),
        name="select_rows",
    )(level_group, *arrays)


def unpack_kernel(
    groups_ref, enc_ref, fus_ref, fus_extra, table_in,
    gain_ref, shift_ref, qkv_ref, out_ref, up_ref, down_ref, lift_ref,
    fg_ref, fs_ref, fq_ref, fo_ref, fu_ref, fd_ref, table_ref,
):
    width = qkv_ref.shape[1]

    def panel(n):
        return enc_ref[0, n * width : (n + 1) * width].astype(F32)

    half = LANES // 2
    for n in range(4):
        qkv_ref[0, :, n * LANES : (n + 1) * LANES] = panel(n)
    mixed, last = panel(4), panel(5)
    qkv_ref[0, :, 4 * LANES :] = mixed[:, :half]
    out_ref[0] = jnp.concatenate([mixed[:, half:], last], 1)
    for n in range(6):
        up_ref[0, :, n * LANES : (n + 1) * LANES] = panel(6 + n)
        down_ref[0, :, n * LANES : (n + 1) * LANES] = panel(15 + n)
    for n in range(3):
        lift_ref[0, :, n * LANES : (n + 1) * LANES] = panel(12 + n)
    norms = enc_ref[0, 21 * width : 21 * width + EXTRA].astype(F32)
    norms = jnp.concatenate([norms[0:4], norms[4:8]], 1)[:, :width]
    gain_ref[0] = norms[0:2]
    shift_ref[0] = norms[2:4]
    i = pl.program_id(0)
    size = fo_ref.shape[0]

    def joining(dest):
        for n in range(size // LANES):
            dest[:, n * LANES : (n + 1) * LANES] = fus_ref[0, n * size : (n + 1) * size].astype(F32)

    @pl.when(i < 3)
    def _():
        joining(fq_ref)

    @pl.when(i == 3)
    def _():
        joining(fo_ref)

    @pl.when((i >= 4) & (i < 8))
    def _():
        joining(fu_ref)

    @pl.when(i >= 8)
    def _():
        joining(fd_ref)

    heads, types, count = table_ref.shape

    @pl.when(i == 0)
    def _():
        extra = fus_extra[0].astype(F32)
        extra = jnp.concatenate([extra[4 * n : 4 * n + 4] for n in range(size // LANES)], 1)
        fg_ref[...] = extra[0:2]
        fs_ref[...] = extra[2:4]
        each = heads * types
        per = table_in.shape[1] // each
        for n in range(2 * per):
            wide = min(LANES, count - n * LANES)
            if wide > 0:
                at = n % per * each
                block = table_in[n // per, at : at + each].astype(F32).reshape(heads, types, LANES)
                table_ref[:, :, n * LANES : n * LANES + wide] = block[:, :, :wide]


def unpack(level_group, enc, fus, table, width1, width2, table_shape):
    groups = enc.shape[0]
    pairs = groups // 4

    def group_of(i, s):
        return s[i % 2 * (groups // 2) + i // (2 * pairs) * pairs + i // 2 % pairs]

    heads, types, count = table_shape
    table_rows = -(-count // SPAN) * heads * types
    panels = width2 * width2 // LANES
    sizes1 = [(2, width1), (2, width1), (width1, 3 * width1), (width1, width1), (width1, 4 * width1), (width1, 4 * width1), (width1, 2 * width1)]
    sizes2 = [(2, width2), (2, width2), (width2, 3 * width2), (width2, width2), (width2, 4 * width2), (4 * width2, width2)]
    square = (width2, width2)
    return pl.pallas_call(
        unpack_kernel,
        out_shape=tuple(jax.ShapeDtypeStruct((groups,) + s, F32) for s in sizes1)
        + tuple(jax.ShapeDtypeStruct(s, F32) for s in sizes2)
        + (jax.ShapeDtypeStruct(table_shape, F32),),
        grid_spec=pltpu.PrefetchScalarGridSpec(
            num_scalar_prefetch=1,
            grid=(groups,),
            in_specs=[
                pl.BlockSpec((1,) + enc.shape[1:], lambda i, s: (i, 0, 0)),
                pl.BlockSpec((1, panels, LANES), lambda i, s: (i // 6, i % 6, 0)),
                pl.BlockSpec((1, EXTRA, LANES), lambda i, s: (0, 6 * panels // EXTRA, 0)),
                pl.BlockSpec((2, table_rows, LANES), lambda i, s: (0, 0, 0)),
            ],
            out_specs=tuple(pl.BlockSpec((1,) + s, lambda i, s: (group_of(i, s), 0, 0)) for s in sizes1)
            + (
                pl.BlockSpec((2, width2), lambda i, s: (0, 0)),
                pl.BlockSpec((2, width2), lambda i, s: (0, 0)),
                pl.BlockSpec(square, lambda i, s: (0, jnp.minimum(i, 2))),
                pl.BlockSpec(square, lambda i, s: (0, 0)),
                pl.BlockSpec(square, lambda i, s: (0, jnp.clip(i - 4, 0, 3))),
                pl.BlockSpec(square, lambda i, s: (jnp.clip(i - 8, 0, 3), 0)),
                pl.BlockSpec(table_shape, lambda i, s: (0, 0, 0)),
            ),
        ),
        compiler_params=pltpu.CompilerParams(vmem_limit_bytes=VMEM_LIMIT),
        name="unpack",
    )(level_group, enc, fus, fus, table)


def shards(
    tokens_in,
    enc_gains,
    enc_shifts,
    enc_qkv,
    enc_out,
    enc_up,
    enc_down,
    enc_lift,
    fus_gains,
    fus_shifts,
    fus_qkv,
    fus_out,
    fus_up,
    fus_down,
    fus_table,
    target,
    loss_code,
    level_group,
    window_type,
    pos_index,
):
    enc = select_rows(
        level_group, (enc_gains, enc_shifts, enc_qkv, enc_out, enc_up, jnp.swapaxes(enc_down, 1, 2), enc_lift)
    )
    output, x_grad, enc_sums, fus_sums, table_sums = layer(
        window_type.T,
        tokens_in,
        enc,
        (fus_gains, fus_shifts, fus_qkv, fus_out, fus_up, fus_down),
        fus_table,
        pos_index,
        target,
        jnp.swapaxes(loss_code, 0, 1),
    )
    grads = unpack(
        level_group,
        enc_sums.reshape(level_group.shape[0], ROWS1, LANES),
        fus_sums,
        table_sums,
        enc_out.shape[1],
        fus_out.shape[0],
        fus_table.shape,
    )
    return (output, x_grad, *grads[:5], jnp.swapaxes(grads[5], 1, 2), *grads[6:])


def solution(mesh):
    copied = P()
    in_specs = (
        (P("lvl", None, "win", None),)
        + (copied,) * 14
        + (P(None, "lvl", "win", None), P(None, "lvl", "win"), copied, P("lvl", "win"), copied)
    )
    out_specs = (P(None, "lvl", "win", None), P("lvl", None, "win", None)) + (copied,) * 14
    return jax.shard_map(shards, mesh=mesh, in_specs=in_specs, out_specs=out_specs, check_vma=False)
```

```python
import functools

import jax
import jax.numpy as jnp
from jax import lax
from jax.experimental import pallas as pl
from jax.experimental.pallas import tpu as pltpu
from jax.sharding import PartitionSpec as P

HEADS1 = 6
HEADS2 = 12
HEAD = 32
EPS = 1e-05
LANES = 128
SPAN = 256
PER = 4
UNROLL = 6
ROWS1 = 4096
CHUNKS1 = (48, 48, 32)
CHUNKS2 = (32, 32, 48)
CHUNKS3 = (16, 16, 16)
EXTRA = 16
VMEM_LIMIT = 60 * 1024 * 1024

BF = jnp.bfloat16
F32 = jnp.float32


def nn(a, b):
    return lax.dot_general(a, b, (((1,), (0,)), ((), ())), preferred_element_type=F32)


def nt(a, b):
    return lax.dot_general(a, b, (((1,), (1,)), ((), ())), preferred_element_type=F32)


def tn(a, b):
    return lax.dot_general(a, b, (((0,), (0,)), ((), ())), preferred_element_type=F32)


RING = 4
STRIDES = (16, 4, 1)
ORDERS = ((0, 1, 2), (1, 2, 0), (2, 0, 1))
MESH = pl.DeviceIdType.MESH
MESSAGES = 22


def coordinate(axis):
    return lax.rem(lax.axis_index("win") // STRIDES[axis], RING)


def along(axis, hops):
    place = lax.axis_index("win")
    mine = coordinate(axis)
    other = lax.rem(mine + hops, RING)
    return (lax.axis_index("lvl"), place + (other - mine) * STRIDES[axis])


def partner():
    return (1 - lax.axis_index("lvl"), lax.axis_index("win"))


def add_rows(dest, at, rows, others):
    step = max(s for s in (128, 112, 96, 64, 48, 32, 16) if rows % s == 0)

    @pl.loop(0, rows // step)
    def _(i):
        here = pl.ds(pl.multiple_of(at + i * step, 16), step)
        total = dest[here, :].astype(F32)
        for ref, start in others:
            total += ref[pl.ds(pl.multiple_of(start + i * step, 16), step), :].astype(F32)
        dest[here, :] = total.astype(BF)


def rows_of(ref, at, size):
    return ref.at[pl.ds(pl.multiple_of(at, 16), size)]


class Place:
    def __init__(self):
        self.here = [coordinate(axis) for axis in range(3)]
        self.chips = {(axis, hops): along(axis, hops) for axis in range(3) for hops in (1, 2, 3)}
        self.partner = partner()


class Part:
    def __init__(self, place, own, out, box, send, recv, keep, base, chunk, order, ring):
        self.own, self.out, self.box, self.send, self.recv, self.keep = own, out, box, send, recv, keep
        self.place, self.axes, self.ring = place, order, ring
        self.here = [place.here[a] for a in order]
        self.big, self.mid, self.chunk = 16 * chunk, 4 * chunk, chunk
        self.base = base
        self.first = base + self.here[0] * self.big
        self.second = self.first + self.here[1] * self.mid
        self.third = self.second + self.here[2] * chunk

    def top(self, hops):
        return self.base + jnp.bitwise_and(self.here[0] + hops, RING - 1) * self.big

    def message(self, n):
        big, mid, chunk = self.big, self.mid, self.chunk
        half = big // 2
        up, down = (0, 1), (0, RING - 1)
        own, out, box = self.own, self.out, self.box
        after = 3 * big
        if n < 6 and not self.ring:
            hops = (1, 3, 2)[n]
            src, dst, to = rows_of(own, self.top(hops), big), rows_of(box, n * big, big), (0, hops)
        elif n == 0:
            src, dst, to = rows_of(own, self.top(2), half), rows_of(box, 0, half), up
        elif n == 1:
            src, dst, to = rows_of(own, self.top(2) + half, half), rows_of(box, half, half), down
        elif n == 2:
            src, dst, to = rows_of(own, self.top(1) + half, half), rows_of(box, big + half, half), up
        elif n == 3:
            src, dst, to = rows_of(own, self.top(3), half), rows_of(box, 2 * big, half), down
        elif n == 4:
            src, dst, to = rows_of(own, self.top(1), half), rows_of(box, big, half), up
        elif n == 5:
            src, dst, to = rows_of(own, self.top(3) + half, half), rows_of(box, 2 * big + half, half), down
        elif n < 9:
            hops = (1, 3, 2)[n - 6]
            at = self.first + jnp.bitwise_and(self.here[1] + hops, RING - 1) * mid
            src, dst, to = rows_of(own, at, mid), rows_of(box, after + (n - 6) * mid, mid), (1, hops)
        elif n < 12:
            hops = (1, 3, 2)[n - 9]
            at = self.second + jnp.bitwise_and(self.here[2] + hops, RING - 1) * chunk
            src, to = rows_of(own, at, chunk), (2, hops)
            dst = rows_of(box, after + 3 * mid + (n - 9) * chunk, chunk)
        elif n < 15:
            src, dst = rows_of(own, self.third, chunk), rows_of(out, self.third, chunk)
            to = (2, (1, 3, 2)[n - 12])
        elif n < 18:
            src = dst = rows_of(out, self.second, mid)
            to = (1, (1, 3, 2)[n - 15])
        elif not self.ring:
            src = dst = rows_of(out, self.first, big)
            to = (0, (1, 3, 2)[n - 18])
        elif n < 20:
            src = dst = rows_of(out, self.first, big)
            to = (up, down)[n - 18]
        elif n == 20:
            src = dst = rows_of(out, self.top(3), half)
            to = up
        else:
            src = dst = rows_of(out, self.top(1) + half, half)
            to = down
        device = self.place.chips[self.axes[to[0]], to[1]]
        return pltpu.make_async_remote_copy(
            src, dst, self.send.at[n], self.recv.at[n], device_id=device, device_id_type=MESH
        )

    def start(self, *numbers):
        for n in numbers:
            self.message(n).start()

    def wait(self, *numbers):
        for n in numbers:
            self.message(n).wait()

    def kept(self):
        return pltpu.make_async_copy(
            rows_of(self.own, self.third, self.chunk), rows_of(self.out, self.third, self.chunk), self.keep
        )

    def stage(self, k):
        big, mid, chunk, own, box = self.big, self.mid, self.chunk, self.own, self.box
        half, after = big // 2, 3 * big
        if k == 0:
            self.start(*((0, 1, 2, 3) if self.ring else (2, 0, 1)))
        elif k == 1 and self.ring:
            self.wait(0)
            add_rows(own, self.top(1), half, [(box, 0)])
            self.start(4)
            self.wait(1)
            add_rows(own, self.top(3) + half, half, [(box, half)])
            self.start(5)
        elif k == 2:
            if self.ring:
                self.wait(2, 3, 4, 5)
            else:
                self.wait(0, 1, 2)
            add_rows(own, self.first, big, [(box, n * big) for n in ((1, 2) if self.ring else (0, 1, 2))])
            self.start(6, 7, 8)
        elif k == 3:
            self.wait(6, 7, 8)
            add_rows(own, self.second, mid, [(box, after + n * mid) for n in range(3)])
            self.start(9, 10, 11)
        elif k == 4:
            self.wait(9, 10, 11)
            add_rows(own, self.third, chunk, [(box, after + 3 * mid + n * chunk) for n in range(3)])
            self.kept().start()
            self.start(12, 13, 14)
        elif k == 5:
            self.kept().wait()
            self.wait(12, 13, 14)
            self.start(15, 16, 17)
        elif k == 6:
            self.wait(15, 16, 17)
            self.start(*((18, 19) if self.ring else (20, 18, 19)))
        elif k == 7 and self.ring:
            self.wait(18)
            self.start(20)
            self.wait(19)
            self.start(21)
        elif k == 8:
            self.wait(*((20, 21) if self.ring else (18, 19, 20)))


def parts_of(place, chunks, own, out, boxes, sems, ring):
    parts, base = [], 0
    for n, chunk in enumerate(chunks):
        send, recv, keep = (sem.at[n] for sem in sems)
        parts.append(Part(place, own, out, boxes[n], send, recv, keep, base, chunk, ORDERS[n], ring))
        base += 64 * chunk
    return parts


def run(parts, k):
    for part in parts:
        part.stage(k)


def type_picker(kinds, heads, types):
    shape = (heads * types, len(kinds) * heads)
    row = lax.broadcasted_iota(jnp.int32, shape, 0)
    column = lax.broadcasted_iota(jnp.int32, shape, 1)
    kind = jnp.full(shape, kinds[-1], jnp.int32)
    for n in reversed(range(len(kinds) - 1)):
        kind = jnp.where(column < (n + 1) * heads, kinds[n], kind)
    same_head = (row // types) == (column % heads)
    return (same_head & ((row % types) == kind)).astype(F32).astype(BF)


def lay_positions(pos_ref, all_pos):
    keys = pos_ref.shape[0]
    tails = keys - LANES
    all_pos[:keys] = pos_ref[...].astype(F32).T[:, :LANES].astype(jnp.int32)
    all_pos[keys : keys + tails] = pos_ref[LANES:, :LANES]
    all_pos[keys + tails :] = jnp.full((tails, LANES), -1, jnp.int32)
    all_pos[keys + tails :, : keys - LANES] = pos_ref[LANES:, LANES:]


def one_hot_of(pos):
    low = jnp.bitwise_and(pos, SPAN - 1).astype(F32).astype(BF)
    line = lax.broadcasted_iota(jnp.int32, (SPAN, pos.shape[1]), 0).astype(F32).astype(BF)
    return jnp.where(line == low, jnp.ones((), BF), jnp.zeros((), BF))


def spread_table(picker, table_ref, t2):
    rows, count = picker.shape[1], table_ref.shape[1]
    for k in range(t2.shape[0] // rows):
        width = min(SPAN, count - k * SPAN)
        part = table_ref[:, k * SPAN : k * SPAN + width].astype(BF)
        t2[k * rows : (k + 1) * rows, :width] = tn(picker, part).astype(BF)
        if width < SPAN:
            t2[k * rows : (k + 1) * rows, width:] = jnp.zeros((rows, SPAN - width), BF)


def look_up(t2, all_pos, dest, first, last):
    rows = dest.shape[0]
    high = t2.shape[0] // rows

    @pl.loop(first, last, unroll=2)
    def _(i):
        at = pl.multiple_of(i * 8, 8)
        eight = all_pos[pl.ds(at, 8), :]
        for s in range(0, 8, PER):
            pos = jnp.concatenate([eight[s + j : s + j + 1] for j in range(PER)], 1)
            top = jnp.right_shift(pos, 8)
            spread = nn(t2[...], one_hot_of(pos))
            picked = jnp.zeros((rows, PER * LANES), F32)
            for k in range(high):
                picked = jnp.where(top == k, spread[k * rows : (k + 1) * rows], picked)
            for j in range(PER):
                dest[:, pl.ds(at + s + j, 1), :] = picked[:, j * LANES : (j + 1) * LANES].reshape(rows, 1, LANES)


def turn_tails(bias, bias_tail, keys):
    tails = keys - LANES
    per = bias_tail.shape[2] // tails
    for i in range(bias_tail.shape[0]):
        lines = bias[i * per : (i + 1) * per, keys : keys + tails].reshape(per * tails, LANES)
        bias_tail[i, :LANES] = lines.T
        lines = bias[i * per : (i + 1) * per, keys + tails : keys + 2 * tails].reshape(per * tails, LANES)
        bias_tail[i, LANES:] = lines.T[: keys - LANES]


def lay_terms(ds_main, ds_tail, lines):
    rows, keys = ds_main.shape[:2]
    tails = keys - LANES
    per = ds_tail.shape[2] // tails

    @pl.loop(0, ds_tail.shape[0])
    def _(i):
        at = pl.ds(i * per, per)
        lines[at, :keys] = ds_main[at].astype(F32)
        block = ds_tail[i].astype(F32)
        lines[at, keys : keys + tails] = block[:LANES].T.reshape(per, tails, LANES)
        lines[at, keys + tails : keys + 2 * tails] = jnp.zeros((per, tails, LANES), F32)
        lines[at, keys + tails : keys + 2 * tails, : keys - LANES] = block[LANES:].T.reshape(per, tails, keys - LANES)


def add_terms(acc, all_pos, lines, first, last):
    rows = lines.shape[0]
    high = acc.shape[0] // rows

    @pl.loop(first, last, unroll=2)
    def _(i):
        at = pl.multiple_of(i * 8, 8)
        eight = all_pos[pl.ds(at, 8), :]
        total = None
        for s in range(0, 8, PER):
            pos = jnp.concatenate([eight[s + j : s + j + 1] for j in range(PER)], 1)
            terms = jnp.concatenate([lines[:, pl.ds(at + s + j, 1), :].reshape(rows, LANES) for j in range(PER)], 1)
            top = jnp.right_shift(pos, 8)
            parts = jnp.concatenate([jnp.where(top == k, terms, 0.0) for k in range(high)], 0)
            term = nt(parts.astype(BF), one_hot_of(pos))
            total = term if total is None else total + term
        acc[...] += total


def norm(values):
    centred = values - jnp.mean(values, -1, keepdims=True)
    spread = jnp.mean(centred * centred, -1, keepdims=True)
    scale = lax.rsqrt(spread + EPS)
    return centred * scale, scale


def norm_back(grad, gain, unit, scale):
    scaled = grad * gain
    first = jnp.mean(scaled, -1, keepdims=True)
    second = jnp.mean(scaled * unit, -1, keepdims=True)
    return (scaled - first - unit * second) * scale


def gelu_pair(v):
    half = jnp.exp(-0.5 * v * v)
    t = 1.0 / (1.0 + 0.23164189 * jnp.abs(v))
    series = t * (0.127414796 + t * (-0.142248368 + t * (0.7107068705 + t * (-0.7265760135 + t * 0.5307027145))))
    tail = series * half
    phi = jnp.where(v >= 0.0, 1.0 - tail, tail)
    return v * phi, phi + v * half * 0.3989422804014327


def head_masks(width):
    lane = lax.broadcasted_iota(jnp.int32, (1, width), 1)
    return [(lane // HEAD) == h for h in range(width // HEAD)]


def keep(mask, values):
    return jnp.where(mask, values, 0.0)


def put_panels(ref, at, values):
    rows = values.shape[0]
    for j in range(values.shape[1] // LANES):
        ref[at + j * rows : at + (j + 1) * rows] = values[:, j * LANES : (j + 1) * LANES].astype(ref.dtype)


def softmax_rows(scores):
    top = jnp.max(scores, 0, keepdims=True)
    e = jnp.exp(scores - top)
    return e * (1.0 / jnp.sum(e, 0, keepdims=True))


def score_back(prob, grad):
    return prob * (grad - jnp.sum(grad * prob, 0, keepdims=True))


def layer_kernel(
    kinds_ref, tokens_ref,
    e_gain0, e_gain1, e_shift0, e_shift1,
    e_qkv0, e_qkv1, e_out0, e_out1, e_up0, e_up1, e_down0, e_down1, e_lift0, e_lift1,
    f_gain, f_shift, f_qkv_ref, f_out_ref, f_up_ref, f_down_ref,
    table_ref, pos_ref, target_ref, code_ref,
    out_ref, xg_out, e_all, f_all, t_all,
    f_qkv, f_out, f_up, f_down,
    x_s, xg_s, n1_s, q_s, k_s, v_s, p_s, o_s, n2_s, h_s, act_s, gp_s, res_s,
    win_s, fq, fk, fv, fp, fo, fdq, fdk, fdv, fh, fn2, fdy, fgrad,
    t2, all_pos, bias_main, bias_tail, ds_main, ds_tail, acc_t,
    acc, acc_norm, own_e, own_f, give_f, peer_f, own_t, give_t, peer_t,
    be0, be1, be2, bf0, bf1, bf2, bt0, bt1, bt2,
    se, re, ke, sf, rf, kf, st, rt, kt, misc_send, misc_recv, misc_near,
):
    boxes_e, boxes_f, boxes_t = (be0, be1, be2), (bf0, bf1, bf2), (bt0, bt1, bt2)
    sems_e, sems_f, sems_t = (se, re, ke), (sf, rf, kf), (st, rt, kt)
    step = pl.program_id(0)
    side = lax.axis_index("lvl")
    rows = x_s.shape[2]
    width1 = x_s.shape[3]
    width2 = f_qkv.shape[0]
    half = rows // 2
    keys = rows
    root = HEAD ** (-0.5)
    masks1 = head_masks(width1)
    masks2 = head_masks(LANES)
    picks2 = [m.astype(F32).astype(BF) for m in masks2]
    gains1, shifts1 = (e_gain0, e_gain1), (e_shift0, e_shift1)
    w_qkv, w_out, w_up = (e_qkv0, e_qkv1), (e_out0, e_out1), (e_up0, e_up1)
    w_down, w_lift = (e_down0, e_down1), (e_lift0, e_lift1)

    pairs = x_s.shape[1]
    heads_all = width2 // HEAD
    types = table_ref.shape[0] // heads_all
    terms_each = 2 * heads_all
    panels = 12 * width2 // LANES
    halves = panels // 2 * width2

    place = Place()

    def encoder(q, ring=False):
        return parts_of(
            place, CHUNKS1, own_e.at[q], e_all.at[side, q], [b.at[q] for b in boxes_e], [s.at[q] for s in sems_e], ring
        )

    def joining():
        return parts_of(place, CHUNKS2, own_f, f_all.at[side], boxes_f, sems_f, True)

    def table():
        return parts_of(place, CHUNKS3, own_t, t_all.at[side], boxes_t, sems_t, False)

    def hand_over(ref, n):
        return remote(ref.at[side], ref.at[side], 3 + pairs + n)

    def hand_encoder(q):
        return remote(e_all.at[side, q], e_all.at[side, q], 5 + pairs + q)

    def hand_quarters(parts, first, quarters, what):
        for k, part in enumerate(parts):
            for hops in quarters:
                rows = rows_of(part.out, part.top(hops), part.big)
                getattr(remote(rows, rows, first + 4 * k + hops), what)()

    def hand_last(quarters, what):
        hand_quarters(encoder(2, ring=True), 4 + 2 * pairs, quarters, what)

    def hand_joining(quarters, what):
        hand_quarters(joining(), 16 + 2 * pairs, quarters, what)

    def tick(new=None, old=None):
        if new is not None:

            @pl.when(step >= 1)
            def _():
                run(encoder(step - 1), new)

        if old is not None:

            @pl.when(step == 2)
            def _():
                if old < 9:
                    run(encoder(0), old)
                if old == 8:
                    hand_encoder(0).start()

    def remote(src, dst, n):
        return pltpu.make_async_remote_copy(
            src, dst, misc_send.at[n], misc_recv.at[n], device_id=place.partner, device_id_type=MESH
        )

    def near(src, dst, n):
        return pltpu.make_async_copy(src, dst, misc_near.at[n])

    def tokens():
        given = remote(tokens_ref.at[0, pl.ds((1 - side) * pairs, pairs)], x_s.at[side], 0)
        taken = near(tokens_ref.at[0, pl.ds(side * pairs, pairs)], x_s.at[side], 0)
        return given, taken

    def joining_weights():
        pairs_of = ((f_qkv_ref, f_qkv), (f_out_ref, f_out), (f_up_ref, f_up), (f_down_ref, f_down))
        return tuple(near(src, dst, 1 + pairs + n) for n, (src, dst) in enumerate(pairs_of))

    def tokens_grad(q):
        given = remote(xg_s.at[1 - side, q], xg_out.at[0, side * pairs + q], 1 + q)
        taken = near(xg_s.at[side, q], xg_out.at[0, side * pairs + q], 1 + q)
        return given, taken

    def joining_half():
        return remote(give_f, peer_f, 1 + pairs)

    def table_half():
        return remote(give_t.at[1 - side], peer_t, 2 + pairs)

    @pl.when(step == 0)
    def _():
        barrier = pltpu.get_barrier_semaphore()
        friends = list(place.chips.values()) + [place.partner]
        for device in friends:
            pl.semaphore_signal(barrier, inc=1, device_id=device, device_id_type=MESH)
        pl.semaphore_wait(barrier, len(friends))
        for copy in tokens() + joining_weights():
            copy.start()
        lay_positions(pos_ref, all_pos)
        for q in range(pairs):
            picker = type_picker([kinds_ref[w, q] for w in range(2)], heads_all, types)
            spread_table(picker, table_ref, t2.at[q])
        acc[...] = jnp.zeros_like(acc)
        acc_norm[...] = jnp.zeros_like(acc_norm)

    eights = (keys + 2 * (keys - LANES)) // 8
    look_up(t2.at[step], all_pos, bias_main, 0, eights)
    turn_tails(bias_main, bias_tail, keys)
    tick(new=2, old=8)

    @pl.when(step == 0)
    def _():
        for copy in tokens():
            copy.wait()

    def stack1(values):
        return jnp.concatenate([keep(m, values) for m in masks1], 0).astype(BF)

    def fold1(stacked):
        total = keep(masks1[0], stacked[:half])
        for h in range(1, HEADS1):
            total += keep(masks1[h], stacked[h * half : (h + 1) * half])
        return total

    both = range(2)
    windows = [(l, w, slice(w * half, (w + 1) * half)) for l in both for w in both]
    xs = [x_s[l, step].astype(F32) for l in both]
    for l in both:
        z1, _ = norm(xs[l])
        n1_s[l] = (z1 * gains1[l][0, 0:1] + shifts1[l][0, 0:1]).astype(BF)
    for l in both:
        qkv = nn(n1_s[l], w_qkv[l][0])
        q_s[l] = qkv[:, :width1].astype(BF).astype(F32)
        k_s[l] = qkv[:, width1 : 2 * width1].astype(BF).astype(F32)
        v_s[l] = qkv[:, 2 * width1 :].astype(BF).astype(F32)
    for l, w, part in windows:
        p_s[l, w] = softmax_rows(nt(k_s[l, part].astype(BF), stack1(q_s[l, part])) * root)
    for l, w, part in windows:
        o_s[l, part] = fold1(tn(p_s[l, w].astype(BF), v_s[l, part].astype(BF)))
    for l in both:
        h = x_s[l, step].astype(F32) + nn(o_s[l].astype(BF), w_out[l][0])
        h_s[l] = h
        z2, _ = norm(h)
        n2_s[l] = (z2 * gains1[l][0, 1:2] + shifts1[l][0, 1:2]).astype(BF)
    for l in both:
        act, slope = gelu_pair(nn(n2_s[l], w_up[l][0]))
        act = act.astype(BF)
        act_s[l] = act
        gp_s[l] = slope
        res_s[l] = (h_s[l] + nt(act, w_down[l][0])).astype(BF)
    for l in both:
        lifted = nn(res_s[l], w_lift[l][0]).astype(BF).astype(F32)
        for w in range(2):
            win_s[w * rows + l * half : w * rows + (l + 1) * half] = lifted[w * half : (w + 1) * half]

    eye = lax.broadcasted_iota(jnp.int32, (rows, rows), 0) == lax.broadcasted_iota(jnp.int32, (rows, rows), 1)
    for l in range(2):
        codes = code_ref[:, l].astype(F32)
        chosen = lax.broadcasted_iota(jnp.int32, codes.shape, 0) == step
        weight = 0.5 * jnp.exp(0.35 * jnp.sum(jnp.where(chosen, codes, 0.0), 0, keepdims=True))
        column = jnp.sum(jnp.where(eye, weight, 0.0), 1, keepdims=True)
        direction = column * target_ref[l, 0].astype(F32)
        for w in range(2):
            fdy[w * rows + l * half : w * rows + (l + 1) * half] = direction[w * half : (w + 1) * half]

    @pl.when(step == 0)
    def _():
        for copy in joining_weights():
            copy.wait()

    lane_groups = width2 // LANES
    z1, _ = norm(win_s[...])
    fn1 = (z1 * f_gain[0:1] + f_shift[0:1]).astype(BF)
    for t, dest in enumerate((fq, fk, fv)):
        part = nn(fn1, f_qkv[:, t * width2 : (t + 1) * width2]).astype(BF)
        for w in range(2):
            for g in range(lane_groups):
                dest[w * lane_groups + g] = part[w * rows : (w + 1) * rows, g * LANES : (g + 1) * LANES]
    tails = rows - LANES
    tick(new=3)

    heads = LANES // HEAD
    lanes = heads * LANES + heads * tails
    spans = [slice(j * LANES, min((j + 1) * LANES, lanes)) for j in range(heads + 1)]

    def stack2(values):
        main, tail = values[:LANES], values[LANES:]
        return jnp.concatenate([main * m for m in picks2] + [tail * m for m in picks2], 0)

    def fold2(stacked):
        main = keep(masks2[0], stacked[:LANES])
        tail = keep(masks2[0], stacked[heads * LANES : heads * LANES + tails])
        for h in range(1, heads):
            main += keep(masks2[h], stacked[h * LANES : (h + 1) * LANES])
            tail += keep(masks2[h], stacked[heads * LANES + h * tails : heads * LANES + (h + 1) * tails])
        return jnp.concatenate([main, tail], 0)

    @pl.loop(0, 2 * lane_groups, unroll=UNROLL)
    def _(i):
        scores = nt(fk[i], stack2(fq[i]))
        probs = []
        for j, span in enumerate(spans):
            bias = bias_main[i * heads + j, :keys] if j < heads else bias_tail[i]
            prob = softmax_rows(scores[:, span] * root + bias)
            fp[i, :, span] = prob
            probs.append(prob.astype(BF))
        fo[i] = fold2(tn(jnp.concatenate(probs, 1), fv[i])).astype(BF)


    def joined(ref):
        return jnp.concatenate(
            [jnp.concatenate([ref[w * lane_groups + g] for g in range(lane_groups)], 1) for w in range(2)], 0
        )

    hidden = win_s[...] + nn(joined(fo), f_out[...])
    fh[...] = hidden
    z2, _ = norm(hidden)
    fn2[...] = (z2 * f_gain[1:2] + f_shift[1:2]).astype(BF)

    def add_panels(n, values):
        for j in range(values.shape[1] // LANES):
            panel = values[:, j * LANES : (j + 1) * LANES]
            acc[2 * (n + j) : 2 * (n + j) + 2] += panel.reshape(2, width2 // 2, LANES)

    blocks = f_up.shape[1] // width2
    fgrad[...] = jnp.zeros_like(fgrad)

    per_block = width2 // LANES
    wide = 2 * width2
    for j in range(blocks // 2):
        up = f_up[:, j * wide : (j + 1) * wide]
        down = f_down[j * wide : (j + 1) * wide, :]
        n2 = fn2[...]
        low = fdy[...].astype(BF)
        act, slope = gelu_pair(nn(n2, up))
        act = act.astype(BF)
        fh[...] += nn(act, down)
        inner_grad = (nt(low, down) * slope).astype(BF)
        down_grad = tn(act, low)
        add_panels((8 + 2 * j) * per_block, down_grad[:width2])
        add_panels((9 + 2 * j) * per_block, down_grad[width2:])
        add_panels((4 + 2 * j) * per_block, tn(n2, inner_grad))
        fgrad[...] += nt(inner_grad, up)
        if j == 0:
            tick(new=4)

    for l in range(2):
        for w in range(2):
            out_ref[l, 0, w * half : (w + 1) * half] = fh[w * rows + l * half : w * rows + (l + 1) * half].astype(BF)

    hidden = win_s[...] + nn(joined(fo), f_out[...])
    z2, r2 = norm(hidden)
    grad = fgrad[...]
    acc_norm[1:2] += jnp.sum(grad * z2, 0, keepdims=True)
    acc_norm[3:4] += jnp.sum(grad, 0, keepdims=True)
    hidden_grad = fdy[...] + norm_back(grad, f_gain[1:2], z2, r2)
    fgrad[...] = hidden_grad
    low = hidden_grad.astype(BF)
    add_panels(3 * per_block, tn(joined(fo), low))
    att_grad = nt(low, f_out[...]).astype(BF)
    tick(new=5)
    for w in range(2):
        for g in range(lane_groups):
            fo[w * lane_groups + g] = att_grad[w * rows : (w + 1) * rows, g * LANES : (g + 1) * LANES]

    @pl.loop(0, 2 * lane_groups, unroll=UNROLL)
    def _(i):
        queries = stack2(fq[i])
        grads = stack2(fo[i])
        prob_grads = nt(fv[i], grads)
        probs, terms = [], []
        for j, span in enumerate(spans):
            prob = fp[i, :, span]
            probs.append(prob.astype(BF))
            ds = score_back(prob, prob_grads[:, span]).astype(BF)
            terms.append(ds)
            if j < heads:
                ds_main[i * heads + j] = ds
            else:
                ds_tail[i] = ds
        probs, terms = jnp.concatenate(probs, 1), jnp.concatenate(terms, 1)
        fdv[i] = nn(probs, grads).astype(BF)
        fdk[i] = (nn(terms, queries) * root).astype(BF)
        fdq[i] = (fold2(tn(terms, fk[i])) * root).astype(BF)

    z1, r1 = norm(win_s[...])
    n1 = (z1 * f_gain[0:1] + f_shift[0:1]).astype(BF)
    first = jnp.zeros((2 * rows, width2), F32)
    for t, src in enumerate((fdq, fdk, fdv)):
        part = joined(src)
        add_panels(t * per_block, tn(n1, part))
        first += nt(part, f_qkv[:, t * width2 : (t + 1) * width2])
    acc_norm[0:1] += jnp.sum(first * z1, 0, keepdims=True)
    acc_norm[2:3] += jnp.sum(first, 0, keepdims=True)
    fgrad[...] += norm_back(first, f_gain[0:1], z1, r1)

    tick(new=6)

    @pl.when(step == 2)
    def _():
        for owner, dest in ((side, own_f), (1 - side, give_f)):

            @pl.loop(0, panels // 2)
            def _(n):
                panel = acc[pl.ds(2 * (owner * (panels // 2) + n), 2)].reshape(width2, LANES)
                dest[pl.ds(pl.multiple_of(n * width2, 16), width2), :] = panel.astype(BF)

            norms = acc_norm[...]
            norms = jnp.concatenate(
                [norms[:, g * LANES : (g + 1) * LANES] for g in range(lane_groups)]
                + [jnp.zeros((EXTRA - 4 * lane_groups, LANES), F32)],
                0,
            )
            dest[halves : halves + EXTRA] = norms.astype(BF)
        own_f[halves + EXTRA :] = jnp.zeros((own_f.shape[0] - halves - EXTRA, LANES), BF)
        joining_half().start()

    packs = [own_e.at[step, l * ROWS1 : (l + 1) * ROWS1] for l in both]
    lift_grads = [
        jnp.concatenate([fgrad[w * rows + l * half : w * rows + (l + 1) * half] for w in both], 0).astype(BF)
        for l in both
    ]
    d_outs = [nt(lift_grads[l], w_lift[l][0]) for l in both]
    for l in both:
        put_panels(packs[l], 12 * width1, tn(res_s[l], lift_grads[l]))
    norm_grads = [[None] * 4 for _ in both]
    hidden_grads, att_grads, mixed, first_grads = [None] * 2, [None] * 2, [None] * 2, [None] * 2
    inner_grads = [(nn(d_outs[l].astype(BF), w_down[l][0]) * gp_s[l]).astype(BF) for l in both]
    for l in both:
        put_panels(packs[l], 15 * width1, tn(d_outs[l].astype(BF), act_s[l]))
        put_panels(packs[l], 6 * width1, tn(n2_s[l], inner_grads[l]))
    for l in both:
        grad = nt(inner_grads[l], w_up[l][0])
        z2, r2 = norm(h_s[l])
        norm_grads[l][1] = jnp.sum(grad * z2, 0, keepdims=True)
        norm_grads[l][3] = jnp.sum(grad, 0, keepdims=True)
        hidden_grads[l] = d_outs[l] + norm_back(grad, gains1[l][0, 1:2], z2, r2)
    for l in both:
        att_grads[l] = nt(hidden_grads[l].astype(BF), w_out[l][0]).astype(BF).astype(F32)
    out_grads = [tn(o_s[l].astype(BF), hidden_grads[l].astype(BF)) for l in both]
    for l in both:
        h_s[l] = hidden_grads[l]

    grads = [stack1(att_grads[l][part]) for l, w, part in windows]
    terms = [
        score_back(p_s[l, w], nt(v_s[l, part].astype(BF), grads[n])).astype(BF)
        for n, (l, w, part) in enumerate(windows)
    ]
    dvs = [nn(p_s[l, w].astype(BF), grads[n]) for n, (l, w, part) in enumerate(windows)]
    dks = [nn(terms[n], stack1(q_s[l, part])) * root for n, (l, w, part) in enumerate(windows)]
    dqs = [fold1(tn(terms[n], k_s[l, part].astype(BF))) * root for n, (l, w, part) in enumerate(windows)]
    for l in both:
        mixed[l] = jnp.concatenate(
            [jnp.concatenate([dqs[n], dks[n], dvs[n]], 1) for n in (2 * l, 2 * l + 1)], 0
        ).astype(BF)
    for l in both:
        put_panels(packs[l], 0, jnp.concatenate([tn(n1_s[l], mixed[l]), out_grads[l]], 1))
    for l in both:
        first = nt(mixed[l], w_qkv[l][0])
        z1, r1 = norm(x_s[l, step].astype(F32))
        norm_grads[l][0] = jnp.sum(first * z1, 0, keepdims=True)
        norm_grads[l][2] = jnp.sum(first, 0, keepdims=True)
        norms = jnp.pad(jnp.concatenate(norm_grads[l], 0), ((0, 4), (0, 2 * LANES - width1)))
        norms = jnp.concatenate([norms[:4, :LANES], norms[:4, LANES:], jnp.zeros((8, LANES), F32)], 0)
        packs[l][21 * width1 : 21 * width1 + EXTRA] = norms.astype(BF)
        packs[l][21 * width1 + EXTRA :] = jnp.zeros((ROWS1 - 21 * width1 - EXTRA, LANES), BF)
        xg_s[l, step] = h_s[l] + norm_back(first, gains1[l][0, 0:1], z1, r1)
    for copy in tokens_grad(step):
        copy.start()

    @pl.when(step < 2)
    def _():
        run(encoder(step), 0)

    last = encoder(2, ring=True)

    @pl.when(step == 2)
    def _():
        run(last, 0)
        joining_half().wait()
        add_rows(own_f, 0, halves + EXTRA, [(peer_f, 0)])
        run(joining(), 0)

    lay_terms(ds_main, ds_tail, bias_main)
    acc_t[step] = jnp.zeros(acc_t.shape[1:], F32)
    add_terms(acc_t.at[step], all_pos, bias_main, 0, eights // 2)

    @pl.when(step == 2)
    def _():
        run(last, 1)
        run(joining(), 1)

    add_terms(acc_t.at[step], all_pos, bias_main, eights // 2, eights)

    @pl.when(step == 2)
    def _():
        kinds = [kinds_ref[n % 2, n // 2] for n in range(2 * pairs)]
        picker = type_picker(kinds, heads_all, types)
        many = heads_all * types
        high = acc_t.shape[1] // terms_each
        for k in range(high):
            part = jnp.concatenate([acc_t[q, k * terms_each : (k + 1) * terms_each] for q in range(pairs)], 0)
            part = nn(picker, part.astype(BF)).astype(BF)
            for j in range(SPAN // LANES):
                n = k * (SPAN // LANES) + j
                at = n % high * many
                give_t[n // high, at : at + many] = part[:, j * LANES : (j + 1) * LANES]
        table_half().start()
        table_rows = high * many
        own_t[table_rows:] = jnp.zeros((own_t.shape[0] - table_rows, LANES), BF)
        for copy in [near(give_t.at[side], own_t.at[:table_rows], 0)]:
            copy.start()
            copy.wait()
        run(last, 2)
        run(joining(), 2)
        table_half().wait()
        add_rows(own_t, 0, table_rows, [(peer_t, 0)])
        run(table(), 0)
        run(last, 3)
        run(joining(), 3)
        run(encoder(1), 8)
        hand_encoder(1).start()
        run(table(), 2)
        run(last, 4)
        run(joining(), 4)
        run(table(), 3)
        run(last, 5)
        run(table(), 4)
        run(joining(), 5)
        run(last, 6)
        hand_last((0,), "start")
        run(table(), 5)
        run(joining(), 6)
        hand_joining((0,), "start")
        run(table(), 6)
        run(last, 7)
        hand_last((3, 1), "start")
        run(joining(), 7)
        hand_joining((3, 1), "start")
        run(table(), 8)
        hand_over(t_all, 1).start()
        run(last, 8)
        hand_last((2,), "start")
        run(joining(), 8)
        hand_joining((2,), "start")
        hand_last((0, 3, 1, 2), "wait")
        hand_joining((0, 3, 1, 2), "wait")
        for q in range(pairs - 1):
            hand_encoder(q).wait()
        for q in range(pairs):
            for copy in tokens_grad(q):
                copy.wait()
        hand_over(t_all, 1).wait()


def layer(kinds, tokens, enc, fus, table, pos_index, target, code):
    pairs, rows, width2 = target.shape[1:]
    width1 = tokens.shape[3]
    ff1 = enc[4].shape[2]
    keys = rows
    tails = rows - LANES
    half = rows // 2
    heads, types, count = table.shape
    high = -(-count // SPAN)
    groups = 2 * width2 // LANES
    per = LANES // HEAD
    lanes = per * (LANES + tails)
    panels = 12 * width2 // LANES
    halves = panels // 2 * width2 + EXTRA
    table_rows = high * heads * types
    total1, total2, total3 = (64 * sum(c) for c in (CHUNKS1, CHUNKS2, CHUNKS3))

    def by_row(array, level):
        return pl.BlockSpec((1,) + array.shape[1:], lambda q, level=level: (level * pairs + q, 0, 0))

    def whole(array):
        return pl.BlockSpec(array.shape, lambda q: (0,) * array.ndim, pipeline_mode=pl.Buffered(1))

    anywhere = pl.BlockSpec(memory_space=pl.ANY)
    table = table.reshape(heads * types, count)
    enc_args, enc_specs = [], []
    for array in enc:
        for level in range(2):
            enc_args.append(array)
            enc_specs.append(by_row(array, level))
    moving = pl.BlockSpec((2, 1, rows, width2), lambda q: (0, q, 0, 0))
    dma = pltpu.SemaphoreType.DMA
    vmem = pltpu.VMEM
    return pl.pallas_call(
        layer_kernel,
        grid=(pairs,),
        out_shape=(
            jax.ShapeDtypeStruct((2, pairs, rows, width2), BF),
            jax.ShapeDtypeStruct((1, 2 * pairs, rows, width1), F32),
            jax.ShapeDtypeStruct((2, pairs, total1, LANES), BF),
            jax.ShapeDtypeStruct((2, total2, LANES), BF),
            jax.ShapeDtypeStruct((2, total3, LANES), BF),
        ),
        in_specs=[pl.BlockSpec(memory_space=pltpu.SMEM), anywhere]
        + enc_specs
        + [whole(a) for a in fus[:2]]
        + [anywhere] * 4
        + [whole(table), whole(pos_index), moving, whole(code)],
        out_specs=(moving, anywhere, anywhere, anywhere, anywhere),
        scratch_shapes=[vmem(a.shape, a.dtype) for a in fus[2:]]
        + [
            vmem((2, pairs, rows, width1), BF),
            vmem((2, pairs, rows, width1), F32),
            vmem((2, rows, width1), BF),
            vmem((2, rows, width1), F32),
            vmem((2, rows, width1), F32),
            vmem((2, rows, width1), F32),
            vmem((2, 2, half, HEADS1 * half), F32),
            vmem((2, rows, width1), F32),
            vmem((2, rows, width1), BF),
            vmem((2, rows, width1), F32),
            vmem((2, rows, ff1), BF),
            vmem((2, rows, ff1), F32),
            vmem((2, rows, width1), BF),
            vmem((2 * rows, width2), F32),
            vmem((groups, rows, LANES), BF),
            vmem((groups, rows, LANES), BF),
            vmem((groups, rows, LANES), BF),
            vmem((groups, rows, lanes), F32),
            vmem((groups, rows, LANES), BF),
            vmem((groups, rows, LANES), BF),
            vmem((groups, rows, LANES), BF),
            vmem((groups, rows, LANES), BF),
            vmem((2 * rows, width2), F32),
            vmem((2 * rows, width2), BF),
            vmem((2 * rows, width2), F32),
            vmem((2 * rows, width2), F32),
            vmem((pairs, high * 2 * heads, SPAN), BF),
            vmem((keys + 2 * tails, LANES), jnp.int32),
            vmem((2 * heads, keys + 2 * tails, LANES), F32),
            vmem((groups, keys, per * tails), F32),
            vmem((2 * heads, keys, LANES), BF),
            vmem((groups, keys, per * tails), BF),
            vmem((pairs, high * 2 * heads, SPAN), F32),
            vmem((2 * panels, width2 // 2, LANES), F32),
            vmem((4, width2), F32),
            vmem((pairs, total1, LANES), BF),
            vmem((total2, LANES), BF),
            vmem((halves, LANES), BF),
            vmem((halves, LANES), BF),
            vmem((total3, LANES), BF),
            vmem((2, table_rows, LANES), BF),
            vmem((table_rows, LANES), BF),
        ]
        + [vmem((pairs, 63 * chunk, LANES), BF) for chunk in CHUNKS1]
        + [vmem((63 * chunk, LANES), BF) for chunk in CHUNKS2 + CHUNKS3]
        + [dma((pairs, 3, MESSAGES)), dma((pairs, 3, MESSAGES)), dma((pairs, 3))]
        + [dma((3, MESSAGES)), dma((3, MESSAGES)), dma((3,))] * 2
        + [dma((28 + 2 * pairs,)), dma((28 + 2 * pairs,)), dma((5 + pairs,))],
        compiler_params=pltpu.CompilerParams(
            vmem_limit_bytes=VMEM_LIMIT + 2 * 1024 * 1024, collective_id=0, has_side_effects=True
        ),
        name="layer",
    )(kinds, tokens, *enc_args, *fus, table, pos_index, target, code)


def select_kernel(groups_ref, *refs):
    count = (len(refs) - 2) // 3
    arrays, picked, held = (refs[n * count : (n + 1) * count] for n in range(3))
    into, out_of = refs[-2:]
    rows = picked[0].shape[0]
    side = lax.axis_index("lvl")

    def load(n, row):
        level, pair = row // (rows // 2), row % (rows // 2)
        group = groups_ref[level * rows + side * (rows // 2) + pair]
        return pltpu.make_async_copy(arrays[n].at[group], held[n].at[row], into.at[n, row])

    def store(n, row):
        return pltpu.make_async_copy(held[n].at[row], picked[n].at[row], out_of.at[n, row])

    every = [(n, row) for row in range(rows) for n in range(count)]
    for at in every:
        load(*at).start()
    for at in every:
        load(*at).wait()
        store(*at).start()
    for at in every:
        store(*at).wait()


def select_rows(level_group, arrays):
    count = level_group.shape[0] // 2
    anywhere = pl.BlockSpec(memory_space=pl.ANY)
    return pl.pallas_call(
        select_kernel,
        out_shape=tuple(jax.ShapeDtypeStruct((count,) + a.shape[1:], a.dtype) for a in arrays),
        in_specs=[pl.BlockSpec(memory_space=pltpu.SMEM)] + [anywhere] * len(arrays),
        out_specs=(anywhere,) * len(arrays),
        scratch_shapes=[pltpu.VMEM((count,) + a.shape[1:], a.dtype) for a in arrays]
        + [pltpu.SemaphoreType.DMA((len(arrays), count))] * 2,
        compiler_params=pltpu.CompilerParams(vmem_limit_bytes=VMEM_LIMIT),
        name="select_rows",
    )(level_group, *arrays)


def unpack_kernel(
    groups_ref, enc_ref, fus_ref, fus_extra, table_in,
    gain_ref, shift_ref, qkv_ref, out_ref, up_ref, down_ref, lift_ref,
    fg_ref, fs_ref, fq_ref, fo_ref, fu_ref, fd_ref, table_ref,
):
    width = qkv_ref.shape[1]

    def panel(n):
        return enc_ref[0, n * width : (n + 1) * width].astype(F32)

    half = LANES // 2
    for n in range(4):
        qkv_ref[0, :, n * LANES : (n + 1) * LANES] = panel(n)
    mixed, last = panel(4), panel(5)
    qkv_ref[0, :, 4 * LANES :] = mixed[:, :half]
    out_ref[0] = jnp.concatenate([mixed[:, half:], last], 1)
    for n in range(6):
        up_ref[0, :, n * LANES : (n + 1) * LANES] = panel(6 + n)
        down_ref[0, :, n * LANES : (n + 1) * LANES] = panel(15 + n)
    for n in range(3):
        lift_ref[0, :, n * LANES : (n + 1) * LANES] = panel(12 + n)
    norms = enc_ref[0, 21 * width : 21 * width + EXTRA].astype(F32)
    norms = jnp.concatenate([norms[0:4], norms[4:8]], 1)[:, :width]
    gain_ref[0] = norms[0:2]
    shift_ref[0] = norms[2:4]
    i = pl.program_id(0)
    size = fo_ref.shape[0]

    def joining(dest):
        for n in range(size // LANES):
            dest[:, n * LANES : (n + 1) * LANES] = fus_ref[0, n * size : (n + 1) * size].astype(F32)

    @pl.when(i < 3)
    def _():
        joining(fq_ref)

    @pl.when(i == 3)
    def _():
        joining(fo_ref)

    @pl.when((i >= 4) & (i < 8))
    def _():
        joining(fu_ref)

    @pl.when(i >= 8)
    def _():
        joining(fd_ref)

    heads, types, count = table_ref.shape

    @pl.when(i == 0)
    def _():
        extra = fus_extra[0].astype(F32)
        extra = jnp.concatenate([extra[4 * n : 4 * n + 4] for n in range(size // LANES)], 1)
        fg_ref[...] = extra[0:2]
        fs_ref[...] = extra[2:4]
        each = heads * types
        per = table_in.shape[1] // each
        for n in range(2 * per):
            wide = min(LANES, count - n * LANES)
            if wide > 0:
                at = n % per * each
                block = table_in[n // per, at : at + each].astype(F32).reshape(heads, types, LANES)
                table_ref[:, :, n * LANES : n * LANES + wide] = block[:, :, :wide]


def unpack(level_group, enc, fus, table, width1, width2, table_shape):
    groups = enc.shape[0]
    pairs = groups // 4

    def group_of(i, s):
        return s[i % 2 * (groups // 2) + i // (2 * pairs) * pairs + i // 2 % pairs]

    heads, types, count = table_shape
    table_rows = -(-count // SPAN) * heads * types
    panels = width2 * width2 // LANES
    sizes1 = [(2, width1), (2, width1), (width1, 3 * width1), (width1, width1), (width1, 4 * width1), (width1, 4 * width1), (width1, 2 * width1)]
    sizes2 = [(2, width2), (2, width2), (width2, 3 * width2), (width2, width2), (width2, 4 * width2), (4 * width2, width2)]
    square = (width2, width2)
    return pl.pallas_call(
        unpack_kernel,
        out_shape=tuple(jax.ShapeDtypeStruct((groups,) + s, F32) for s in sizes1)
        + tuple(jax.ShapeDtypeStruct(s, F32) for s in sizes2)
        + (jax.ShapeDtypeStruct(table_shape, F32),),
        grid_spec=pltpu.PrefetchScalarGridSpec(
            num_scalar_prefetch=1,
            grid=(groups,),
            in_specs=[
                pl.BlockSpec((1,) + enc.shape[1:], lambda i, s: (i, 0, 0)),
                pl.BlockSpec((1, panels, LANES), lambda i, s: (i // 6, i % 6, 0)),
                pl.BlockSpec((1, EXTRA, LANES), lambda i, s: (0, 6 * panels // EXTRA, 0)),
                pl.BlockSpec((2, table_rows, LANES), lambda i, s: (0, 0, 0)),
            ],
            out_specs=tuple(pl.BlockSpec((1,) + s, lambda i, s: (group_of(i, s), 0, 0)) for s in sizes1)
            + (
                pl.BlockSpec((2, width2), lambda i, s: (0, 0)),
                pl.BlockSpec((2, width2), lambda i, s: (0, 0)),
                pl.BlockSpec(square, lambda i, s: (0, jnp.minimum(i, 2))),
                pl.BlockSpec(square, lambda i, s: (0, 0)),
                pl.BlockSpec(square, lambda i, s: (0, jnp.clip(i - 4, 0, 3))),
                pl.BlockSpec(square, lambda i, s: (jnp.clip(i - 8, 0, 3), 0)),
                pl.BlockSpec(table_shape, lambda i, s: (0, 0, 0)),
            ),
        ),
        compiler_params=pltpu.CompilerParams(vmem_limit_bytes=VMEM_LIMIT),
        name="unpack",
    )(level_group, enc, fus, fus, table)


def shards(
    tokens_in,
    enc_gains,
    enc_shifts,
    enc_qkv,
    enc_out,
    enc_up,
    enc_down,
    enc_lift,
    fus_gains,
    fus_shifts,
    fus_qkv,
    fus_out,
    fus_up,
    fus_down,
    fus_table,
    target,
    loss_code,
    level_group,
    window_type,
    pos_index,
):
    enc = select_rows(
        level_group, (enc_gains, enc_shifts, enc_qkv, enc_out, enc_up, jnp.swapaxes(enc_down, 1, 2), enc_lift)
    )
    output, x_grad, enc_sums, fus_sums, table_sums = layer(
        window_type.T,
        tokens_in,
        enc,
        (fus_gains, fus_shifts, fus_qkv, fus_out, fus_up, fus_down),
        fus_table,
        pos_index,
        target,
        jnp.swapaxes(loss_code, 0, 1),
    )
    grads = unpack(
        level_group,
        enc_sums.reshape(level_group.shape[0], ROWS1, LANES),
        fus_sums,
        table_sums,
        enc_out.shape[1],
        fus_out.shape[0],
        fus_table.shape,
    )
    return (output, x_grad, *grads[:5], jnp.swapaxes(grads[5], 1, 2), *grads[6:])


def solution(mesh):
    copied = P()
    in_specs = (
        (P("lvl", None, "win", None),)
        + (copied,) * 14
        + (P(None, "lvl", "win", None), P(None, "lvl", "win"), copied, P("lvl", "win"), copied)
    )
    out_specs = (P(None, "lvl", "win", None), P("lvl", None, "win", None)) + (copied,) * 14
    return jax.shard_map(shards, mesh=mesh, in_specs=in_specs, out_specs=out_specs, check_vma=False)
```

```python
import functools

import jax
import jax.numpy as jnp
from jax import lax
from jax.experimental import pallas as pl
from jax.experimental.pallas import tpu as pltpu
from jax.sharding import PartitionSpec as P

HEADS1 = 6
HEADS2 = 12
HEAD = 32
EPS = 1e-05
LANES = 128
SPAN = 256
PER = 4
UNROLL = 6
ROWS1 = 4096
CHUNKS1 = (48, 48, 32)
CHUNKS2 = (32, 32, 48)
CHUNKS3 = (16, 16, 16)
EXTRA = 16
VMEM_LIMIT = 60 * 1024 * 1024

BF = jnp.bfloat16
F32 = jnp.float32


def nn(a, b):
    return lax.dot_general(a, b, (((1,), (0,)), ((), ())), preferred_element_type=F32)


def nt(a, b):
    return lax.dot_general(a, b, (((1,), (1,)), ((), ())), preferred_element_type=F32)


def tn(a, b):
    return lax.dot_general(a, b, (((0,), (0,)), ((), ())), preferred_element_type=F32)


RING = 4
STRIDES = (16, 4, 1)
ORDERS = ((0, 1, 2), (1, 2, 0), (2, 0, 1))
MESH = pl.DeviceIdType.MESH
MESSAGES = 22


def coordinate(axis):
    return lax.rem(lax.axis_index("win") // STRIDES[axis], RING)


def along(axis, hops):
    place = lax.axis_index("win")
    mine = coordinate(axis)
    other = lax.rem(mine + hops, RING)
    return (lax.axis_index("lvl"), place + (other - mine) * STRIDES[axis])


def partner():
    return (1 - lax.axis_index("lvl"), lax.axis_index("win"))


def add_rows(dest, at, rows, others):
    step = max(s for s in (128, 112, 96, 64, 48, 32, 16) if rows % s == 0)

    @pl.loop(0, rows // step)
    def _(i):
        here = pl.ds(pl.multiple_of(at + i * step, 16), step)
        total = dest[here, :].astype(F32)
        for ref, start in others:
            total += ref[pl.ds(pl.multiple_of(start + i * step, 16), step), :].astype(F32)
        dest[here, :] = total.astype(BF)


def rows_of(ref, at, size):
    return ref.at[pl.ds(pl.multiple_of(at, 16), size)]


class Place:
    def __init__(self):
        self.here = [coordinate(axis) for axis in range(3)]
        self.chips = {(axis, hops): along(axis, hops) for axis in range(3) for hops in (1, 2, 3)}
        self.partner = partner()


class Part:
    def __init__(self, place, own, out, box, send, recv, keep, base, chunk, order, ring):
        self.own, self.out, self.box, self.send, self.recv, self.keep = own, out, box, send, recv, keep
        self.place, self.axes, self.ring = place, order, ring
        self.here = [place.here[a] for a in order]
        self.big, self.mid, self.chunk = 16 * chunk, 4 * chunk, chunk
        self.base = base
        self.first = base + self.here[0] * self.big
        self.second = self.first + self.here[1] * self.mid
        self.third = self.second + self.here[2] * chunk

    def top(self, hops):
        return self.base + jnp.bitwise_and(self.here[0] + hops, RING - 1) * self.big

    def message(self, n):
        big, mid, chunk = self.big, self.mid, self.chunk
        half = big // 2
        up, down = (0, 1), (0, RING - 1)
        own, out, box = self.own, self.out, self.box
        after = 3 * big
        if n < 6 and not self.ring:
            hops = (1, 3, 2)[n]
            src, dst, to = rows_of(own, self.top(hops), big), rows_of(box, n * big, big), (0, hops)
        elif n == 0:
            src, dst, to = rows_of(own, self.top(2), half), rows_of(box, 0, half), up
        elif n == 1:
            src, dst, to = rows_of(own, self.top(2) + half, half), rows_of(box, half, half), down
        elif n == 2:
            src, dst, to = rows_of(own, self.top(1) + half, half), rows_of(box, big + half, half), up
        elif n == 3:
            src, dst, to = rows_of(own, self.top(3), half), rows_of(box, 2 * big, half), down
        elif n == 4:
            src, dst, to = rows_of(own, self.top(1), half), rows_of(box, big, half), up
        elif n == 5:
            src, dst, to = rows_of(own, self.top(3) + half, half), rows_of(box, 2 * big + half, half), down
        elif n < 9:
            hops = (1, 3, 2)[n - 6]
            at = self.first + jnp.bitwise_and(self.here[1] + hops, RING - 1) * mid
            src, dst, to = rows_of(own, at, mid), rows_of(box, after + (n - 6) * mid, mid), (1, hops)
        elif n < 12:
            hops = (1, 3, 2)[n - 9]
            at = self.second + jnp.bitwise_and(self.here[2] + hops, RING - 1) * chunk
            src, to = rows_of(own, at, chunk), (2, hops)
            dst = rows_of(box, after + 3 * mid + (n - 9) * chunk, chunk)
        elif n < 15:
            src, dst = rows_of(own, self.third, chunk), rows_of(out, self.third, chunk)
            to = (2, (1, 3, 2)[n - 12])
        elif n < 18:
            src = dst = rows_of(out, self.second, mid)
            to = (1, (1, 3, 2)[n - 15])
        elif not self.ring:
            src = dst = rows_of(out, self.first, big)
            to = (0, (1, 3, 2)[n - 18])
        elif n < 20:
            src = dst = rows_of(out, self.first, big)
            to = (up, down)[n - 18]
        elif n == 20:
            src = dst = rows_of(out, self.top(3), half)
            to = up
        else:
            src = dst = rows_of(out, self.top(1) + half, half)
            to = down
        device = self.place.chips[self.axes[to[0]], to[1]]
        g = self.group(n)
        return pltpu.make_async_remote_copy(
            src, dst, self.send.at[g], self.recv.at[g], device_id=device, device_id_type=MESH
        )

    def group(self, n):
        if n < 6:
            return 0 if not self.ring else (n if n < 2 else 2)
        if n < 18:
            return n // 3 * 3
        return 18 if not self.ring else (n if n < 20 else 20)

    def start(self, *numbers):
        for n in numbers:
            self.message(n).start()

    def wait(self, *numbers):
        if len(numbers) == 1:
            self.message(numbers[0]).wait()
            return
        g = self.group(numbers[0])
        big, mid, chunk = self.big, self.mid, self.chunk
        ref, at, size = {
            0: (self.box, 0, 3 * big),
            2: (self.box, big, 2 * big),
            6: (self.box, 3 * big, 3 * mid),
            9: (self.box, 3 * big + 3 * mid, 3 * chunk),
            12: (self.out, self.base, 3 * chunk),
            15: (self.out, self.base, 3 * mid),
            18: (self.out, self.base, 3 * big),
            20: (self.out, self.base, big),
        }[g]
        rows = rows_of(ref, at, size)
        pltpu.make_async_copy(rows, rows, self.send.at[g]).wait()
        pltpu.make_async_copy(rows, rows, self.recv.at[g]).wait()

    def kept(self):
        return pltpu.make_async_copy(
            rows_of(self.own, self.third, self.chunk), rows_of(self.out, self.third, self.chunk), self.keep
        )

    def stage(self, k):
        big, mid, chunk, own, box = self.big, self.mid, self.chunk, self.own, self.box
        half, after = big // 2, 3 * big
        if k == 0:
            self.start(*((0, 1, 2, 3) if self.ring else (2, 0, 1)))
        elif k == 1 and self.ring:
            self.wait(0)
            add_rows(own, self.top(1), half, [(box, 0)])
            self.start(4)
            self.wait(1)
            add_rows(own, self.top(3) + half, half, [(box, half)])
            self.start(5)
        elif k == 2:
            if self.ring:
                self.wait(2, 3, 4, 5)
            else:
                self.wait(0, 1, 2)
            add_rows(own, self.first, big, [(box, n * big) for n in ((1, 2) if self.ring else (0, 1, 2))])
            self.start(6, 7, 8)
        elif k == 3:
            self.wait(6, 7, 8)
            add_rows(own, self.second, mid, [(box, after + n * mid) for n in range(3)])
            self.start(9, 10, 11)
        elif k == 4:
            self.wait(9, 10, 11)
            add_rows(own, self.third, chunk, [(box, after + 3 * mid + n * chunk) for n in range(3)])
            self.kept().start()
            self.start(12, 13, 14)
        elif k == 5:
            self.kept().wait()
            self.wait(12, 13, 14)
            self.start(15, 16, 17)
        elif k == 6:
            self.wait(15, 16, 17)
            self.start(*((18, 19) if self.ring else (20, 18, 19)))
        elif k == 7 and self.ring:
            self.wait(18)
            self.start(20)
            self.wait(19)
            self.start(21)
        elif k == 8:
            self.wait(*((20, 21) if self.ring else (18, 19, 20)))


def parts_of(place, chunks, own, out, boxes, sems, ring):
    parts, base = [], 0
    for n, chunk in enumerate(chunks):
        send, recv, keep = (sem.at[n] for sem in sems)
        parts.append(Part(place, own, out, boxes[n], send, recv, keep, base, chunk, ORDERS[n], ring))
        base += 64 * chunk
    return parts


def run(parts, k):
    for part in parts:
        part.stage(k)


def type_picker(kinds, heads, types):
    shape = (heads * types, len(kinds) * heads)
    row = lax.broadcasted_iota(jnp.int32, shape, 0)
    column = lax.broadcasted_iota(jnp.int32, shape, 1)
    kind = jnp.full(shape, kinds[-1], jnp.int32)
    for n in reversed(range(len(kinds) - 1)):
        kind = jnp.where(column < (n + 1) * heads, kinds[n], kind)
    same_head = (row // types) == (column % heads)
    return (same_head & ((row % types) == kind)).astype(F32).astype(BF)


def lay_positions(pos_ref, all_pos):
    keys = pos_ref.shape[0]
    tails = keys - LANES
    all_pos[:keys] = pos_ref[...].astype(F32).T[:, :LANES].astype(jnp.int32)
    all_pos[keys : keys + tails] = pos_ref[LANES:, :LANES]
    all_pos[keys + tails :] = jnp.full((tails, LANES), -1, jnp.int32)
    all_pos[keys + tails :, : keys - LANES] = pos_ref[LANES:, LANES:]


def one_hot_of(pos):
    low = jnp.bitwise_and(pos, SPAN - 1).astype(F32).astype(BF)
    line = lax.broadcasted_iota(jnp.int32, (SPAN, pos.shape[1]), 0).astype(F32).astype(BF)
    return jnp.where(line == low, jnp.ones((), BF), jnp.zeros((), BF))


def spread_table(picker, table_ref, t2):
    rows, count = picker.shape[1], table_ref.shape[1]
    for k in range(t2.shape[0] // rows):
        width = min(SPAN, count - k * SPAN)
        part = table_ref[:, k * SPAN : k * SPAN + width].astype(BF)
        t2[k * rows : (k + 1) * rows, :width] = tn(picker, part).astype(BF)
        if width < SPAN:
            t2[k * rows : (k + 1) * rows, width:] = jnp.zeros((rows, SPAN - width), BF)


def look_up(t2, all_pos, dest, first, last):
    rows = dest.shape[0]
    high = t2.shape[0] // rows

    @pl.loop(first, last, unroll=3)
    def _(i):
        at = pl.multiple_of(i * 8, 8)
        eight = all_pos[pl.ds(at, 8), :]
        for s in range(0, 8, PER):
            pos = jnp.concatenate([eight[s + j : s + j + 1] for j in range(PER)], 1)
            top = jnp.right_shift(pos, 8)
            spread = nn(t2[...], one_hot_of(pos))
            picked = jnp.zeros((rows, PER * LANES), F32)
            for k in range(high):
                picked = jnp.where(top == k, spread[k * rows : (k + 1) * rows], picked)
            for j in range(PER):
                dest[:, pl.ds(at + s + j, 1), :] = picked[:, j * LANES : (j + 1) * LANES].reshape(rows, 1, LANES)


def turn_tails(bias, bias_tail, keys):
    tails = keys - LANES
    per = bias_tail.shape[2] // tails
    for i in range(bias_tail.shape[0]):
        lines = bias[i * per : (i + 1) * per, keys : keys + tails].reshape(per * tails, LANES)
        bias_tail[i, :LANES] = lines.T
        lines = bias[i * per : (i + 1) * per, keys + tails : keys + 2 * tails].reshape(per * tails, LANES)
        bias_tail[i, LANES:] = lines.T[: keys - LANES]


def lay_terms(ds_main, ds_tail, lines):
    rows, keys = ds_main.shape[:2]
    tails = keys - LANES
    per = ds_tail.shape[2] // tails

    @pl.loop(0, ds_tail.shape[0])
    def _(i):
        at = pl.ds(i * per, per)
        lines[at, :keys] = ds_main[at].astype(F32)
        block = ds_tail[i].astype(F32)
        lines[at, keys : keys + tails] = block[:LANES].T.reshape(per, tails, LANES)
        lines[at, keys + tails : keys + 2 * tails] = jnp.zeros((per, tails, LANES), F32)
        lines[at, keys + tails : keys + 2 * tails, : keys - LANES] = block[LANES:].T.reshape(per, tails, keys - LANES)


def add_terms(acc, all_pos, lines, first, last):
    rows = lines.shape[0]
    high = acc.shape[0] // rows

    @pl.loop(first, last, unroll=2)
    def _(i):
        at = pl.multiple_of(i * 8, 8)
        eight = all_pos[pl.ds(at, 8), :]
        total = None
        for s in range(0, 8, PER):
            pos = jnp.concatenate([eight[s + j : s + j + 1] for j in range(PER)], 1)
            terms = jnp.concatenate([lines[:, pl.ds(at + s + j, 1), :].reshape(rows, LANES) for j in range(PER)], 1)
            top = jnp.right_shift(pos, 8)
            parts = jnp.concatenate([jnp.where(top == k, terms, 0.0) for k in range(high)], 0)
            term = nt(parts.astype(BF), one_hot_of(pos))
            total = term if total is None else total + term
        acc[...] += total


def norm(values):
    centred = values - jnp.mean(values, -1, keepdims=True)
    spread = jnp.mean(centred * centred, -1, keepdims=True)
    scale = lax.rsqrt(spread + EPS)
    return centred * scale, scale


def norm_back(grad, gain, unit, scale):
    scaled = grad * gain
    first = jnp.mean(scaled, -1, keepdims=True)
    second = jnp.mean(scaled * unit, -1, keepdims=True)
    return (scaled - first - unit * second) * scale


def gelu_pair(v):
    half = jnp.exp(-0.5 * v * v)
    t = 1.0 / (1.0 + 0.23164189 * jnp.abs(v))
    series = t * (0.127414796 + t * (-0.142248368 + t * (0.7107068705 + t * (-0.7265760135 + t * 0.5307027145))))
    tail = series * half
    phi = jnp.where(v >= 0.0, 1.0 - tail, tail)
    return v * phi, phi + v * half * 0.3989422804014327


def head_masks(width):
    lane = lax.broadcasted_iota(jnp.int32, (1, width), 1)
    return [(lane // HEAD) == h for h in range(width // HEAD)]


def keep(mask, values):
    return jnp.where(mask, values, 0.0)


def put_panels(ref, at, values):
    rows = values.shape[0]
    for j in range(values.shape[1] // LANES):
        ref[at + j * rows : at + (j + 1) * rows] = values[:, j * LANES : (j + 1) * LANES].astype(ref.dtype)


def softmax_rows(scores):
    top = jnp.max(scores, 0, keepdims=True)
    e = jnp.exp(scores - top)
    return e * (1.0 / jnp.sum(e, 0, keepdims=True))


def score_back(prob, grad):
    return prob * (grad - jnp.sum(grad * prob, 0, keepdims=True))


def layer_kernel(
    kinds_ref, tokens_ref,
    e_gain0, e_gain1, e_shift0, e_shift1,
    e_qkv0, e_qkv1, e_out0, e_out1, e_up0, e_up1, e_down0, e_down1, e_lift0, e_lift1,
    f_gain, f_shift, f_qkv_ref, f_out_ref, f_up_ref, f_down_ref,
    table_ref, pos_ref, target_ref, code_ref,
    out_ref, xg_out, e_all, f_all, t_all,
    f_qkv, f_out, f_up, f_down,
    x_s, xg_s, n1_s, q_s, k_s, v_s, p_s, o_s, n2_s, h_s, act_s, gp_s, res_s,
    win_s, fq, fk, fv, fp, fo, fdq, fdk, fdv, fh, fn2, fdy, fgrad,
    t2, all_pos, bias_main, bias_tail, ds_main, ds_tail, acc_t,
    acc, acc_norm, own_e, own_f, give_f, peer_f, own_t, give_t, peer_t,
    be0, be1, be2, bf0, bf1, bf2, bt0, bt1, bt2,
    se, re, ke, sf, rf, kf, st, rt, kt, misc_send, misc_recv, misc_near,
):
    boxes_e, boxes_f, boxes_t = (be0, be1, be2), (bf0, bf1, bf2), (bt0, bt1, bt2)
    sems_e, sems_f, sems_t = (se, re, ke), (sf, rf, kf), (st, rt, kt)
    step = pl.program_id(0)
    side = lax.axis_index("lvl")
    rows = x_s.shape[2]
    width1 = x_s.shape[3]
    width2 = f_qkv.shape[0]
    half = rows // 2
    keys = rows
    root = HEAD ** (-0.5)
    masks1 = head_masks(width1)
    masks2 = head_masks(LANES)
    picks2 = [m.astype(F32).astype(BF) for m in masks2]
    gains1, shifts1 = (e_gain0, e_gain1), (e_shift0, e_shift1)
    w_qkv, w_out, w_up = (e_qkv0, e_qkv1), (e_out0, e_out1), (e_up0, e_up1)
    w_down, w_lift = (e_down0, e_down1), (e_lift0, e_lift1)

    pairs = x_s.shape[1]
    heads_all = width2 // HEAD
    types = table_ref.shape[0] // heads_all
    terms_each = 2 * heads_all
    panels = 12 * width2 // LANES
    halves = panels // 2 * width2

    place = Place()

    def encoder(q, ring=False):
        return parts_of(
            place, CHUNKS1, own_e.at[q], e_all.at[side, q], [b.at[q] for b in boxes_e], [s.at[q] for s in sems_e], ring
        )

    def joining():
        return parts_of(place, CHUNKS2, own_f, f_all.at[side], boxes_f, sems_f, True)

    def table():
        return parts_of(place, CHUNKS3, own_t, t_all.at[side], boxes_t, sems_t, False)

    def hand_over(ref, n):
        return remote(ref.at[side], ref.at[side], 3 + pairs + n)

    def hand_encoder(q):
        return remote(e_all.at[side, q], e_all.at[side, q], 5 + pairs + q)

    def hand_quarters(parts, first, quarters, what):
        for k, part in enumerate(parts):
            for hops in quarters:
                rows = rows_of(part.out, part.top(hops), part.big)
                getattr(remote(rows, rows, first + 4 * k + hops), what)()

    def hand_last(quarters, what):
        hand_quarters(encoder(2, ring=True), 4 + 2 * pairs, quarters, what)

    def hand_joining(quarters, what):
        hand_quarters(joining(), 16 + 2 * pairs, quarters, what)

    def tick(new=None, old=None):
        if new is not None:

            @pl.when(step >= 1)
            def _():
                run(encoder(step - 1), new)

        if old is not None:

            @pl.when(step == 2)
            def _():
                if old < 9:
                    run(encoder(0), old)
                if old == 8:
                    hand_encoder(0).start()

    def remote(src, dst, n):
        return pltpu.make_async_remote_copy(
            src, dst, misc_send.at[n], misc_recv.at[n], device_id=place.partner, device_id_type=MESH
        )

    def near(src, dst, n):
        return pltpu.make_async_copy(src, dst, misc_near.at[n])

    def tokens():
        given = remote(tokens_ref.at[0, pl.ds((1 - side) * pairs, pairs)], x_s.at[side], 0)
        taken = near(tokens_ref.at[0, pl.ds(side * pairs, pairs)], x_s.at[side], 0)
        return given, taken

    def joining_weights():
        pairs_of = ((f_qkv_ref, f_qkv), (f_out_ref, f_out), (f_up_ref, f_up), (f_down_ref, f_down))
        return tuple(near(src, dst, 1 + pairs + n) for n, (src, dst) in enumerate(pairs_of))

    def tokens_grad(q):
        given = remote(xg_s.at[1 - side, q], xg_out.at[0, side * pairs + q], 1 + q)
        taken = near(xg_s.at[side, q], xg_out.at[0, side * pairs + q], 1 + q)
        return given, taken

    def joining_half():
        return remote(give_f, peer_f, 1 + pairs)

    def table_half():
        return remote(give_t.at[1 - side], peer_t, 2 + pairs)

    @pl.when(step == 0)
    def _():
        barrier = pltpu.get_barrier_semaphore()
        friends = list(place.chips.values()) + [place.partner]
        for device in friends:
            pl.semaphore_signal(barrier, inc=1, device_id=device, device_id_type=MESH)
        pl.semaphore_wait(barrier, len(friends))
        for copy in tokens() + joining_weights():
            copy.start()
        lay_positions(pos_ref, all_pos)
        for q in range(pairs):
            picker = type_picker([kinds_ref[w, q] for w in range(2)], heads_all, types)
            spread_table(picker, table_ref, t2.at[q])
        acc[...] = jnp.zeros_like(acc)
        acc_norm[...] = jnp.zeros_like(acc_norm)

    eights = (keys + 2 * (keys - LANES)) // 8
    look_up(t2.at[step], all_pos, bias_main, 0, eights)
    turn_tails(bias_main, bias_tail, keys)
    tick(new=2, old=8)

    @pl.when(step == 0)
    def _():
        for copy in tokens():
            copy.wait()

    def stack1(values):
        return jnp.concatenate([keep(m, values) for m in masks1], 0).astype(BF)

    def fold1(stacked):
        total = keep(masks1[0], stacked[:half])
        for h in range(1, HEADS1):
            total += keep(masks1[h], stacked[h * half : (h + 1) * half])
        return total

    both = range(2)
    windows = [(l, w, slice(w * half, (w + 1) * half)) for l in both for w in both]
    xs = [x_s[l, step].astype(F32) for l in both]
    for l in both:
        z1, _ = norm(xs[l])
        n1_s[l] = (z1 * gains1[l][0, 0:1] + shifts1[l][0, 0:1]).astype(BF)
    for l in both:
        qkv = nn(n1_s[l], w_qkv[l][0])
        q_s[l] = qkv[:, :width1].astype(BF).astype(F32)
        k_s[l] = qkv[:, width1 : 2 * width1].astype(BF).astype(F32)
        v_s[l] = qkv[:, 2 * width1 :].astype(BF).astype(F32)
    for l, w, part in windows:
        p_s[l, w] = softmax_rows(nt(k_s[l, part].astype(BF), stack1(q_s[l, part])) * root)
    for l, w, part in windows:
        o_s[l, part] = fold1(tn(p_s[l, w].astype(BF), v_s[l, part].astype(BF)))
    for l in both:
        h = x_s[l, step].astype(F32) + nn(o_s[l].astype(BF), w_out[l][0])
        h_s[l] = h
        z2, _ = norm(h)
        n2_s[l] = (z2 * gains1[l][0, 1:2] + shifts1[l][0, 1:2]).astype(BF)
    for l in both:
        act, slope = gelu_pair(nn(n2_s[l], w_up[l][0]))
        act = act.astype(BF)
        act_s[l] = act
        gp_s[l] = slope
        res_s[l] = (h_s[l] + nt(act, w_down[l][0])).astype(BF)
    for l in both:
        lifted = nn(res_s[l], w_lift[l][0]).astype(BF).astype(F32)
        for w in range(2):
            win_s[w * rows + l * half : w * rows + (l + 1) * half] = lifted[w * half : (w + 1) * half]

    eye = lax.broadcasted_iota(jnp.int32, (rows, rows), 0) == lax.broadcasted_iota(jnp.int32, (rows, rows), 1)
    for l in range(2):
        codes = code_ref[:, l].astype(F32)
        chosen = lax.broadcasted_iota(jnp.int32, codes.shape, 0) == step
        weight = 0.5 * jnp.exp(0.35 * jnp.sum(jnp.where(chosen, codes, 0.0), 0, keepdims=True))
        column = jnp.sum(jnp.where(eye, weight, 0.0), 1, keepdims=True)
        direction = column * target_ref[l, 0].astype(F32)
        for w in range(2):
            fdy[w * rows + l * half : w * rows + (l + 1) * half] = direction[w * half : (w + 1) * half]

    @pl.when(step == 0)
    def _():
        for copy in joining_weights():
            copy.wait()

    lane_groups = width2 // LANES
    z1, _ = norm(win_s[...])
    fn1 = (z1 * f_gain[0:1] + f_shift[0:1]).astype(BF)
    for t, dest in enumerate((fq, fk, fv)):
        part = nn(fn1, f_qkv[:, t * width2 : (t + 1) * width2]).astype(BF)
        for w in range(2):
            for g in range(lane_groups):
                dest[w * lane_groups + g] = part[w * rows : (w + 1) * rows, g * LANES : (g + 1) * LANES]
    tails = rows - LANES
    tick(new=3)

    heads = LANES // HEAD
    lanes = heads * LANES + heads * tails
    spans = [slice(j * LANES, min((j + 1) * LANES, lanes)) for j in range(heads + 1)]

    def stack2(values):
        main, tail = values[:LANES], values[LANES:]
        return jnp.concatenate([main * m for m in picks2] + [tail * m for m in picks2], 0)

    def fold2(stacked):
        main = keep(masks2[0], stacked[:LANES])
        tail = keep(masks2[0], stacked[heads * LANES : heads * LANES + tails])
        for h in range(1, heads):
            main += keep(masks2[h], stacked[h * LANES : (h + 1) * LANES])
            tail += keep(masks2[h], stacked[heads * LANES + h * tails : heads * LANES + (h + 1) * tails])
        return jnp.concatenate([main, tail], 0)

    @pl.loop(0, 2 * lane_groups, unroll=UNROLL)
    def _(i):
        scores = nt(fk[i], stack2(fq[i]))
        probs = []
        for j, span in enumerate(spans):
            bias = bias_main[i * heads + j, :keys] if j < heads else bias_tail[i]
            prob = softmax_rows(scores[:, span] * root + bias)
            fp[i, :, span] = prob
            probs.append(prob.astype(BF))
        fo[i] = fold2(tn(jnp.concatenate(probs, 1), fv[i])).astype(BF)


    def joined(ref):
        return jnp.concatenate(
            [jnp.concatenate([ref[w * lane_groups + g] for g in range(lane_groups)], 1) for w in range(2)], 0
        )

    hidden = win_s[...] + nn(joined(fo), f_out[...])
    fh[...] = hidden
    z2, _ = norm(hidden)
    fn2[...] = (z2 * f_gain[1:2] + f_shift[1:2]).astype(BF)

    def add_panels(n, values):
        for j in range(values.shape[1] // LANES):
            panel = values[:, j * LANES : (j + 1) * LANES]
            acc[2 * (n + j) : 2 * (n + j) + 2] += panel.reshape(2, width2 // 2, LANES)

    blocks = f_up.shape[1] // width2
    fgrad[...] = jnp.zeros_like(fgrad)

    per_block = width2 // LANES
    wide = 2 * width2
    for j in range(blocks // 2):
        up = f_up[:, j * wide : (j + 1) * wide]
        down = f_down[j * wide : (j + 1) * wide, :]
        n2 = fn2[...]
        low = fdy[...].astype(BF)
        act, slope = gelu_pair(nn(n2, up))
        act = act.astype(BF)
        fh[...] += nn(act, down)
        inner_grad = (nt(low, down) * slope).astype(BF)
        down_grad = tn(act, low)
        add_panels((8 + 2 * j) * per_block, down_grad[:width2])
        add_panels((9 + 2 * j) * per_block, down_grad[width2:])
        add_panels((4 + 2 * j) * per_block, tn(n2, inner_grad))
        fgrad[...] += nt(inner_grad, up)
        if j == 0:
            tick(new=4)

    for l in range(2):
        for w in range(2):
            out_ref[l, 0, w * half : (w + 1) * half] = fh[w * rows + l * half : w * rows + (l + 1) * half].astype(BF)

    hidden = win_s[...] + nn(joined(fo), f_out[...])
    z2, r2 = norm(hidden)
    grad = fgrad[...]
    acc_norm[1:2] += jnp.sum(grad * z2, 0, keepdims=True)
    acc_norm[3:4] += jnp.sum(grad, 0, keepdims=True)
    hidden_grad = fdy[...] + norm_back(grad, f_gain[1:2], z2, r2)
    fgrad[...] = hidden_grad
    low = hidden_grad.astype(BF)
    add_panels(3 * per_block, tn(joined(fo), low))
    att_grad = nt(low, f_out[...]).astype(BF)
    tick(new=5)
    for w in range(2):
        for g in range(lane_groups):
            fo[w * lane_groups + g] = att_grad[w * rows : (w + 1) * rows, g * LANES : (g + 1) * LANES]

    @pl.loop(0, 2 * lane_groups, unroll=UNROLL)
    def _(i):
        queries = stack2(fq[i])
        grads = stack2(fo[i])
        prob_grads = nt(fv[i], grads)
        probs, terms = [], []
        for j, span in enumerate(spans):
            prob = fp[i, :, span]
            probs.append(prob.astype(BF))
            ds = score_back(prob, prob_grads[:, span]).astype(BF)
            terms.append(ds)
            if j < heads:
                ds_main[i * heads + j] = ds
            else:
                ds_tail[i] = ds
        probs, terms = jnp.concatenate(probs, 1), jnp.concatenate(terms, 1)
        fdv[i] = nn(probs, grads).astype(BF)
        fdk[i] = (nn(terms, queries) * root).astype(BF)
        fdq[i] = (fold2(tn(terms, fk[i])) * root).astype(BF)

    z1, r1 = norm(win_s[...])
    n1 = (z1 * f_gain[0:1] + f_shift[0:1]).astype(BF)
    first = jnp.zeros((2 * rows, width2), F32)
    for t, src in enumerate((fdq, fdk, fdv)):
        part = joined(src)
        add_panels(t * per_block, tn(n1, part))
        first += nt(part, f_qkv[:, t * width2 : (t + 1) * width2])
    acc_norm[0:1] += jnp.sum(first * z1, 0, keepdims=True)
    acc_norm[2:3] += jnp.sum(first, 0, keepdims=True)
    fgrad[...] += norm_back(first, f_gain[0:1], z1, r1)

    tick(new=6)

    @pl.when(step == 2)
    def _():
        for owner, dest in ((side, own_f), (1 - side, give_f)):

            @pl.loop(0, panels // 2)
            def _(n):
                panel = acc[pl.ds(2 * (owner * (panels // 2) + n), 2)].reshape(width2, LANES)
                dest[pl.ds(pl.multiple_of(n * width2, 16), width2), :] = panel.astype(BF)

            norms = acc_norm[...]
            norms = jnp.concatenate(
                [norms[:, g * LANES : (g + 1) * LANES] for g in range(lane_groups)]
                + [jnp.zeros((EXTRA - 4 * lane_groups, LANES), F32)],
                0,
            )
            dest[halves : halves + EXTRA] = norms.astype(BF)
        own_f[halves + EXTRA :] = jnp.zeros((own_f.shape[0] - halves - EXTRA, LANES), BF)
        joining_half().start()

    packs = [own_e.at[step, l * ROWS1 : (l + 1) * ROWS1] for l in both]
    lift_grads = [
        jnp.concatenate([fgrad[w * rows + l * half : w * rows + (l + 1) * half] for w in both], 0).astype(BF)
        for l in both
    ]
    d_outs = [nt(lift_grads[l], w_lift[l][0]) for l in both]
    for l in both:
        put_panels(packs[l], 12 * width1, tn(res_s[l], lift_grads[l]))
    norm_grads = [[None] * 4 for _ in both]
    hidden_grads, att_grads, mixed, first_grads = [None] * 2, [None] * 2, [None] * 2, [None] * 2
    inner_grads = [(nn(d_outs[l].astype(BF), w_down[l][0]) * gp_s[l]).astype(BF) for l in both]
    for l in both:
        put_panels(packs[l], 15 * width1, tn(d_outs[l].astype(BF), act_s[l]))
        put_panels(packs[l], 6 * width1, tn(n2_s[l], inner_grads[l]))
    for l in both:
        grad = nt(inner_grads[l], w_up[l][0])
        z2, r2 = norm(h_s[l])
        norm_grads[l][1] = jnp.sum(grad * z2, 0, keepdims=True)
        norm_grads[l][3] = jnp.sum(grad, 0, keepdims=True)
        hidden_grads[l] = d_outs[l] + norm_back(grad, gains1[l][0, 1:2], z2, r2)
    for l in both:
        att_grads[l] = nt(hidden_grads[l].astype(BF), w_out[l][0]).astype(BF).astype(F32)
    out_grads = [tn(o_s[l].astype(BF), hidden_grads[l].astype(BF)) for l in both]
    for l in both:
        h_s[l] = hidden_grads[l]

    grads = [stack1(att_grads[l][part]) for l, w, part in windows]
    terms = [
        score_back(p_s[l, w], nt(v_s[l, part].astype(BF), grads[n])).astype(BF)
        for n, (l, w, part) in enumerate(windows)
    ]
    dvs = [nn(p_s[l, w].astype(BF), grads[n]) for n, (l, w, part) in enumerate(windows)]
    dks = [nn(terms[n], stack1(q_s[l, part])) * root for n, (l, w, part) in enumerate(windows)]
    dqs = [fold1(tn(terms[n], k_s[l, part].astype(BF))) * root for n, (l, w, part) in enumerate(windows)]
    for l in both:
        mixed[l] = jnp.concatenate(
            [jnp.concatenate([dqs[n], dks[n], dvs[n]], 1) for n in (2 * l, 2 * l + 1)], 0
        ).astype(BF)
    for l in both:
        put_panels(packs[l], 0, jnp.concatenate([tn(n1_s[l], mixed[l]), out_grads[l]], 1))
    for l in both:
        first = nt(mixed[l], w_qkv[l][0])
        z1, r1 = norm(x_s[l, step].astype(F32))
        norm_grads[l][0] = jnp.sum(first * z1, 0, keepdims=True)
        norm_grads[l][2] = jnp.sum(first, 0, keepdims=True)
        norms = jnp.pad(jnp.concatenate(norm_grads[l], 0), ((0, 4), (0, 2 * LANES - width1)))
        norms = jnp.concatenate([norms[:4, :LANES], norms[:4, LANES:], jnp.zeros((8, LANES), F32)], 0)
        packs[l][21 * width1 : 21 * width1 + EXTRA] = norms.astype(BF)
        packs[l][21 * width1 + EXTRA :] = jnp.zeros((ROWS1 - 21 * width1 - EXTRA, LANES), BF)
        xg_s[l, step] = h_s[l] + norm_back(first, gains1[l][0, 0:1], z1, r1)
    for copy in tokens_grad(step):
        copy.start()

    @pl.when(step < 2)
    def _():
        run(encoder(step), 0)

    last = encoder(2, ring=True)

    @pl.when(step == 2)
    def _():
        run(last, 0)
        joining_half().wait()
        add_rows(own_f, 0, halves + EXTRA, [(peer_f, 0)])
        run(joining(), 0)

    lay_terms(ds_main, ds_tail, bias_main)
    acc_t[step] = jnp.zeros(acc_t.shape[1:], F32)
    add_terms(acc_t.at[step], all_pos, bias_main, 0, eights // 2)

    @pl.when(step == 2)
    def _():
        run(last, 1)
        run(joining(), 1)

    add_terms(acc_t.at[step], all_pos, bias_main, eights // 2, eights)

    @pl.when(step == 2)
    def _():
        kinds = [kinds_ref[n % 2, n // 2] for n in range(2 * pairs)]
        picker = type_picker(kinds, heads_all, types)
        many = heads_all * types
        high = acc_t.shape[1] // terms_each
        for k in range(high):
            part = jnp.concatenate([acc_t[q, k * terms_each : (k + 1) * terms_each] for q in range(pairs)], 0)
            part = nn(picker, part.astype(BF)).astype(BF)
            for j in range(SPAN // LANES):
                n = k * (SPAN // LANES) + j
                at = n % high * many
                give_t[n // high, at : at + many] = part[:, j * LANES : (j + 1) * LANES]
        table_half().start()
        table_rows = high * many
        own_t[table_rows:] = jnp.zeros((own_t.shape[0] - table_rows, LANES), BF)
        for copy in [near(give_t.at[side], own_t.at[:table_rows], 0)]:
            copy.start()
            copy.wait()
        run(last, 2)
        run(joining(), 2)
        table_half().wait()
        add_rows(own_t, 0, table_rows, [(peer_t, 0)])
        run(table(), 0)
        run(last, 3)
        run(joining(), 3)
        run(encoder(1), 8)
        hand_encoder(1).start()
        run(table(), 2)
        run(last, 4)
        run(joining(), 4)
        run(table(), 3)
        run(last, 5)
        run(table(), 4)
        run(joining(), 5)
        run(last, 6)
        hand_last((0,), "start")
        run(table(), 5)
        run(joining(), 6)
        hand_joining((0,), "start")
        run(table(), 6)
        run(last, 7)
        hand_last((3, 1), "start")
        run(joining(), 7)
        hand_joining((3, 1), "start")
        run(table(), 8)
        hand_over(t_all, 1).start()
        run(last, 8)
        hand_last((2,), "start")
        run(joining(), 8)
        hand_joining((2,), "start")
        hand_last((0, 3, 1, 2), "wait")
        hand_joining((0, 3, 1, 2), "wait")
        for q in range(pairs - 1):
            hand_encoder(q).wait()
        for q in range(pairs):
            for copy in tokens_grad(q):
                copy.wait()
        hand_over(t_all, 1).wait()


def layer(kinds, tokens, enc, fus, table, pos_index, target, code):
    pairs, rows, width2 = target.shape[1:]
    width1 = tokens.shape[3]
    ff1 = enc[4].shape[2]
    keys = rows
    tails = rows - LANES
    half = rows // 2
    heads, types, count = table.shape
    high = -(-count // SPAN)
    groups = 2 * width2 // LANES
    per = LANES // HEAD
    lanes = per * (LANES + tails)
    panels = 12 * width2 // LANES
    halves = panels // 2 * width2 + EXTRA
    table_rows = high * heads * types
    total1, total2, total3 = (64 * sum(c) for c in (CHUNKS1, CHUNKS2, CHUNKS3))

    def by_row(array, level):
        return pl.BlockSpec((1,) + array.shape[1:], lambda q, level=level: (level * pairs + q, 0, 0))

    def whole(array):
        return pl.BlockSpec(array.shape, lambda q: (0,) * array.ndim, pipeline_mode=pl.Buffered(1))

    anywhere = pl.BlockSpec(memory_space=pl.ANY)
    table = table.reshape(heads * types, count)
    enc_args, enc_specs = [], []
    for array in enc:
        for level in range(2):
            enc_args.append(array)
            enc_specs.append(by_row(array, level))
    moving = pl.BlockSpec((2, 1, rows, width2), lambda q: (0, q, 0, 0))
    dma = pltpu.SemaphoreType.DMA
    vmem = pltpu.VMEM
    return pl.pallas_call(
        layer_kernel,
        grid=(pairs,),
        out_shape=(
            jax.ShapeDtypeStruct((2, pairs, rows, width2), BF),
            jax.ShapeDtypeStruct((1, 2 * pairs, rows, width1), F32),
            jax.ShapeDtypeStruct((2, pairs, total1, LANES), BF),
            jax.ShapeDtypeStruct((2, total2, LANES), BF),
            jax.ShapeDtypeStruct((2, total3, LANES), BF),
        ),
        in_specs=[pl.BlockSpec(memory_space=pltpu.SMEM), anywhere]
        + enc_specs
        + [whole(a) for a in fus[:2]]
        + [anywhere] * 4
        + [whole(table), whole(pos_index), moving, whole(code)],
        out_specs=(moving, anywhere, anywhere, anywhere, anywhere),
        scratch_shapes=[vmem(a.shape, a.dtype) for a in fus[2:]]
        + [
            vmem((2, pairs, rows, width1), BF),
            vmem((2, pairs, rows, width1), F32),
            vmem((2, rows, width1), BF),
            vmem((2, rows, width1), F32),
            vmem((2, rows, width1), F32),
            vmem((2, rows, width1), F32),
            vmem((2, 2, half, HEADS1 * half), F32),
            vmem((2, rows, width1), F32),
            vmem((2, rows, width1), BF),
            vmem((2, rows, width1), F32),
            vmem((2, rows, ff1), BF),
            vmem((2, rows, ff1), F32),
            vmem((2, rows, width1), BF),
            vmem((2 * rows, width2), F32),
            vmem((groups, rows, LANES), BF),
            vmem((groups, rows, LANES), BF),
            vmem((groups, rows, LANES), BF),
            vmem((groups, rows, lanes), F32),
            vmem((groups, rows, LANES), BF),
            vmem((groups, rows, LANES), BF),
            vmem((groups, rows, LANES), BF),
            vmem((groups, rows, LANES), BF),
            vmem((2 * rows, width2), F32),
            vmem((2 * rows, width2), BF),
            vmem((2 * rows, width2), F32),
            vmem((2 * rows, width2), F32),
            vmem((pairs, high * 2 * heads, SPAN), BF),
            vmem((keys + 2 * tails, LANES), jnp.int32),
            vmem((2 * heads, keys + 2 * tails, LANES), F32),
            vmem((groups, keys, per * tails), F32),
            vmem((2 * heads, keys, LANES), BF),
            vmem((groups, keys, per * tails), BF),
            vmem((pairs, high * 2 * heads, SPAN), F32),
            vmem((2 * panels, width2 // 2, LANES), F32),
            vmem((4, width2), F32),
            vmem((pairs, total1, LANES), BF),
            vmem((total2, LANES), BF),
            vmem((halves, LANES), BF),
            vmem((halves, LANES), BF),
            vmem((total3, LANES), BF),
            vmem((2, table_rows, LANES), BF),
            vmem((table_rows, LANES), BF),
        ]
        + [vmem((pairs, 63 * chunk, LANES), BF) for chunk in CHUNKS1]
        + [vmem((63 * chunk, LANES), BF) for chunk in CHUNKS2 + CHUNKS3]
        + [dma((pairs, 3, MESSAGES)), dma((pairs, 3, MESSAGES)), dma((pairs, 3))]
        + [dma((3, MESSAGES)), dma((3, MESSAGES)), dma((3,))] * 2
        + [dma((28 + 2 * pairs,)), dma((28 + 2 * pairs,)), dma((5 + pairs,))],
        compiler_params=pltpu.CompilerParams(
            vmem_limit_bytes=VMEM_LIMIT + 2 * 1024 * 1024, collective_id=0, has_side_effects=True
        ),
        name="layer",
    )(kinds, tokens, *enc_args, *fus, table, pos_index, target, code)


def select_kernel(groups_ref, *refs):
    count = (len(refs) - 2) // 3
    arrays, picked, held = (refs[n * count : (n + 1) * count] for n in range(3))
    into, out_of = refs[-2:]
    rows = picked[0].shape[0]
    side = lax.axis_index("lvl")

    def load(n, row):
        level, pair = row // (rows // 2), row % (rows // 2)
        group = groups_ref[level * rows + side * (rows // 2) + pair]
        return pltpu.make_async_copy(arrays[n].at[group], held[n].at[row], into.at[n, row])

    def store(n, row):
        return pltpu.make_async_copy(held[n].at[row], picked[n].at[row], out_of.at[n, row])

    every = [(n, row) for row in range(rows) for n in range(count)]
    for at in every:
        load(*at).start()
    for at in every:
        load(*at).wait()
        store(*at).start()
    for at in every:
        store(*at).wait()


def select_rows(level_group, arrays):
    count = level_group.shape[0] // 2
    anywhere = pl.BlockSpec(memory_space=pl.ANY)
    return pl.pallas_call(
        select_kernel,
        out_shape=tuple(jax.ShapeDtypeStruct((count,) + a.shape[1:], a.dtype) for a in arrays),
        in_specs=[pl.BlockSpec(memory_space=pltpu.SMEM)] + [anywhere] * len(arrays),
        out_specs=(anywhere,) * len(arrays),
        scratch_shapes=[pltpu.VMEM((count,) + a.shape[1:], a.dtype) for a in arrays]
        + [pltpu.SemaphoreType.DMA((len(arrays), count))] * 2,
        compiler_params=pltpu.CompilerParams(vmem_limit_bytes=VMEM_LIMIT),
        name="select_rows",
    )(level_group, *arrays)


def unpack_kernel(
    groups_ref, enc_ref, fus_ref, fus_extra, table_in,
    gain_ref, shift_ref, qkv_ref, out_ref, up_ref, down_ref, lift_ref,
    fg_ref, fs_ref, fq_ref, fo_ref, fu_ref, fd_ref, table_ref,
):
    width = qkv_ref.shape[1]

    def panel(n):
        return enc_ref[0, n * width : (n + 1) * width].astype(F32)

    half = LANES // 2
    for n in range(4):
        qkv_ref[0, :, n * LANES : (n + 1) * LANES] = panel(n)
    mixed, last = panel(4), panel(5)
    qkv_ref[0, :, 4 * LANES :] = mixed[:, :half]
    out_ref[0] = jnp.concatenate([mixed[:, half:], last], 1)
    for n in range(6):
        up_ref[0, :, n * LANES : (n + 1) * LANES] = panel(6 + n)
        down_ref[0, :, n * LANES : (n + 1) * LANES] = panel(15 + n)
    for n in range(3):
        lift_ref[0, :, n * LANES : (n + 1) * LANES] = panel(12 + n)
    norms = enc_ref[0, 21 * width : 21 * width + EXTRA].astype(F32)
    norms = jnp.concatenate([norms[0:4], norms[4:8]], 1)[:, :width]
    gain_ref[0] = norms[0:2]
    shift_ref[0] = norms[2:4]
    i = pl.program_id(0)
    size = fo_ref.shape[0]

    def joining(dest):
        for n in range(size // LANES):
            dest[:, n * LANES : (n + 1) * LANES] = fus_ref[0, n * size : (n + 1) * size].astype(F32)

    @pl.when(i < 3)
    def _():
        joining(fq_ref)

    @pl.when(i == 3)
    def _():
        joining(fo_ref)

    @pl.when((i >= 4) & (i < 8))
    def _():
        joining(fu_ref)

    @pl.when(i >= 8)
    def _():
        joining(fd_ref)

    heads, types, count = table_ref.shape

    @pl.when(i == 0)
    def _():
        extra = fus_extra[0].astype(F32)
        extra = jnp.concatenate([extra[4 * n : 4 * n + 4] for n in range(size // LANES)], 1)
        fg_ref[...] = extra[0:2]
        fs_ref[...] = extra[2:4]
        each = heads * types
        per = table_in.shape[1] // each
        for n in range(2 * per):
            wide = min(LANES, count - n * LANES)
            if wide > 0:
                at = n % per * each
                block = table_in[n // per, at : at + each].astype(F32).reshape(heads, types, LANES)
                table_ref[:, :, n * LANES : n * LANES + wide] = block[:, :, :wide]


def unpack(level_group, enc, fus, table, width1, width2, table_shape):
    groups = enc.shape[0]
    pairs = groups // 4

    def group_of(i, s):
        return s[i % 2 * (groups // 2) + i // (2 * pairs) * pairs + i // 2 % pairs]

    heads, types, count = table_shape
    table_rows = -(-count // SPAN) * heads * types
    panels = width2 * width2 // LANES
    sizes1 = [(2, width1), (2, width1), (width1, 3 * width1), (width1, width1), (width1, 4 * width1), (width1, 4 * width1), (width1, 2 * width1)]
    sizes2 = [(2, width2), (2, width2), (width2, 3 * width2), (width2, width2), (width2, 4 * width2), (4 * width2, width2)]
    square = (width2, width2)
    return pl.pallas_call(
        unpack_kernel,
        out_shape=tuple(jax.ShapeDtypeStruct((groups,) + s, F32) for s in sizes1)
        + tuple(jax.ShapeDtypeStruct(s, F32) for s in sizes2)
        + (jax.ShapeDtypeStruct(table_shape, F32),),
        grid_spec=pltpu.PrefetchScalarGridSpec(
            num_scalar_prefetch=1,
            grid=(groups,),
            in_specs=[
                pl.BlockSpec((1,) + enc.shape[1:], lambda i, s: (i, 0, 0)),
                pl.BlockSpec((1, panels, LANES), lambda i, s: (i // 6, i % 6, 0)),
                pl.BlockSpec((1, EXTRA, LANES), lambda i, s: (0, 6 * panels // EXTRA, 0)),
                pl.BlockSpec((2, table_rows, LANES), lambda i, s: (0, 0, 0)),
            ],
            out_specs=tuple(pl.BlockSpec((1,) + s, lambda i, s: (group_of(i, s), 0, 0)) for s in sizes1)
            + (
                pl.BlockSpec((2, width2), lambda i, s: (0, 0)),
                pl.BlockSpec((2, width2), lambda i, s: (0, 0)),
                pl.BlockSpec(square, lambda i, s: (0, jnp.minimum(i, 2))),
                pl.BlockSpec(square, lambda i, s: (0, 0)),
                pl.BlockSpec(square, lambda i, s: (0, jnp.clip(i - 4, 0, 3))),
                pl.BlockSpec(square, lambda i, s: (jnp.clip(i - 8, 0, 3), 0)),
                pl.BlockSpec(table_shape, lambda i, s: (0, 0, 0)),
            ),
        ),
        compiler_params=pltpu.CompilerParams(vmem_limit_bytes=VMEM_LIMIT),
        name="unpack",
    )(level_group, enc, fus, fus, table)


def shards(
    tokens_in,
    enc_gains,
    enc_shifts,
    enc_qkv,
    enc_out,
    enc_up,
    enc_down,
    enc_lift,
    fus_gains,
    fus_shifts,
    fus_qkv,
    fus_out,
    fus_up,
    fus_down,
    fus_table,
    target,
    loss_code,
    level_group,
    window_type,
    pos_index,
):
    enc = select_rows(
        level_group, (enc_gains, enc_shifts, enc_qkv, enc_out, enc_up, jnp.swapaxes(enc_down, 1, 2), enc_lift)
    )
    output, x_grad, enc_sums, fus_sums, table_sums = layer(
        window_type.T,
        tokens_in,
        enc,
        (fus_gains, fus_shifts, fus_qkv, fus_out, fus_up, fus_down),
        fus_table,
        pos_index,
        target,
        jnp.swapaxes(loss_code, 0, 1),
    )
    grads = unpack(
        level_group,
        enc_sums.reshape(level_group.shape[0], ROWS1, LANES),
        fus_sums,
        table_sums,
        enc_out.shape[1],
        fus_out.shape[0],
        fus_table.shape,
    )
    return (output, x_grad, *grads[:5], jnp.swapaxes(grads[5], 1, 2), *grads[6:])


def solution(mesh):
    copied = P()
    in_specs = (
        (P("lvl", None, "win", None),)
        + (copied,) * 14
        + (P(None, "lvl", "win", None), P(None, "lvl", "win"), copied, P("lvl", "win"), copied)
    )
    out_specs = (P(None, "lvl", "win", None), P("lvl", None, "win", None)) + (copied,) * 14
    return jax.shard_map(shards, mesh=mesh, in_specs=in_specs, out_specs=out_specs, check_vma=False)
```
